32 devices in a mesh: dp: 8 (over z, y), tensor: 4 (over x, core).
Axes of the slice: x: 2, y: 2, z: 4, core: 2. Of those that a mesh axis runs over, the one named last changes fastest.
Arguments:
- query_tokens: bfloat16 [8192, 768], P(('dp', 'tensor')), may hold values from -6 to 6
- key_tokens: bfloat16 [8192, 768], P(('dp', 'tensor')), may hold values from -6 to 6
- query_lengths: int32 [32], P('dp'), may hold values from 64 to 256, as said below
- key_lengths: int32 [32], P('dp'), may hold values from 64 to 256, as said below
- positives: int32 [32], replicated, may hold values from 0 to 31, each once
- key_queue: bfloat16 [16384, 768], P(('dp', 'tensor')), may hold values from -0.59765625 to 0.59765625
- token_cotangent: bfloat16 [8192, 768], P(('dp', 'tensor')), may hold values from -0.0059814453 to 0.0059814453
- heads_in: bfloat16 [3, 768, 768], P(None, None, 'tensor'), may hold values from -0.21875 to 0.21875
- heads_bias: bfloat16 [2, 768], P(None, 'tensor'), may hold values from -1.796875 to 1.796875
- heads_out: bfloat16 [768, 768], P('tensor'), may hold values from -1.25 to 1.25
- expand_weight: bfloat16 [768, 3072], P(None, 'tensor'), may hold values from -0.21875 to 0.21875
- expand_bias: bfloat16 [3072], replicated, may hold values from -1.796875 to 1.796875
- shrink_weight: bfloat16 [3072, 768], P('tensor'), may hold values from -0.109375 to 0.109375
- branch_bias: bfloat16 [2, 768], replicated, may hold values from -1.796875 to 1.796875
- norm_gain: bfloat16 [2, 768], replicated, may hold values from 0.099609375 to 1.8984375
- norm_shift: bfloat16 [2, 768], replicated, may hold values from -0.59765625 to 0.59765625
- momentum_heads_in: float32 [3, 768, 768], P(None, 'dp', 'tensor'), may hold values from -0.21875 to 0.21875
- momentum_heads_bias: float32 [2, 768], P(None, 'tensor'), may hold values from -1.8 to 1.8
- momentum_heads_out: float32 [768, 768], P('tensor', 'dp'), may hold values from -1.25 to 1.25
- momentum_expand_weight: float32 [768, 3072], P('dp', 'tensor'), may hold values from -0.21875 to 0.21875
- momentum_expand_bias: float32 [3072], replicated, may hold values from -1.8 to 1.8
- momentum_shrink_weight: float32 [3072, 768], P('tensor', 'dp'), may hold values from -0.109375 to 0.109375
- momentum_branch_bias: float32 [2, 768], replicated, may hold values from -1.8 to 1.8
- momentum_norm_gain: float32 [2, 768], replicated, may hold values from 0.4 to 1.6
- momentum_norm_shift: float32 [2, 768], replicated, may hold values from -0.6 to 0.6
Outputs:
- query_output: bfloat16 [8192, 768], P(('dp', 'tensor'))
- key_output: bfloat16 [8192, 768], P(('dp', 'tensor'))
- contrast_loss: float32 [], replicated
- input_gradient: float32 [8192, 768], P(('dp', 'tensor'))
- gradient_heads_in: float32 [3, 768, 768], P(None, None, 'tensor')
- gradient_heads_bias: float32 [2, 768], P(None, 'tensor')
- gradient_heads_out: float32 [768, 768], P('tensor')
- gradient_expand_weight: float32 [768, 3072], P(None, 'tensor')
- gradient_expand_bias: float32 [3072], P('tensor')
- gradient_shrink_weight: float32 [3072, 768], P('tensor')
- gradient_branch_bias: float32 [2, 768], replicated
- gradient_norm_gain: float32 [2, 768], replicated
- gradient_norm_shift: float32 [2, 768], replicated
- updated_heads_in: float32 [3, 768, 768], P(None, 'dp', 'tensor')
- updated_heads_bias: float32 [2, 768], P(None, 'tensor')
- updated_heads_out: float32 [768, 768], P('tensor', 'dp')
- updated_expand_weight: float32 [768, 3072], P('dp', 'tensor')
- updated_expand_bias: float32 [3072], P('tensor')
- updated_shrink_weight: float32 [3072, 768], P('tensor', 'dp')
- updated_branch_bias: float32 [2, 768], replicated
- updated_norm_gain: float32 [2, 768], replicated
- updated_norm_shift: float32 [2, 768], replicated
The draws below stay inside these ranges and needn't reach their ends.
Inputs may be any that keep to these rules, and one draw needn't show every extreme that they name: `query_lengths`: some crop has exactly 256 valid tokens and some exactly 64. `key_lengths`: some crop has exactly 256 valid tokens and some exactly 64. `positives`: every key crop is the positive of exactly one query crop.
All inputs are finite; a program needn't handle non-finite values.
Results may differ from the reference program's by a relative error of at most 0.018.
Values may be sent and summed in bfloat16 or wider, within the bound.
A program may use at most 128 MiB of HBM per device.

```python
import math
import jax
import jax.numpy as jnp
from jax import lax

D = 768
HEAD = 64
FF = 3072
SEQ = 256
CROPS = 32
QUEUE = 16384


def crop_lengths(seeded):
    first_key, second_key = jax.random.split(seeded)
    lengths = jax.random.randint(first_key, (CROPS,), SEQ // 4, SEQ + 1)
    order = jax.random.permutation(second_key, CROPS)
    lengths = lengths.at[order[0]].set(SEQ)
    return lengths.at[order[1]].set(SEQ // 4).astype(jnp.int32)


def draw_query_lengths(key, part):
    key = jax.random.fold_in(key, 11)
    return crop_lengths(key)


def draw_key_lengths(key, part):
    key = jax.random.fold_in(key, 12)
    return crop_lengths(key)


def steps_of(rng, extent, shards, smallest, high):
    loudness = 1.0
    for position, parts in shards:
        steps = jax.random.uniform(jax.random.fold_in(jax.random.fold_in(rng, 6), position), (parts,), jnp.float32, smallest / len(shards), high / len(shards))
        loudness = loudness * jnp.repeat(jnp.exp(steps), extent[position] // parts).reshape((-1,) + (1,) * (len(extent) - 1 - position))
    return loudness


def normal_values(stream_key, dims, scale, most, shards=(), held_as=jnp.bfloat16):
    gain = steps_of(stream_key, dims, shards, -0.22, 0.18) if shards else 1.0
    drawn = jax.random.normal(stream_key, dims, jnp.float32) * scale * gain
    return jnp.minimum(jnp.maximum(drawn, -most), most).astype(held_as)


def setup_inputs(seed: int = 0) -> dict:
    arg_keys = jax.random.split(jax.random.key(seed), 26)
    return {
        "query_tokens": normal_values(arg_keys[0], (CROPS * SEQ, D), 1.0, 6.0, ((0, 32),)),
        "key_tokens": normal_values(arg_keys[1], (CROPS * SEQ, D), 1.0, 6.0, ((0, 32),)),
        "query_lengths": draw_query_lengths(jax.random.fold_in(arg_keys[25], 71), 0),
        "key_lengths": draw_key_lengths(jax.random.fold_in(arg_keys[25], 71), 0),
        "positives": jax.random.permutation(arg_keys[4], CROPS).astype(jnp.int32),
        "key_queue": normal_values(arg_keys[5], (QUEUE, D), 0.1, 0.59765625, ((0, 32),)),
        "token_cotangent": normal_values(arg_keys[6], (CROPS * SEQ, D), 0.001, 0.0059814453, ((0, 32),)),
        "heads_in": normal_values(arg_keys[7], (3, D, D), D ** -0.5, 0.21875, ((2, 4),)),
        "heads_bias": normal_values(arg_keys[8], (2, D), 0.3, 1.796875, ((1, 4),)),
        "heads_out": normal_values(arg_keys[9], (D, D), (D // 32) ** -0.5, 1.25, ((0, 4),)),
        "expand_weight": normal_values(arg_keys[10], (D, FF), D ** -0.5, 0.21875, ((1, 4),)),
        "expand_bias": normal_values(arg_keys[11], (FF,), 0.3, 1.796875),
        "shrink_weight": normal_values(arg_keys[12], (FF, D), FF ** -0.5, 0.109375, ((0, 4),)),
        "branch_bias": normal_values(arg_keys[13], (2, D), 0.3, 1.796875),
        "norm_gain": jnp.clip(1.0 + 0.18 * jax.random.normal(arg_keys[14], (2, D), jnp.float32), 0.099609375, 1.8984375).astype(jnp.bfloat16),
        "norm_shift": normal_values(arg_keys[15], (2, D), 0.1, 0.59765625),
        "momentum_heads_in": normal_values(arg_keys[16], (3, D, D), D ** -0.5, 0.21875, ((1, 8), (2, 4)), jnp.float32),
        "momentum_heads_bias": normal_values(arg_keys[17], (2, D), 0.3, 1.8, ((1, 4),), jnp.float32),
        "momentum_heads_out": normal_values(arg_keys[18], (D, D), (D // 32) ** -0.5, 1.25, ((0, 4), (1, 8)), jnp.float32),
        "momentum_expand_weight": normal_values(arg_keys[19], (D, FF), D ** -0.5, 0.21875, ((0, 8), (1, 4)), jnp.float32),
        "momentum_expand_bias": normal_values(arg_keys[20], (FF,), 0.3, 1.8, (), jnp.float32),
        "momentum_shrink_weight": normal_values(arg_keys[21], (FF, D), FF ** -0.5, 0.109375, ((0, 4), (1, 8)), jnp.float32),
        "momentum_branch_bias": normal_values(arg_keys[22], (2, D), 0.3, 1.8, (), jnp.float32),
        "momentum_norm_gain": jnp.clip(jax.random.uniform(arg_keys[23], (2, D), jnp.float32, 0.4, 1.6), 0.4, 1.6),
        "momentum_norm_shift": normal_values(arg_keys[24], (2, D), 0.1, 0.6, (), jnp.float32),
    }


SOFTMAX_DIVISOR = 0.05
MOMENTUM = 0.5
NORM_EPSILON = 1e-12
MASKED_SCORE = -1e+30
EXACT_ARITHMETIC = lax.Precision.HIGHEST

@jax.custom_vjp
def low(v):
    return lax.optimization_barrier(v.astype(jnp.bfloat16)).astype(jnp.float32)

@jax.custom_vjp
def low_back(v):
    return v

def low_keep(v):
    return (low(v), None)

def low_pass(kept, grad):
    return (grad,)

def back_keep(v):
    return (v, None)

def back_low(kept, grad):
    return (low(grad),)
low.defvjp(low_keep, low_pass)
low_back.defvjp(back_keep, back_low)

def norm_rows(inputs, gain_row, shift_row):
    row_mean = lax.optimization_barrier(jnp.mean(inputs, axis=-1, keepdims=True))
    centered = inputs - row_mean
    inverse_std = lax.rsqrt(lax.optimization_barrier(jnp.mean(centered * centered, axis=-1, keepdims=True)) + NORM_EPSILON)
    return centered * inverse_std * gain_row + shift_row

def layer(tokens, lengths, params):
    heads_in, heads_bias, heads_out, expand_weight, expand_bias, shrink_weight, branch_bias, norm_gain, norm_shift = params
    crops, length, width = tokens.shape
    head_count = width // HEAD
    flat = tokens.reshape(crops * length, width)
    head_shape = (crops, length, head_count, HEAD)
    query_heads = low(low_back(jnp.dot(flat, heads_in[0], precision=EXACT_ARITHMETIC) + heads_bias[0])).reshape(head_shape)
    key_heads = low(low_back(jnp.dot(flat, heads_in[1], precision=EXACT_ARITHMETIC))).reshape(head_shape)
    value_heads = low(low_back(jnp.dot(flat, heads_in[2], precision=EXACT_ARITHMETIC) + heads_bias[1])).reshape(head_shape)
    raw_scores = low_back(jnp.einsum('cshd,cthd->chst', query_heads, key_heads, precision=EXACT_ARITHMETIC))
    valid_key = jnp.arange(length)[None, None, None, :] < lengths[:, None, None, None]
    scores = jnp.where(valid_key, raw_scores * HEAD ** (-0.5), MASKED_SCORE)
    largest_score_each = lax.optimization_barrier(jnp.max(scores, axis=-1, keepdims=True))
    powers = jnp.exp(scores - largest_score_each)
    weights = low(powers / lax.optimization_barrier(jnp.sum(powers, axis=-1, keepdims=True)))
    context = jnp.einsum('chst,cthd->cshd', weights, value_heads, precision=EXACT_ARITHMETIC).reshape(crops * length, width)
    context = low(low_back(context))
    attended = low_back(jnp.dot(context, heads_out, precision=EXACT_ARITHMETIC))
    middle = norm_rows(flat + attended + branch_bias[0], norm_gain[0], norm_shift[0])
    hidden_pre = low_back(jnp.dot(low(middle), expand_weight, precision=EXACT_ARITHMETIC) + expand_bias)
    hidden = low(jax.nn.gelu(hidden_pre, approximate=False))
    branch = low_back(jnp.dot(hidden, shrink_weight, precision=EXACT_ARITHMETIC))
    output = norm_rows(middle + branch + branch_bias[1], norm_gain[1], norm_shift[1])
    return output.reshape(crops, length, width)

def pool(output, lengths):
    length = output.shape[1]
    mask = (jnp.arange(length)[None, :] < lengths[:, None]).astype(jnp.float32)
    return lax.optimization_barrier(jnp.sum(output * mask[:, :, None], axis=1)) / lengths[:, None].astype(jnp.float32)

def unit_rows(pooled):
    return pooled * lax.rsqrt(lax.optimization_barrier(jnp.sum(pooled * pooled, axis=-1, keepdims=True)) + 1e-06)

def reference(query_tokens, key_tokens, query_lengths, key_lengths, positives, key_queue, token_cotangent, heads_in, heads_bias, heads_out, expand_weight, expand_bias, shrink_weight, branch_bias, norm_gain, norm_shift, momentum_heads_in, momentum_heads_bias, momentum_heads_out, momentum_expand_weight, momentum_expand_bias, momentum_shrink_weight, momentum_branch_bias, momentum_norm_gain, momentum_norm_shift):
    query_params = tuple((item.astype(jnp.float32) for item in (heads_in, heads_bias, heads_out, expand_weight, expand_bias, shrink_weight, branch_bias, norm_gain, norm_shift)))
    momentum_params = (momentum_heads_in, momentum_heads_bias, momentum_heads_out, momentum_expand_weight, momentum_expand_bias, momentum_shrink_weight, momentum_branch_bias, momentum_norm_gain, momentum_norm_shift)
    updated = tuple((MOMENTUM * old + (1.0 - MOMENTUM) * new for old, new in zip(momentum_params, query_params)))
    key_params = tuple((low(item) if index in (0, 2, 3, 5) else item for index, item in enumerate(updated)))
    block = math.gcd(CROPS, max(1, 4096 // SEQ))
    batches = CROPS // block
    queue_rows = key_queue.astype(jnp.float32)

    def shaped(tokens):
        return tokens.astype(jnp.float32).reshape(batches, block, SEQ, D)

    def key_block(items):
        tokens, lengths = items
        output = layer(tokens, lengths, key_params)
        return (pool(output, lengths), output.astype(jnp.bfloat16))
    key_pooled, key_out = lax.map(key_block, (shaped(key_tokens), key_lengths.reshape(batches, block)))
    key_unit = low(unit_rows(key_pooled.reshape(CROPS, D)))
    partner_units = jnp.take(key_unit, positives, axis=0)
    query_blocks = math.gcd(CROPS, 64)

    def objective(params, tokens):

        def one_block(items):
            block_tokens, lengths, cotangent = items
            output = layer(block_tokens, lengths, params)
            return (pool(output, lengths), jnp.sum(cotangent * output), output)
        pooled, terms, outputs = lax.map(jax.checkpoint(one_block), (tokens, query_lengths.reshape(batches, block), shaped(token_cotangent)))
        query_units = low(unit_rows(pooled.reshape(CROPS, D)))
        match_score = lax.optimization_barrier(jnp.sum(query_units * partner_units, axis=-1)) / SOFTMAX_DIVISOR

        def negatives(unit_block):
            queue_logits = low_back(jnp.dot(unit_block, queue_rows.T, precision=EXACT_ARITHMETIC)) / SOFTMAX_DIVISOR
            largest_each = lax.optimization_barrier(jnp.max(queue_logits, axis=-1))
            return largest_each + jnp.log(lax.optimization_barrier(jnp.sum(jnp.exp(queue_logits - largest_each[:, None]), axis=-1)))
        negative = lax.map(jax.checkpoint(negatives), query_units.reshape(CROPS // query_blocks, query_blocks, D)).reshape(CROPS)
        level = jnp.logaddexp(negative, match_score)
        loss_value = jnp.sum(level - match_score)
        return (loss_value + jnp.sum(terms), (loss_value, outputs))
    total_value, pullback, (contrast_loss, query_full) = jax.vjp(objective, query_params, shaped(query_tokens), has_aux=True)
    param_grads, token_grads = pullback(jnp.ones_like(total_value))
    query_out = query_full.astype(jnp.bfloat16)
    return (query_out.reshape(CROPS * SEQ, D), key_out.reshape(CROPS * SEQ, D), contrast_loss, token_grads.reshape(CROPS * SEQ, D), param_grads[0], param_grads[1], param_grads[2], param_grads[3], param_grads[4], param_grads[5], param_grads[6], param_grads[7], param_grads[8], updated[0], updated[1], updated[2], updated[3], updated[4], updated[5], updated[6], updated[7], updated[8])
```

```python
import types

import jax
import jax.numpy as jnp
from jax import lax
from jax.experimental import pallas as pl
from jax.experimental.pallas import tpu as pltpu
from jax.sharding import PartitionSpec as P

HEAD = 64
SOFTMAX_DIVISOR = 0.05
MOMENTUM = 0.5
NORM_EPSILON = 1e-12
MASKED_SCORE = -1e30
ROOT_HALF = 0.7071067811865476
GAUSS_SCALE = 0.3989422804014327
MESH = pl.DeviceIdType.MESH
F32, BF16 = jnp.float32, jnp.bfloat16
NN = (((1,), (0,)), ((), ()))
NT = (((1,), (1,)), ((), ()))
TN = (((0,), (0,)), ((), ()))
TENSOR = 4
PIECES = 6


def dot(a, b, dims=NN):
    return lax.dot_general(a, b, dims, preferred_element_type=F32)


def norm_rows(v, gain, shift):
    c = v - jnp.mean(v, axis=-1, keepdims=True)
    inverse = lax.rsqrt(jnp.mean(c * c, axis=-1, keepdims=True) + NORM_EPSILON)
    n = c * inverse
    return n * gain + shift, n, inverse


def norm_back(up, n, inverse, gain):
    e = up * gain
    inner = e - jnp.mean(e, axis=-1, keepdims=True) - n * jnp.mean(e * n, axis=-1, keepdims=True)
    return inner * inverse


def gelu_parts(z):
    a = jnp.abs(z) * ROOT_HALF
    g = jnp.exp(-0.5 * z * z)
    s = 1.0 / (1.0 + 0.3275911 * a)
    poly = ((((1.061405429 * s - 1.453152027) * s + 1.421413741) * s - 0.284496736) * s + 0.254829592) * s
    q = 0.5 * poly * g
    cdf = jnp.where(z >= 0, 1.0 - q, q)
    return z * cdf, cdf + z * GAUSS_SCALE * g


def kernel(cfg, *refs):
    r = types.SimpleNamespace(**dict(zip(cfg.names, refs)))
    D, HS, FS, L, DP, RC = cfg.D, cfg.HS, cfg.FS, cfg.L, cfg.DP, cfg.RC
    N, SH, NZ = DP * TENSOR, cfg.SH, DP // 2
    NCH = L // RC
    dp, t = lax.axis_index("dp"), lax.axis_index("tensor")
    px = lax.rem(t + 2, TENSOR)
    sib = t + 1 - 2 * lax.rem(t, 2)
    y, z = lax.rem(dp, 2), dp // 2
    me = dp * TENSOR + t
    d_x, d_sib, d_y = (dp, px), (dp, sib), (dp + 1 - 2 * y, t)

    def d_z(k):
        return (lax.rem(z + k, NZ) * 2 + y, t)

    def from_z(k):
        return lax.rem(z - k + NZ, NZ)

    def remote(src, dst, sems, i, dev):
        return pltpu.make_async_remote_copy(
            src_ref=src, dst_ref=dst, send_sem=sems[0].at[i], recv_sem=sems[1].at[i], device_id=dev, device_id_type=MESH
        )

    sends = []

    def send(src, dst, sems, i, dev):
        c = remote(src, dst, sems, i, dev)
        c.start()
        sends.append(c)
        return c

    loads = {}

    def load(name, src, dst):
        c = pltpu.make_async_copy(src, dst, r.lsem.at[len(loads)])
        c.start()
        loads[name] = c

    stores = []

    def store(src, dst):
        c = pltpu.make_async_copy(src, dst, r.ssem.at[len(stores)])
        c.start()
        stores.append(c)

    xs, cs = (r.xs, r.xr), (r.cs, r.cr)

    load("q", r.query_tokens, r.X.at[0, 0])
    load("hi", r.heads_in, r.wqi.at[0])
    load("mhi", r.momentum_heads_in, r.mhi) if cfg.gather else None
    load("we", r.expand_weight, r.we.at[0])
    load("wo", r.heads_out, r.wo.at[0])
    load("ws", r.shrink_weight, r.ws.at[0])
    if cfg.gather:
        load("me", r.momentum_expand_weight, r.mex)
        load("mo", r.momentum_heads_out, r.mho)
        load("ms", r.momentum_shrink_weight, r.msh)
    else:
        load("kh", r.key_heads, r.wkh.at[0])
        load("kf", r.key_ffn, r.wkf.at[0])
    load("k", r.key_tokens, r.X.at[1, 0])
    load("queue", r.key_queue, r.queue)
    load("cot", r.token_cotangent, r.cot)

    bar = pltpu.get_barrier_semaphore()

    def greet(i, c):
        o = lax.rem(me + i, N)
        pl.semaphore_signal(bar, inc=1, device_id=(o // TENSOR, lax.rem(o, TENSOR)), device_id_type=MESH)
        return c

    lax.fori_loop(1, N, greet, 0)
    pl.semaphore_wait(bar, N - 1)

    c_xq = send(r.query_tokens, r.X.at[0, 1], xs, 0, d_x)
    c_hi = send(r.heads_in, r.wqi.at[1], cs, 0, d_sib)
    c_wo = send(r.heads_out, r.wo.at[1], cs, 1, d_sib)
    c_we = send(r.expand_weight, r.we.at[1], cs, 2, d_sib)
    c_ws = send(r.shrink_weight, r.ws.at[1], cs, 3, d_sib)
    c_xk = send(r.key_tokens, r.X.at[1, 1], xs, 1, d_x)

    def vec(ref, k):
        return ref[...].astype(F32)[k : k + 1, :]

    def blend_vec(old, new):
        return MOMENTUM * old[...] + (1.0 - MOMENTUM) * new[...].astype(F32)

    r.hb[0, 0:2, :] = r.heads_bias[...].astype(F32)
    r.hb[0, 2:4, :] = blend_vec(r.momentum_heads_bias, r.heads_bias)
    c_hb = send(r.hb.at[0], r.hb.at[1], cs, 4, d_sib)
    kbb = blend_vec(r.momentum_branch_bias, r.branch_bias)
    kgain = blend_vec(r.momentum_norm_gain, r.norm_gain)
    kshift = blend_vec(r.momentum_norm_shift, r.norm_shift)
    bb = (r.branch_bias[...].astype(F32), kbb)
    gain = (r.norm_gain[...].astype(F32), kgain)
    shift = (r.norm_shift[...].astype(F32), kshift)
    r.eb[0] = r.expand_bias[...].astype(F32)
    r.eb[1] = MOMENTUM * r.momentum_expand_bias[...] + (1.0 - MOMENTUM) * r.expand_bias[...].astype(F32)

    gs = (r.gs, r.gr)
    gy0, gc0 = 2 * (NZ - 1), 2 * (NZ - 1) + 2 * NZ
    gparts = ((r.wkh, 4), (r.wkf, 2))

    def g_rows(part, owner):
        return gparts[part][0].at[0, :, pl.ds(pl.multiple_of(owner * SH, SH), SH), :]

    gz, gy = {}, {}

    def g_start(part):
        for k in range(1, NZ):
            gz[part, k] = send(g_rows(part, dp), g_rows(part, dp), gs, part * (NZ - 1) + k - 1, d_z(k))
        gy[part, 0] = send(g_rows(part, dp), g_rows(part, dp), gs, gy0 + part * NZ, d_y)

    def g_forward(part):
        for k in range(1, NZ):
            gz[part, k].wait_recv()
            rows = g_rows(part, from_z(k) * 2 + y)
            gy[part, k] = send(rows, rows, gs, gy0 + part * NZ + k, d_y)

    g_done = {}

    def g_finish(part):
        for k in range(NZ):
            gy[part, k].wait_recv()
        buf = gparts[part][0]
        g_done[part] = send(buf.at[0], buf.at[1], gs, gc0 + part, d_sib)

    if cfg.gather:
        own = pl.ds(pl.multiple_of(dp * SH, SH), SH)
        pick = (
            lax.broadcasted_iota(jnp.int32, (D, SH), 0) == lax.broadcasted_iota(jnp.int32, (D, SH), 1) + dp * SH
        ).astype(F32).astype(BF16)
        eye = (
            lax.broadcasted_iota(jnp.int32, (SH, SH), 0) == lax.broadcasted_iota(jnp.int32, (SH, SH), 1)
        ).astype(F32).astype(BF16)
        for name in ("hi", "mhi", "wo", "mo"):
            loads[name].wait()
        for i in range(3):
            u = MOMENTUM * r.mhi[i] + (1.0 - MOMENTUM) * r.wqi[0, i, own, :].astype(F32)
            r.mhi[i] = u
            r.wkh[0, i, own, :] = u.astype(BF16)
        u = MOMENTUM * r.mho[...] + (1.0 - MOMENTUM) * dot(r.wo[0], pick)
        r.mho[...] = u
        r.wkh[0, 3, own, :] = dot(eye, u.astype(BF16), NT).astype(BF16)
        g_start(0)
        for name in ("we", "me", "ws", "ms"):
            loads[name].wait()
        u = MOMENTUM * r.mex[...] + (1.0 - MOMENTUM) * r.we[0, own, :].astype(F32)
        r.mex[...] = u
        r.wkf[0, 0, own, :] = u.astype(BF16)
        u = MOMENTUM * r.msh[...] + (1.0 - MOMENTUM) * dot(r.ws[0], pick)
        r.msh[...] = u
        r.wkf[0, 1, own, :] = dot(eye, u.astype(BF16), NT).astype(BF16)
        g_start(1)
        store(r.mhi, r.o_heads_in)
        store(r.mho, r.o_heads_out)
        store(r.mex, r.o_expand)
        store(r.msh, r.o_shrink)
    else:
        for name in ("hi", "wo", "we", "ws", "kh", "kf"):
            loads[name].wait()
        for part in range(2):
            buf = gparts[part][0]
            g_done[part] = send(buf.at[0], buf.at[1], gs, gc0 + part, d_sib)

    lengths = ((r.query_lengths[t], r.query_lengths[px]), (r.key_lengths[t], r.key_lengths[px]))
    low_half = lax.broadcasted_iota(jnp.int32, (1, 128), 1) < HEAD
    key_at = lax.broadcasted_iota(jnp.int32, (1, L), 1)

    def heads_of(arr):
        pair, last = arr[:, 0:128], arr[:, 128:192]
        zero = jnp.zeros_like(pair)
        return (jnp.where(low_half, pair, zero), jnp.where(low_half, zero, pair), last)

    def attend(w, crop, out):
        x = r.X[w, crop]
        valid = key_at < lengths[w][crop]

        def slot_step(s, c):
            if w == 0:
                wq, wk, wv = r.wqi[s, 0], r.wqi[s, 1], r.wqi[s, 2]
            else:
                wq, wk, wv = r.wkh[s, 0], r.wkh[s, 1], r.wkh[s, 2]
            hb = r.hb[s]
            q = ((dot(x, wq) + hb[2 * w : 2 * w + 1, :]).astype(BF16).astype(F32) * HEAD**-0.5).astype(BF16)
            k = dot(x, wk).astype(BF16)
            v = (dot(x, wv) + hb[2 * w + 1 : 2 * w + 2, :]).astype(BF16)
            if w == 0:
                r.qkv[s, 0, crop], r.qkv[s, 1, crop], r.qkv[s, 2, crop] = q, k, v
            ks, vs, qs = heads_of(k), heads_of(v), (q[:, 0:128], q[:, 0:128], q[:, 128:192])
            parts, logs = [], []
            for h in range(3):
                sc = jnp.where(valid, dot(qs[h], ks[h], NT), MASKED_SCORE)
                top = jnp.max(sc, axis=-1, keepdims=True)
                e = jnp.exp(sc - top)
                tot = jnp.sum(e, axis=-1, keepdims=True)
                logs.append(top + jnp.log(tot))
                parts.append(dot((e * (1.0 / tot)).astype(BF16), vs[h]))
            c01 = (parts[0] + parts[1]).astype(BF16)
            c2 = parts[2].astype(BF16)
            ctx = jnp.concatenate([c01, c2], axis=1)
            if w == 0:
                at = lax.broadcasted_iota(jnp.int32, (L, 128), 1)
                r.G[s, crop] = jnp.where(at == 0, logs[0], jnp.where(at == 1, logs[1], logs[2]))
                r.C[s, crop] = ctx
                a = dot(ctx, r.wo[s])
            else:
                a = dot(ctx, r.wkh[s, 3], NT)

            @pl.when(s == 0)
            def _():
                out[...] = a

            @pl.when(s != 0)
            def _():
                out[...] += a

            return c

        lax.fori_loop(0, 2, slot_step, 0)

    def swap(src32, sbuf, rbuf, base):
        out = []
        for j in range(NCH):
            rows = pl.ds(j * RC, RC)
            sbuf[rows, :] = src32[rows, :].astype(BF16)
            out.append(send(sbuf.at[rows], rbuf.at[rows], xs, base + j, d_x))
        return out

    FT = 256

    def feed(w, crop, row0, rows_n, out):
        rows = pl.ds(row0, rows_n)
        u = r.U[w, crop, rows, :]

        def step(i, c):
            s, j = i // (FS // FT), lax.rem(i, FS // FT)
            cols = pl.ds(pl.multiple_of(j * FT, FT), FT)
            at = jnp.where(s == 0, t, sib)
            b = r.eb[w, pl.ds(at, 1), cols]
            if w == 0:
                zz = dot(u, r.we[s, :, cols]) + b
            else:
                zz = dot(u, r.wkf[s, 0, :, cols]) + b
            h, slope = gelu_parts(zz)
            h = h.astype(BF16)
            if w == 0:
                r.H[s, crop, rows, cols] = h
                r.slope[s, crop, rows, cols] = slope.astype(BF16)
                f = dot(h, r.ws[s, cols, :])
            else:
                f = dot(h, r.wkf[s, 1, :, cols], NT)

            @pl.when(i == 0)
            def _():
                out[rows, :] = f

            @pl.when(i != 0)
            def _():
                out[rows, :] += f

            return c

        lax.fori_loop(0, 2 * (FS // FT), step, 0)

    x_of = {}

    def first_norm(w, base):
        out = []
        for j in range(NCH):
            rows = pl.ds(j * RC, RC)
            x_of["A", w][j].wait_recv()
            m = r.X[w, 0, rows, :].astype(F32) + (r.own[w, rows, :] + r.arecv[w, rows, :].astype(F32)) + bb[w][0:1, :]
            u, n, inv = norm_rows(m, gain[w][0:1, :], shift[w][0:1, :])
            r.Uf[w, rows, :] = u
            r.U[w, 0, rows, :] = u.astype(BF16)
            if w == 0:
                r.N1[rows, :] = n
                r.i1[rows, :] = jnp.broadcast_to(inv, (RC, 128))
            out.append(send(r.U.at[w, 0, rows], r.U.at[w, 1, rows], xs, base + j, d_x))
        x_of["U", w] = out

    def second_norm(w, o_ref, o_hbm):
        pooled = jnp.zeros((1, D), F32)
        length = lengths[w][0]
        for j in range(NCH):
            rows = pl.ds(j * RC, RC)
            x_of["F", w][j].wait_recv()
            m = r.Uf[w, rows, :] + (r.own[w, rows, :] + r.frecv[w, rows, :].astype(F32)) + bb[w][1:2, :]
            out, n, inv = norm_rows(m, gain[w][1:2, :], shift[w][1:2, :])
            o_ref[rows, :] = out.astype(BF16)
            if w == 0:
                r.N2[rows, :] = n
                r.i2[rows, :] = jnp.broadcast_to(inv, (RC, 128))
            valid = lax.broadcasted_iota(jnp.int32, (RC, 1), 0) + j * RC < length
            pooled += jnp.sum(jnp.where(valid, out, 0.0), axis=0, keepdims=True)
        store(o_ref, o_hbm)
        pooled = pooled / length.astype(F32)
        inverse = lax.rsqrt(jnp.sum(pooled * pooled, axis=-1, keepdims=True) + 1e-06)
        unit = (pooled * inverse).astype(BF16).astype(F32)
        return pooled, inverse, unit

    KL = D // 128

    def tile_of(row):
        return jnp.concatenate([row[:, i * 128 : (i + 1) * 128] for i in range(KL)], axis=0)

    def to_all(sbuf_of, rbuf, sems, base):
        def go(i, c):
            o = lax.rem(me + i, N)
            remote(sbuf_of(o), rbuf.at[me], sems, base + i - 1, (o // TENSOR, lax.rem(o, TENSOR))).start()
            return c

        lax.fori_loop(1, N, go, 0)

    def from_all(rbuf, sems, base):
        def go(i, c):
            o = lax.rem(me - i + N, N)
            remote(rbuf.at[o], rbuf.at[o], sems, base + i - 1, d_x).wait_recv()
            return c

        lax.fori_loop(1, N, go, 0)

    def sent_all(sbuf, sems, base):
        def go(i, c):
            remote(sbuf.at[0], sbuf.at[0], sems, base + i - 1, d_x).wait_send()
            return c

        lax.fori_loop(1, N, go, 0)

    us = (r.us, r.ur)

    loads["q"].wait()
    c_hi.wait_recv()
    c_wo.wait_recv()
    c_hb.wait_recv()
    attend(0, 0, r.own.at[0])
    c_xq.wait_recv()
    attend(0, 1, r.part)
    x_of["A", 0] = swap(r.part, r.asend.at[0], r.arecv.at[0], 2)
    if cfg.gather:
        g_forward(0)
    c_we.wait_recv()
    c_ws.wait_recv()
    first_norm(0, 2 + NCH)
    feed(0, 0, 0, L, r.own.at[0])
    if cfg.gather:
        g_finish(0)
    for j in range(NCH):
        x_of["U", 0][j].wait_recv()
        feed(0, 1, j * RC, RC, r.part)
        if j == 0:
            x_of["F", 0] = []
        rows = pl.ds(j * RC, RC)
        r.fsend[0, rows, :] = r.part[rows, :].astype(BF16)
        x_of["F", 0].append(send(r.fsend.at[0, rows], r.frecv.at[0, rows], xs, 2 + 2 * NCH + j, d_x))
    kb = 2 + 3 * NCH
    c_xk.wait_recv()
    loads["k"].wait()
    g_done[0].wait_recv()
    attend(1, 1, r.part)
    x_of["A", 1] = swap(r.part, r.asend.at[1], r.arecv.at[1], kb)
    if cfg.gather:
        g_forward(1)
    attend(1, 0, r.own.at[1])
    q_pooled, q_inverse, q_unit = second_norm(0, r.oq, r.query_output)
    r.usend[0, 0:KL, :] = tile_of(q_unit)
    r.units[0, me, 0:KL, :] = tile_of(q_unit)
    to_all(lambda o: r.usend.at[0], r.units.at[0], us, 0)
    first_norm(1, kb + NCH)
    if cfg.gather:
        g_finish(1)
    g_done[1].wait_recv()
    feed(1, 0, 0, L, r.own.at[1])
    for j in range(NCH):
        x_of["U", 1][j].wait_recv()
        feed(1, 1, j * RC, RC, r.part)
        if j == 0:
            x_of["F", 1] = []
        rows = pl.ds(j * RC, RC)
        r.fsend[1, rows, :] = r.part[rows, :].astype(BF16)
        x_of["F", 1].append(send(r.fsend.at[1, rows], r.frecv.at[1, rows], xs, kb + 2 * NCH + j, d_x))
    loads["queue"].wait()
    from_all(r.units.at[0], us, 0)
    all_q = jnp.concatenate([r.units[0, :, i, :] for i in range(KL)], axis=1).astype(BF16)
    logits = dot(all_q, r.queue[...], NT) / SOFTMAX_DIVISOR
    top = jnp.max(logits, axis=-1, keepdims=True)
    e = jnp.exp(logits - top)
    tot = jnp.sum(e, axis=-1, keepdims=True)
    grad = dot(e.astype(BF16), r.queue[...])
    for i in range(KL):
        r.nsend[:, i, :] = grad[:, i * 128 : (i + 1) * 128]
    r.nsend[:, KL, :] = jnp.broadcast_to(top, (N, 128))
    r.nsend[:, KL + 1, :] = jnp.broadcast_to(tot, (N, 128))
    r.nrecv[me] = r.nsend[me]
    to_all(lambda o: r.nsend.at[o], r.nrecv, us, N - 1)
    k_pooled, k_inverse, k_unit = second_norm(1, r.ok, r.key_output)
    r.usend[1, 0:KL, :] = tile_of(k_unit)
    r.units[1, me, 0:KL, :] = tile_of(k_unit)
    to_all(lambda o: r.usend.at[1], r.units.at[1], us, 2 * (N - 1))
    from_all(r.nrecv, us, N - 1)
    from_all(r.units.at[1], us, 2 * (N - 1))

    pos = r.positives[me]
    hit = lax.broadcasted_iota(jnp.int32, (N, 1, 1), 0) == pos
    partner = jnp.sum(jnp.where(hit, r.units[1][:, 0:KL, :], 0.0), axis=0)
    mine = r.usend[0, 0:KL, :]
    match = jnp.sum(jnp.sum(mine * partner, axis=1, keepdims=True), axis=0, keepdims=True) / SOFTMAX_DIVISOR
    tops, tots = r.nrecv[:, KL, :], r.nrecv[:, KL + 1, :]
    peak = jnp.maximum(jnp.max(jnp.max(tops, axis=0, keepdims=True), axis=1, keepdims=True), match)
    total = jnp.sum(tots * jnp.exp(tops - peak), axis=0, keepdims=True)[:, 0:1]
    level = peak + jnp.log(total + jnp.exp(match - peak))
    loss = level - match
    scale = jnp.exp(r.nrecv[:, KL : KL + 1, :] - level.reshape(1, 1, 1)) * (1.0 / SOFTMAX_DIVISOR)
    du = jnp.sum(r.nrecv[:, 0:KL, :] * scale, axis=0) + (jnp.exp(match - level) - 1.0) / SOFTMAX_DIVISOR * partner
    du = jnp.concatenate([du[i : i + 1, :] for i in range(KL)], axis=1)
    along = jnp.sum(q_pooled * du, axis=-1, keepdims=True)
    d_pooled = q_inverse * du - q_pooled * (q_inverse * q_inverse * q_inverse) * along
    per_token = d_pooled / lengths[0][0].astype(F32)

    loads["cot"].wait()
    bbase = kb + 3 * NCH
    small = [jnp.zeros((1, D), F32) for _ in range(6)]
    x_of["dF"] = []
    for j in range(NCH):
        rows = pl.ds(j * RC, RC)
        valid = lax.broadcasted_iota(jnp.int32, (RC, 1), 0) + j * RC < lengths[0][0]
        dy = r.cot[rows, :].astype(F32) + jnp.where(valid, per_token, 0.0)
        n2 = r.N2[rows, :]
        d2 = norm_back(dy, n2, r.i2[rows, 0:1], gain[0][1:2, :])
        r.d2[rows, :] = d2
        r.dF[0, rows, :] = d2.astype(BF16)
        x_of["dF"].append(send(r.dF.at[0, rows], r.dF.at[1, rows], xs, bbase + j, d_x))
        small[1] += jnp.sum(d2, axis=0, keepdims=True)
        small[3] += jnp.sum(dy * n2, axis=0, keepdims=True)
        small[5] += jnp.sum(dy, axis=0, keepdims=True)

    def feed_back(crop, row0, rows_n, out):
        rows = pl.ds(row0, rows_n)
        df = r.dF[crop, rows, :]

        def step(i, c):
            s, j = i // (FS // FT), lax.rem(i, FS // FT)
            cols = pl.ds(pl.multiple_of(j * FT, FT), FT)
            dh = dot(df, r.ws[s, cols, :], NT)
            dz = (dh * r.slope[s, crop, rows, cols].astype(F32)).astype(BF16)
            r.dZ[s, crop, rows, cols] = dz
            du_ = dot(dz, r.we[s, :, cols], NT)

            @pl.when(i == 0)
            def _():
                out[rows, :] = du_

            @pl.when(i != 0)
            def _():
                out[rows, :] += du_

            return c

        lax.fori_loop(0, 2 * (FS // FT), step, 0)

    feed_back(0, 0, L, r.own.at[0])
    x_of["dU"] = []
    for j in range(NCH):
        x_of["dF"][j].wait_recv()
        feed_back(1, j * RC, RC, r.part)
        rows = pl.ds(j * RC, RC)
        r.dusend[rows, :] = r.part[rows, :].astype(BF16)
        x_of["dU"].append(send(r.dusend.at[rows], r.durecv.at[rows], xs, bbase + NCH + j, d_x))

    PR = 3 * 2 * D // (2 * 3) // 2
    HF, CH = PR // 2, PR // 2 // max(NZ, 1)
    ws_sem = (r.ws_s, r.ws_r)
    per = 2 + 2 * (NZ - 1) + NZ

    def piece_part(p, s, q):
        if p < 2:
            cols = pl.ds(p * PR + q * HF, HF) if (p * PR + q * HF) % 128 == 0 else None
            h = r.H[s].reshape(2 * L, FS)
            h = h[:, p * PR + q * HF : p * PR + (q + 1) * HF]
            return dot(h, r.dF[...].reshape(2 * L, D), TN)
        if p < 4:
            u = r.U[0].reshape(2 * L, D)[:, (p - 2) * PR + q * HF : (p - 2) * PR + (q + 1) * HF]
            return dot(u, r.dZ[s].reshape(2 * L, FS), TN)
        i = (p - 4) * 2 + q
        if i < 3:
            return dot(r.dqkv[s, i].reshape(2 * L, HS), r.X[0].reshape(2 * L, D), TN)
        return dot(r.C[s].reshape(2 * L, HS), r.dA[...].reshape(2 * L, D), TN)

    w_of = {}

    def w_sib(p):
        for q in range(2):
            r.wsend[p, q * HF : (q + 1) * HF, :] = piece_part(p, 1, q).astype(BF16)
        w_of["s", p] = send(r.wsend.at[p], r.wrecv.at[p], ws_sem, p * per, d_sib)

    def half(h):
        return pl.ds(pl.multiple_of(h * HF, HF), HF)

    def w_own(p):
        w_of["s", p].wait_recv()
        for q in range(2):
            rows = slice(q * HF, (q + 1) * HF)
            v = piece_part(p, 0, q) + r.wrecv[p, rows, :].astype(F32)
            if cfg.gather:
                r.wacc[p, rows, :] = v.astype(BF16)
            else:
                r.wacc32[p, rows, :] = v
        if cfg.gather:
            w_of["y", p] = send(r.wacc.at[p, half(1 - y)], r.wyr.at[p], ws_sem, p * per + 1, d_y)
        else:
            store(r.wacc32.at[p], r.grads.at[p])

    def chunk(zz):
        return pl.ds(pl.multiple_of(zz * CH, CH), CH)

    def place(yy, zz):
        return pl.ds(pl.multiple_of(yy * HF + zz * CH, CH), CH)

    def w_y(p):
        w_of["y", p].wait_recv()
        r.wys[p] = (r.wacc[p, half(y), :].astype(F32) + r.wyr[p].astype(F32)).astype(BF16)
        for k in range(1, NZ):
            to = lax.rem(z + k, NZ)
            w_of["z", p, k] = send(r.wys.at[p, chunk(to)], r.wzr.at[p, k - 1], ws_sem, p * per + 1 + k, d_z(k))

    def w_z(p):
        v = r.wys[p, chunk(z), :].astype(F32)
        for k in range(1, NZ):
            w_of["z", p, k].wait_recv()
            v += r.wzr[p, k - 1].astype(F32)
        at = place(y, z)
        r.wout[p, at, :] = v.astype(BF16)
        for k in range(1, NZ):
            w_of["a", p, k] = send(r.wout.at[p, at], r.wout.at[p, at], ws_sem, p * per + NZ + k, d_z(k))
        w_of["b", p, 0] = send(r.wout.at[p, at], r.wout.at[p, at], ws_sem, p * per + 2 * NZ, d_y)

    def w_a(p):
        for k in range(1, NZ):
            w_of["a", p, k].wait_recv()
            at = place(y, from_z(k))
            w_of["b", p, k] = send(r.wout.at[p, at], r.wout.at[p, at], ws_sem, p * per + 2 * NZ + k, d_y)

    def w_b(p):
        for k in range(NZ):
            w_of["b", p, k].wait_recv()
        store(r.wout.at[p], r.grads.at[p])

    if not cfg.gather:
        w_y = w_z = w_a = w_b = lambda p: None

    for p in range(4):
        w_sib(p)
    for p in range(4):
        w_own(p)

    x_of["dA"] = []
    for j in range(NCH):
        rows = pl.ds(j * RC, RC)
        x_of["dU"][j].wait_recv()
        du1 = r.d2[rows, :] + (r.own[0, rows, :] + r.durecv[rows, :].astype(F32))
        n1 = r.N1[rows, :]
        dm = norm_back(du1, n1, r.i1[rows, 0:1], gain[0][0:1, :])
        r.Uf[0, rows, :] = dm
        r.dA[0, rows, :] = dm.astype(BF16)
        x_of["dA"].append(send(r.dA.at[0, rows], r.dA.at[1, rows], xs, bbase + 2 * NCH + j, d_x))
        small[0] += jnp.sum(dm, axis=0, keepdims=True)
        small[2] += jnp.sum(du1 * n1, axis=0, keepdims=True)
        small[4] += jnp.sum(du1, axis=0, keepdims=True)
    for i in range(6):
        r.sm[0, i : i + 1, :] = small[i]
    r.sm[0, 6:7, :] = jnp.broadcast_to(loss, (1, D))
    w_y(0)

    def attend_back(crop, out):
        valid = key_at < lengths[0][crop]

        def slot_step(s, c):
            dc = dot(r.dA[crop], r.wo[s], NT).astype(BF16)
            q, k, v = r.qkv[s, 0, crop], r.qkv[s, 1, crop], r.qkv[s, 2, crop]
            g = r.G[s, crop]
            dcs, qs, ks, vs = heads_of(dc), heads_of(q), heads_of(k), heads_of(v)
            plain = lambda a, h: a[:, 128:192] if h == 2 else a[:, 0:128]
            dq, dk, dv = [], [], []
            for h in range(3):
                sc = jnp.where(valid, dot(plain(q, h), ks[h], NT), MASKED_SCORE)
                pw = jnp.exp(sc - g[:, h : h + 1])
                dpw = dot(plain(dc, h), vs[h], NT)
                inner = jnp.sum(dpw * pw, axis=-1, keepdims=True)
                ds = (pw * (dpw - inner)).astype(BF16)
                dq.append(dot(ds, ks[h]))
                dk.append(dot(ds, qs[h], TN))
                dv.append(dot(pw.astype(BF16), dcs[h], TN))
            join = lambda a, m: jnp.concatenate([((a[0] + a[1]) * m).astype(BF16), (a[2] * m).astype(BF16)], axis=1)
            dq, dk, dv = join(dq, HEAD**-0.5), join(dk, 1.0), join(dv, 1.0)
            r.dqkv[s, 0, crop], r.dqkv[s, 1, crop], r.dqkv[s, 2, crop] = dq, dk, dv
            dx = dot(dq, r.wqi[s, 0], NT) + dot(dk, r.wqi[s, 1], NT) + dot(dv, r.wqi[s, 2], NT)

            @pl.when(s == 0)
            def _():
                out[...] = dx

            @pl.when(s != 0)
            def _():
                out[...] += dx

            return c

        lax.fori_loop(0, 2, slot_step, 0)

    attend_back(0, r.own.at[1])
    w_y(1)
    w_z(0)
    for j in range(NCH):
        x_of["dA"][j].wait_recv()
    attend_back(1, r.part)
    x_of["dX"] = swap(r.part, r.dxsend, r.dxrecv, bbase + 3 * NCH)
    w_sib(4)
    w_sib(5)

    for s in range(2):
        eb = jnp.sum(r.dZ[s].reshape(2 * L, FS).astype(F32), axis=0, keepdims=True)
        bq = jnp.sum(r.dqkv[s, 0].reshape(2 * L, HS).astype(F32), axis=0, keepdims=True)
        bv = jnp.sum(r.dqkv[s, 2].reshape(2 * L, HS).astype(F32), axis=0, keepdims=True)
        dst = r.sm if s == 0 else r.smx
        at = 8 if s == 0 else 0
        if s == 0:
            r.sm[0, 8:9, 0:FS] = eb
            r.sm[0, 9:10, 0:HS] = bq
            r.sm[0, 10:11, 0:HS] = bv
        else:
            r.smx[0:8, :] = r.sm[0, 0:8, :]
            r.smx[8:9, 0:FS] = eb
            r.smx[9:10, 0:HS] = bq
            r.smx[10:11, 0:HS] = bv
    bs = (r.bs, r.br)
    send(r.smx, r.smr.at[0], bs, 0, d_sib).wait_recv()
    r.sm[1] = r.sm[0] + r.smr[0]
    b_x = send(r.sm.at[1, 0:8], r.smr.at[1, 0:8], bs, 1, d_x)
    w_own(4)
    w_own(5)
    w_y(2)
    w_z(1)
    b_x.wait_recv()
    r.sm[2] = r.sm[1]
    r.sm[2, 0:8, :] = r.sm[1, 0:8, :] + r.smr[1, 0:8, :]
    nb = DP.bit_length() - 1 if cfg.gather else 0

    def butterfly(k):
        other = dp + (1 - 2 * lax.rem(dp // (1 << k), 2)) * (1 << k)
        return send(r.sm.at[2 + k], r.smr.at[2 + k], bs, 2 + k, (other, t))

    def add_up(k, c):
        c.wait_recv()
        r.sm[3 + k] = r.sm[2 + k] + r.smr[2 + k]

    b_k = butterfly(0) if nb else None
    for j in range(NCH):
        rows = pl.ds(j * RC, RC)
        x_of["dX"][j].wait_recv()
        r.Uf[1, rows, :] = r.Uf[0, rows, :] + (r.own[1, rows, :] + r.dxrecv[rows, :].astype(F32))
    store(r.Uf.at[1], r.input_gradient)
    order = [(w_y, 3), (w_z, 2), (w_a, 0), (w_y, 4), (w_z, 3), (w_a, 1), (w_y, 5), (w_z, 4), (w_a, 2), (w_b, 0), (w_z, 5),
             (w_a, 3), (w_b, 1), (w_a, 4), (w_b, 2), (w_a, 5), (w_b, 3), (w_b, 4), (w_b, 5)]
    for n, (f, p) in enumerate(order):
        f(p)
        if nb and n % 3 == 0 and n // 3 < nb:
            k = n // 3
            add_up(k, b_k)
            b_k = butterfly(k + 1) if k + 1 < nb else None
    store(r.sm.at[2 + nb], r.vectors)

    for c in sends:
        c.wait_send()
    sent_all(r.usend, us, 0)
    sent_all(r.usend, us, N - 1)
    sent_all(r.usend, us, 2 * (N - 1))
    for c in stores:
        c.wait()


def blend(old, new):
    return MOMENTUM * old + (1.0 - MOMENTUM) * new.astype(F32)


def local(mesh_shape, query_tokens, key_tokens, query_lengths, key_lengths, positives, key_queue, token_cotangent, heads_in,
          heads_bias, heads_out, expand_weight, expand_bias, shrink_weight, branch_bias, norm_gain, norm_shift,
          momentum_heads_in, momentum_heads_bias, momentum_heads_out, momentum_expand_weight, momentum_expand_bias,
          momentum_shrink_weight, momentum_branch_bias, momentum_norm_gain, momentum_norm_shift):
    DP = mesh_shape["dp"]
    L, D = query_tokens.shape
    HS, FS = heads_in.shape[2], expand_weight.shape[1]
    SH = D // DP
    N = DP * TENSOR
    PR = D // 2
    QN = key_queue.shape[0]
    gather = SH % 16 == 0 and (PR // DP) % 16 == 0
    RC = 128
    NCH = L // RC
    NZ = DP // 2
    t, dp = lax.axis_index("tensor"), lax.axis_index("dp")
    cfg = types.SimpleNamespace(D=D, HS=HS, FS=FS, L=L, DP=DP, SH=SH, RC=RC, gather=gather)

    vm = lambda shape, dtype: pltpu.VMEM(shape, dtype)
    any_, vmem, smem = (pl.BlockSpec(memory_space=m) for m in (pl.ANY, pltpu.VMEM, pltpu.SMEM))
    ins = [
        ("query_tokens", query_tokens, any_), ("key_tokens", key_tokens, any_),
        ("query_lengths", query_lengths, smem), ("key_lengths", key_lengths, smem), ("positives", positives, smem),
        ("key_queue", key_queue, any_), ("token_cotangent", token_cotangent, any_),
        ("heads_in", heads_in, any_), ("heads_bias", heads_bias, vmem), ("heads_out", heads_out, any_),
        ("expand_weight", expand_weight, any_), ("expand_bias", expand_bias.reshape(TENSOR, FS), vmem),
        ("shrink_weight", shrink_weight, any_), ("branch_bias", branch_bias, vmem), ("norm_gain", norm_gain, vmem),
        ("norm_shift", norm_shift, vmem), ("momentum_heads_bias", momentum_heads_bias, vmem),
        ("momentum_expand_bias", momentum_expand_bias.reshape(TENSOR, FS), vmem),
        ("momentum_branch_bias", momentum_branch_bias, vmem), ("momentum_norm_gain", momentum_norm_gain, vmem),
        ("momentum_norm_shift", momentum_norm_shift, vmem),
    ]
    outs = [
        ("query_output", (L, D), BF16), ("key_output", (L, D), BF16), ("input_gradient", (L, D), F32),
        ("grads", (PIECES, PR, D), BF16 if gather else F32), ("vectors", (16, D), F32),
    ]
    if gather:
        ins += [("momentum_heads_in", momentum_heads_in, any_), ("momentum_heads_out", momentum_heads_out, any_),
                ("momentum_expand_weight", momentum_expand_weight, any_),
                ("momentum_shrink_weight", momentum_shrink_weight, any_)]
        outs += [("o_heads_in", momentum_heads_in.shape, F32), ("o_heads_out", momentum_heads_out.shape, F32),
                 ("o_expand", momentum_expand_weight.shape, F32), ("o_shrink", momentum_shrink_weight.shape, F32)]
    else:
        updated = (
            blend(momentum_heads_in, lax.dynamic_slice_in_dim(heads_in, dp * SH, SH, 1)),
            blend(momentum_heads_out, lax.dynamic_slice_in_dim(heads_out, dp * SH, SH, 1)),
            blend(momentum_expand_weight, lax.dynamic_slice_in_dim(expand_weight, dp * SH, SH, 0)),
            blend(momentum_shrink_weight, lax.dynamic_slice_in_dim(shrink_weight, dp * SH, SH, 1)),
        )
        whole = lambda a, axis: lax.all_gather(a.astype(BF16), "dp", axis=axis, tiled=True)
        ins += [("key_heads", jnp.concatenate([whole(updated[0], 1), whole(updated[1].T, 0)[None]], axis=0), any_),
                ("key_ffn", jnp.stack([whole(updated[2], 0), whole(updated[3].T, 0)]), any_)]
    scratch = [
        ("X", vm((2, 2, L, D), BF16)), ("wqi", vm((2, 3, D, HS), BF16)), ("wo", vm((2, HS, D), BF16)),
        ("we", vm((2, D, FS), BF16)), ("ws", vm((2, FS, D), BF16)),
        ("wkh", vm((2, 4, D, HS), BF16)), ("wkf", vm((2, 2, D, FS), BF16)),
        ("queue", vm((QN, D), BF16)), ("cot", vm((L, D), BF16)),
        ("hb", vm((2, 4, HS), F32)), ("eb", vm((2, TENSOR, FS), F32)),
        ("qkv", vm((2, 3, 2, L, HS), BF16)), ("G", vm((2, 2, L, 128), F32)), ("C", vm((2, 2, L, HS), BF16)),
        ("U", vm((2, 2, L, D), BF16)), ("Uf", vm((2, L, D), F32)), ("H", vm((2, 2, L, FS), BF16)),
        ("slope", vm((2, 2, L, FS), BF16)), ("N1", vm((L, D), F32)), ("N2", vm((L, D), F32)),
        ("i1", vm((L, 128), F32)), ("i2", vm((L, 128), F32)), ("own", vm((2, L, D), F32)), ("part", vm((L, D), F32)),
        ("asend", vm((2, L, D), BF16)), ("arecv", vm((2, L, D), BF16)), ("fsend", vm((2, L, D), BF16)),
        ("frecv", vm((2, L, D), BF16)), ("oq", vm((L, D), BF16)), ("ok", vm((L, D), BF16)),
        ("usend", vm((2, 8, 128), F32)), ("units", vm((2, N, 8, 128), F32)), ("nsend", vm((N, 8, 128), F32)),
        ("nrecv", vm((N, 8, 128), F32)), ("d2", vm((L, D), F32)), ("dF", vm((2, L, D), BF16)),
        ("dZ", vm((2, 2, L, FS), BF16)), ("dusend", vm((L, D), BF16)), ("durecv", vm((L, D), BF16)),
        ("dA", vm((2, L, D), BF16)), ("dqkv", vm((2, 3, 2, L, HS), BF16)),
        ("dxsend", vm((L, D), BF16)), ("dxrecv", vm((L, D), BF16)),
        ("wsend", vm((PIECES, PR, D), BF16)), ("wrecv", vm((PIECES, PR, D), BF16)),
        ("sm", vm((3 + DP.bit_length(), 16, D), F32)), ("smx", vm((16, D), F32)),
        ("smr", vm((2 + DP.bit_length(), 16, D), F32)),
    ]
    if gather:
        scratch += [
            ("mhi", vm(momentum_heads_in.shape, F32)), ("mho", vm(momentum_heads_out.shape, F32)),
            ("mex", vm(momentum_expand_weight.shape, F32)), ("msh", vm(momentum_shrink_weight.shape, F32)),
            ("wacc", vm((PIECES, PR, D), BF16)), ("wyr", vm((PIECES, PR // 2, D), BF16)),
            ("wys", vm((PIECES, PR // 2, D), BF16)), ("wzr", vm((PIECES, NZ - 1, PR // DP, D), BF16)),
            ("wout", vm((PIECES, PR, D), BF16)),
        ]
    else:
        scratch += [("wacc32", vm((PIECES, PR, D), F32))]
    dma = pltpu.SemaphoreType.DMA
    nx = 2 + 6 * NCH + 4 * NCH
    ng = 2 * (NZ - 1) + 2 * NZ + 2
    nw = PIECES * (2 + 2 * (NZ - 1) + NZ)
    nv = 3 * (N - 1)
    for pair, count in ((("xs", "xr"), nx), (("cs", "cr"), 5), (("gs", "gr"), ng), (("us", "ur"), nv),
                        (("ws_s", "ws_r"), nw), (("bs", "br"), 2 + DP.bit_length())):
        for name in pair:
            scratch.append((name, dma((count,))))
    scratch += [("lsem", dma((16,))), ("ssem", dma((16,)))]
    cfg.names = [n for n, *_ in ins] + [n for n, *_ in outs] + [n for n, _ in scratch]

    def body(*refs):
        kernel(cfg, *refs)

    res = pl.pallas_call(
        body,
        out_shape=[jax.ShapeDtypeStruct(s, d) for _, s, d in outs],
        in_specs=[s for _, _, s in ins],
        out_specs=[any_] * len(outs),
        scratch_shapes=[s for _, s in scratch],
        compiler_params=pltpu.CompilerParams(collective_id=0, has_side_effects=True, vmem_limit_bytes=cfg_limit()),
        name="step",
    )(*[a for _, a, _ in ins])
    query_out, key_out, d_tokens, grads, vectors = res[:5]
    if gather:
        up_in, up_out, up_expand, up_shrink = res[5:]
    else:
        up_in, up_out, up_expand, up_shrink = updated
        grads, vectors = lax.psum((grads, jnp.concatenate([vectors])), "dp")
    g_shrink = grads[0:2].reshape(FS, D).astype(F32)
    g_expand = grads[2:4].reshape(D, FS).astype(F32)
    heads = grads[4:6].reshape(D, D)
    g_in = jnp.swapaxes(heads[: 3 * HS].reshape(3, HS, D), 1, 2).astype(F32)
    g_out = heads[3 * HS :].astype(F32)
    up_eb = blend(momentum_expand_bias, expand_bias)
    return (
        query_out, key_out, vectors[6, 0], d_tokens, g_in, vectors[9:11, :HS], g_out, g_expand, vectors[8, :FS], g_shrink,
        vectors[0:2], vectors[2:4], vectors[4:6], up_in, blend(momentum_heads_bias, heads_bias), up_out, up_expand,
        lax.dynamic_slice_in_dim(up_eb, t * FS, FS, 0), up_shrink, blend(momentum_branch_bias, branch_bias),
        blend(momentum_norm_gain, norm_gain), blend(momentum_norm_shift, norm_shift),
    )


def cfg_limit():
    return 64 * 1024 * 1024 - 4096


def solution(mesh):
    both = ("dp", "tensor")
    in_specs = (
        P(both, None), P(both, None), P("dp"), P("dp"), P(), P(both, None), P(both, None), P(None, None, "tensor"),
        P(None, "tensor"), P("tensor", None), P(None, "tensor"), P(), P("tensor", None), P(), P(), P(),
        P(None, "dp", "tensor"), P(None, "tensor"), P("tensor", "dp"), P("dp", "tensor"), P(), P("tensor", "dp"), P(), P(), P(),
    )
    out_specs = (
        P(both, None), P(both, None), P(), P(both, None), P(None, None, "tensor"), P(None, "tensor"), P("tensor", None),
        P(None, "tensor"), P("tensor"), P("tensor", None), P(), P(), P(), P(None, "dp", "tensor"), P(None, "tensor"),
        P("tensor", "dp"), P("dp", "tensor"), P("tensor"), P("tensor", "dp"), P(), P(), P(),
    )
    shape = dict(mesh.shape)
    return jax.shard_map(lambda *a: local(shape, *a), mesh=mesh, in_specs=in_specs, out_specs=out_specs, check_vma=False)
```

```python
import types

import jax
import jax.numpy as jnp
from jax import lax
from jax.experimental import pallas as pl
from jax.experimental.pallas import tpu as pltpu
from jax.sharding import PartitionSpec as P

HEAD = 64
SOFTMAX_DIVISOR = 0.05
MOMENTUM = 0.5
NORM_EPSILON = 1e-12
MASKED_SCORE = -1e30
ROOT_HALF = 0.7071067811865476
GAUSS_SCALE = 0.3989422804014327
MESH = pl.DeviceIdType.MESH
F32, BF16 = jnp.float32, jnp.bfloat16
NN = (((1,), (0,)), ((), ()))
NT = (((1,), (1,)), ((), ()))
TN = (((0,), (0,)), ((), ()))
TENSOR = 4
PIECES = 6


def dot(a, b, dims=NN):
    return lax.dot_general(a, b, dims, preferred_element_type=F32)


def norm_rows(v, gain, shift):
    c = v - jnp.mean(v, axis=-1, keepdims=True)
    inverse = lax.rsqrt(jnp.mean(c * c, axis=-1, keepdims=True) + NORM_EPSILON)
    n = c * inverse
    return n * gain + shift, n, inverse


def norm_back(up, n, inverse, gain):
    e = up * gain
    inner = e - jnp.mean(e, axis=-1, keepdims=True) - n * jnp.mean(e * n, axis=-1, keepdims=True)
    return inner * inverse


def gelu_parts(z):
    a = jnp.abs(z) * ROOT_HALF
    g = jnp.exp(-0.5 * z * z)
    s = 1.0 / (1.0 + 0.3275911 * a)
    poly = ((((1.061405429 * s - 1.453152027) * s + 1.421413741) * s - 0.284496736) * s + 0.254829592) * s
    q = 0.5 * poly * g
    cdf = jnp.where(z >= 0, 1.0 - q, q)
    return z * cdf, cdf + z * GAUSS_SCALE * g


def pack(q, k, v, o):
    lo, hi = slice(0, 128), slice(128, 192)
    pair = lambda a, b: jnp.concatenate([a[:, hi], b[:, hi]], axis=1)
    tiles = [q[:, lo], pair(q, v), k[:, lo], v[:, lo], pair(k, o), o[:, lo]]
    return jnp.concatenate([a.astype(BF16) for a in tiles], axis=1)


def kernel(cfg, *refs):
    r = types.SimpleNamespace(**dict(zip(cfg.names, refs)))
    D, HS, FS, L, DP, RC = cfg.D, cfg.HS, cfg.FS, cfg.L, cfg.DP, cfg.RC
    N, SH, NZ = DP * TENSOR, cfg.SH, DP // 2
    NCH = L // RC
    dp, t = lax.axis_index("dp"), lax.axis_index("tensor")
    px = lax.rem(t + 2, TENSOR)
    sib = t + 1 - 2 * lax.rem(t, 2)
    y, z = lax.rem(dp, 2), dp // 2
    me = dp * TENSOR + t
    d_x, d_sib, d_y = (dp, px), (dp, sib), (dp + 1 - 2 * y, t)

    def d_z(k):
        return (lax.rem(z + k, NZ) * 2 + y, t)

    def from_z(k):
        return lax.rem(z - k + NZ, NZ)

    def remote(src, dst, sems, i, dev):
        return pltpu.make_async_remote_copy(
            src_ref=src, dst_ref=dst, send_sem=sems[0].at[i], recv_sem=sems[1].at[i], device_id=dev, device_id_type=MESH
        )

    sends = []

    def send(src, dst, sems, i, dev):
        c = remote(src, dst, sems, i, dev)
        c.start()
        sends.append(c)
        return c

    loads = {}

    def load(name, src, dst):
        c = pltpu.make_async_copy(src, dst, r.lsem.at[len(loads)])
        c.start()
        loads[name] = c

    stores = []

    def store(src, dst):
        c = pltpu.make_async_copy(src, dst, r.ssem.at[len(stores)])
        c.start()
        stores.append(c)

    xs, cs = (r.xs, r.xr), (r.cs, r.cr)

    load("q", r.query_tokens, r.X.at[0, 0])
    load("hi", r.heads_in, r.wqi.at[:, 0])
    load("wo", r.heads_out, r.wo.at[0])
    small_in = cfg.small
    for name in small_in:
        load(name, getattr(r, name), getattr(r, "v_" + name))
    if cfg.gather:
        load("mhi", r.momentum_heads_in, r.mhi)
        load("mo", r.momentum_heads_out, r.mho)
    load("we", r.expand_weight, r.we.at[0])
    load("ws", r.shrink_weight, r.ws.at[0])
    if cfg.gather:
        load("me", r.momentum_expand_weight, r.mex)
        load("ms", r.momentum_shrink_weight, r.msh)
    else:
        load("kw", r.key_weights, r.wk.at[0])
    load("k", r.key_tokens, r.X.at[1, 0])
    load("queue", r.key_queue, r.queue)
    load("cot", r.token_cotangent, r.cot)

    bar = pltpu.get_barrier_semaphore()

    def greet(i, c):
        o = lax.rem(me + i, N)
        pl.semaphore_signal(bar, inc=1, device_id=(o // TENSOR, lax.rem(o, TENSOR)), device_id_type=MESH)
        return c

    lax.fori_loop(1, N, greet, 0)
    pl.semaphore_wait(bar, N - 1)

    c_xq = send(r.query_tokens, r.X.at[0, 1], xs, 0, d_x)
    c_hi = send(r.heads_in, r.wqi.at[:, 1], cs, 0, d_sib)
    c_wo = send(r.heads_out, r.wo.at[1], cs, 1, d_sib)

    def small_blend(name):
        return MOMENTUM * getattr(r, "v_momentum_" + name)[...] + (1.0 - MOMENTUM) * getattr(r, "v_" + name)[...].astype(F32)

    for name in small_in:
        loads[name].wait()
    r.hb[0, 0:2, :] = r.v_heads_bias[...].astype(F32)
    r.hb[0, 2:4, :] = small_blend("heads_bias")
    c_hb = send(r.hb.at[0], r.hb.at[1], cs, 4, d_sib)
    bb = (r.v_branch_bias[...].astype(F32), small_blend("branch_bias"))
    gain = (r.v_norm_gain[...].astype(F32), small_blend("norm_gain"))
    shift = (r.v_norm_shift[...].astype(F32), small_blend("norm_shift"))
    for w, b in enumerate((r.v_expand_bias[...].astype(F32), small_blend("expand_bias"))):
        for k in range(TENSOR):
            for i in range(FS // 128):
                at = k * (FS // 128) + i
                r.eb[w, k : k + 1, i * 128 : i * 128 + 128] = b[at : at + 1, :]

    gs = (r.gs, r.gr)
    gy0, gc0 = 3 * (NZ - 1), 3 * (NZ - 1) + 3 * NZ

    def g_rows(part, owner):
        return r.wk.at[0, part, pl.ds(pl.multiple_of(owner * SH, SH), SH), :]

    gz, gy = {}, {}

    def g_start(part):
        rows = g_rows(part, dp)
        for k in range(1, NZ):
            gz[part, k] = send(rows, rows, gs, part * (NZ - 1) + k - 1, d_z(k))
        gy[part, 0] = send(rows, rows, gs, gy0 + part * NZ, d_y)

    def g_forward(part):
        for k in range(1, NZ):
            gz[part, k].wait_recv()
            rows = g_rows(part, from_z(k) * 2 + y)
            gy[part, k] = send(rows, rows, gs, gy0 + part * NZ + k, d_y)

    g_done = {}

    def g_sib(part):
        g_done[part] = send(r.wk.at[0, part], r.wk.at[1, part], gs, gc0 + part, d_sib)

    def g_finish(part):
        for k in range(NZ):
            gy[part, k].wait_recv()
        g_sib(part)

    if cfg.gather:
        own = pl.ds(pl.multiple_of(dp * SH, SH), SH)
        pick = (
            lax.broadcasted_iota(jnp.int32, (SH, D), 1) == lax.broadcasted_iota(jnp.int32, (SH, D), 0) + dp * SH
        ).astype(F32).astype(BF16)
        eye = (
            lax.broadcasted_iota(jnp.int32, (D, D), 0) == lax.broadcasted_iota(jnp.int32, (D, D), 1)
        ).astype(F32).astype(BF16)
        for name in ("hi", "mhi", "wo", "mo"):
            loads[name].wait()
        blocks = [
            MOMENTUM * r.mhi[i] + (1.0 - MOMENTUM) * dot(pick, r.wqi[i, 0], NT) for i in range(3)
        ]
        for i in range(3):
            r.mhi[i] = blocks[i]
        u = MOMENTUM * r.mho[...] + (1.0 - MOMENTUM) * dot(r.wo[0], pick, NT)
        r.mho[...] = u
        blocks.append(dot(eye[:SH, :SH], u.astype(BF16), NT))
        r.wk[0, 0, own, :] = pack(*blocks)
        g_start(0)
        for name in ("we", "me", "ws", "ms"):
            loads[name].wait()
        u = MOMENTUM * r.mex[...] + (1.0 - MOMENTUM) * r.we[0, own, :].astype(F32)
        r.mex[...] = u
        r.wk[0, 1, own, :] = u.astype(BF16)
        g_start(1)
        u = MOMENTUM * r.msh[...] + (1.0 - MOMENTUM) * dot(pick, r.ws[0], NT)
        r.msh[...] = u
        r.wk[0, 2, own, :] = u.astype(BF16)
        g_start(2)
        store(r.mhi, r.o_heads_in)
        store(r.mho, r.o_heads_out)
        store(r.mex, r.o_expand)
        store(r.msh, r.o_shrink)
    else:
        for name in ("hi", "wo", "we", "ws", "kw"):
            loads[name].wait()
        for part in range(3):
            g_sib(part)
    c_we = send(r.expand_weight, r.we.at[1], cs, 2, d_sib)
    c_ws = send(r.shrink_weight, r.ws.at[1], cs, 3, d_sib)

    lengths = ((r.query_lengths[t], r.query_lengths[px]), (r.key_lengths[t], r.key_lengths[px]))
    low_half = lax.broadcasted_iota(jnp.int32, (1, 128), 1) < HEAD
    key_at = lax.broadcasted_iota(jnp.int32, (1, L), 1)

    def split(tile):
        zero = jnp.zeros_like(tile)
        return jnp.where(low_half, tile, zero), jnp.where(low_half, zero, tile)

    def softmax(q, k, valid):
        sc = jnp.where(valid, dot(q, k, NT), MASKED_SCORE)
        top = jnp.max(sc, axis=-1, keepdims=True)
        e = jnp.exp(sc - top)
        tot = jnp.sum(e, axis=-1, keepdims=True)
        return (e * (1.0 / tot)).astype(BF16), top + jnp.log(tot)

    def scaled(v):
        return (v.astype(BF16).astype(F32) * HEAD**-0.5).astype(BF16)

    hpair = 2 * HS // 128

    def attend_query(crop, out):
        x = r.X[0, crop]
        valid = key_at < lengths[0][crop]
        q = scaled(dot(x, r.wqi[0].reshape(2 * HS, D), NT) + bias_q)
        k = dot(x, r.wqi[1].reshape(2 * HS, D), NT).astype(BF16)
        v = (dot(x, r.wqi[2].reshape(2 * HS, D), NT) + bias_v).astype(BF16)
        r.qkv[0, crop], r.qkv[1, crop], r.qkv[2, crop] = q, k, v
        at = lax.broadcasted_iota(jnp.int32, (L, 128), 1)
        logs = jnp.zeros((L, 128), F32)
        ctx = []
        for i in range(hpair):
            tile = slice(128 * i, 128 * i + 128)
            ks, vs = split(k[:, tile]), split(v[:, tile])
            c = None
            for h in range(2):
                p, g = softmax(q[:, tile], ks[h], valid)
                logs = jnp.where(at == 2 * i + h, g, logs)
                d = dot(p, vs[h])
                c = d if c is None else c + d
            ctx.append(c.astype(BF16))
        r.G[crop] = logs
        ctx = jnp.concatenate(ctx, axis=1)
        r.C[crop] = ctx
        out[...] = dot(ctx, r.wo[...].reshape(2 * HS, D))

    def attend_key(crop, out):
        x = r.X[1, crop]
        valid = key_at < lengths[1][crop]
        total = None
        for s in range(2):
            w = r.wk[s, 0]
            hb = r.hb[s]
            qb, vb, none = hb[2:3, :], hb[3:4, :], jnp.zeros((1, 128), F32)
            bias = jnp.concatenate(
                [qb[:, 0:128], jnp.concatenate([qb[:, 128:192], vb[:, 128:192]], axis=1), none, vb[:, 0:128], none], axis=1
            )
            pr = dot(x, w[:, 0:640]) + bias
            q01, m = pr[:, 0:128], pr[:, 128:256].astype(BF16)
            q01, q2 = scaled(q01), (m.astype(F32) * HEAD**-0.5).astype(BF16)
            k01, v01, k2 = (pr[:, 128 * i : 128 * i + 128].astype(BF16) for i in (2, 3, 4))
            ks, vs = split(k01), split(v01)
            p0, _ = softmax(q01, ks[0], valid)
            p1, _ = softmax(q01, ks[1], valid)
            p2, _ = softmax(q2, split(k2)[0], valid)
            c01 = (dot(p0, vs[0]) + dot(p1, vs[1])).astype(BF16)
            c2 = dot(p2, split(m)[1]).astype(BF16)
            a = dot(jnp.concatenate([c2, c01], axis=1), w[:, 512:768], NT)
            total = a if total is None else total + a
        out[...] = total

    def attend(w, crop, out):
        (attend_query, attend_key)[w](crop, out)

    def swap(src32, sbuf, rbuf, base):
        out = []
        for j in range(NCH):
            rows = pl.ds(j * RC, RC)
            sbuf[rows, :] = src32[rows, :].astype(BF16)
            out.append(send(sbuf.at[rows], rbuf.at[rows], xs, base + j, d_x))
        return out

    FT = 256

    def feed(w, crop, row0, rows_n, out):
        rows = pl.ds(row0, rows_n)
        u = r.U[w, crop, rows, :]

        total = None
        for i in range(2 * (FS // FT)):
            s, j = i // (FS // FT), i % (FS // FT)
            cols = slice(j * FT, j * FT + FT)
            b = r.eb[w, pl.ds(t if s == 0 else sib, 1), cols]
            if w == 0:
                zz = dot(u, r.we[s, :, cols]) + b
            else:
                zz = dot(u, r.wk[s, 1, :, cols]) + b
            h, slope = gelu_parts(zz)
            h = h.astype(BF16)
            if w == 0:
                r.H[s, crop, rows, cols] = h
                r.slope[s, crop, rows, cols] = slope.astype(BF16)
                f = dot(h, r.ws[s, cols, :])
            else:
                f = dot(h, r.wk[s, 2, :, cols], NT)

            total = f if total is None else total + f
        out[rows, :] = total

    x_of = {}

    def first_norm(w, base):
        out = []
        for j in range(NCH):
            rows = pl.ds(j * RC, RC)
            x_of["A", w][j].wait_recv()
            m = r.X[w, 0, rows, :].astype(F32) + (r.own[w, rows, :] + r.arecv[w, rows, :].astype(F32)) + bb[w][0:1, :]
            u, n, inv = norm_rows(m, gain[w][0:1, :], shift[w][0:1, :])
            r.Uf[w, rows, :] = u
            r.U[w, 0, rows, :] = u.astype(BF16)
            if w == 0:
                r.N1[rows, :] = n
                r.i1[rows, :] = jnp.broadcast_to(inv, (RC, 128))
            out.append(send(r.U.at[w, 0, rows], r.U.at[w, 1, rows], xs, base + j, d_x))
        x_of["U", w] = out

    def second_norm(w, o_ref, o_hbm):
        pooled = jnp.zeros((1, D), F32)
        length = lengths[w][0]
        for j in range(NCH):
            rows = pl.ds(j * RC, RC)
            x_of["F", w][j].wait_recv()
            m = r.Uf[w, rows, :] + (r.own[w, rows, :] + r.frecv[w, rows, :].astype(F32)) + bb[w][1:2, :]
            out, n, inv = norm_rows(m, gain[w][1:2, :], shift[w][1:2, :])
            o_ref[rows, :] = out.astype(BF16)
            if w == 0:
                r.N2[rows, :] = n
                r.i2[rows, :] = jnp.broadcast_to(inv, (RC, 128))
            valid = lax.broadcasted_iota(jnp.int32, (RC, 1), 0) + j * RC < length
            pooled += jnp.sum(jnp.where(valid, out, 0.0), axis=0, keepdims=True)
        store(o_ref, o_hbm)
        pooled = pooled / length.astype(F32)
        inverse = lax.rsqrt(jnp.sum(pooled * pooled, axis=-1, keepdims=True) + 1e-06)
        unit = (pooled * inverse).astype(BF16).astype(F32)
        return pooled, inverse, unit

    KL = D // 128

    def tile_of(row):
        return jnp.concatenate([row[:, i * 128 : (i + 1) * 128] for i in range(KL)], axis=0)

    def to_all(sbuf_of, rbuf, sems, base):
        def go(i, c):
            o = lax.rem(me + i, N)
            remote(sbuf_of(o), rbuf.at[me], sems, base + i - 1, (o // TENSOR, lax.rem(o, TENSOR))).start()
            return c

        lax.fori_loop(1, N, go, 0)

    def from_all(rbuf, sems, base):
        def go(i, c):
            o = lax.rem(me - i + N, N)
            remote(rbuf.at[o], rbuf.at[o], sems, base + i - 1, d_x).wait_recv()
            return c

        lax.fori_loop(1, N, go, 0)

    def sent_all(sbuf, sems, base):
        def go(i, c):
            remote(sbuf.at[0], sbuf.at[0], sems, base + i - 1, d_x).wait_send()
            return c

        lax.fori_loop(1, N, go, 0)

    us = (r.us, r.ur)

    loads["q"].wait()
    c_hi.wait_recv()
    c_wo.wait_recv()
    c_hb.wait_recv()
    bias_q = jnp.concatenate([r.hb[0, 0:1, :], r.hb[1, 0:1, :]], axis=1)
    bias_v = jnp.concatenate([r.hb[0, 1:2, :], r.hb[1, 1:2, :]], axis=1)
    attend(0, 0, r.own.at[0])
    c_xq.wait_recv()
    c_xk = send(r.key_tokens, r.X.at[1, 1], xs, 1, d_x)
    attend(0, 1, r.part)
    x_of["A", 0] = swap(r.part, r.asend.at[0], r.arecv.at[0], 2)
    if cfg.gather:
        g_forward(0)
    c_we.wait_recv()
    c_ws.wait_recv()
    first_norm(0, 2 + NCH)
    feed(0, 0, 0, L, r.own.at[0])
    if cfg.gather:
        g_forward(1)
        g_finish(0)
    for j in range(NCH):
        x_of["U", 0][j].wait_recv()
        feed(0, 1, j * RC, RC, r.part)
        if j == 0:
            x_of["F", 0] = []
        rows = pl.ds(j * RC, RC)
        r.fsend[0, rows, :] = r.part[rows, :].astype(BF16)
        x_of["F", 0].append(send(r.fsend.at[0, rows], r.frecv.at[0, rows], xs, 2 + 2 * NCH + j, d_x))
    kb = 2 + 3 * NCH
    c_xk.wait_recv()
    loads["k"].wait()
    g_done[0].wait_recv()
    attend(1, 1, r.part)
    x_of["A", 1] = swap(r.part, r.asend.at[1], r.arecv.at[1], kb)
    if cfg.gather:
        g_finish(1)
        g_forward(2)
    attend(1, 0, r.own.at[1])
    q_pooled, q_inverse, q_unit = second_norm(0, r.oq, r.query_output)
    r.usend[0, 0:KL, :] = tile_of(q_unit)
    r.units[0, me, 0:KL, :] = tile_of(q_unit)
    to_all(lambda o: r.usend.at[0], r.units.at[0], us, 0)
    first_norm(1, kb + NCH)
    if cfg.gather:
        g_finish(2)
    g_done[1].wait_recv()
    g_done[2].wait_recv()
    feed(1, 0, 0, L, r.own.at[1])
    for j in range(NCH):
        x_of["U", 1][j].wait_recv()
        feed(1, 1, j * RC, RC, r.part)
        if j == 0:
            x_of["F", 1] = []
        rows = pl.ds(j * RC, RC)
        r.fsend[1, rows, :] = r.part[rows, :].astype(BF16)
        x_of["F", 1].append(send(r.fsend.at[1, rows], r.frecv.at[1, rows], xs, kb + 2 * NCH + j, d_x))
    loads["queue"].wait()
    from_all(r.units.at[0], us, 0)
    all_q = jnp.concatenate([r.units[0, :, i, :] for i in range(KL)], axis=1).astype(BF16)
    logits = dot(all_q, r.queue[...], NT) / SOFTMAX_DIVISOR
    top = jnp.max(logits, axis=-1, keepdims=True)
    e = jnp.exp(logits - top)
    tot = jnp.sum(e, axis=-1, keepdims=True)
    grad = dot(e.astype(BF16), r.queue[...])
    for i in range(KL):
        r.nsend[:, i, :] = grad[:, i * 128 : (i + 1) * 128]
    r.nsend[:, KL, :] = jnp.broadcast_to(top, (N, 128))
    r.nsend[:, KL + 1, :] = jnp.broadcast_to(tot, (N, 128))
    r.nrecv[me] = r.nsend[me]
    to_all(lambda o: r.nsend.at[o], r.nrecv, us, N - 1)
    k_pooled, k_inverse, k_unit = second_norm(1, r.ok, r.key_output)
    r.usend[1, 0:KL, :] = tile_of(k_unit)
    r.units[1, me, 0:KL, :] = tile_of(k_unit)
    to_all(lambda o: r.usend.at[1], r.units.at[1], us, 2 * (N - 1))
    from_all(r.nrecv, us, N - 1)
    from_all(r.units.at[1], us, 2 * (N - 1))

    pos = r.positives[me]
    hit = lax.broadcasted_iota(jnp.int32, (N, 1, 1), 0) == pos
    partner = jnp.sum(jnp.where(hit, r.units[1][:, 0:KL, :], 0.0), axis=0)
    mine = r.usend[0, 0:KL, :]
    match = jnp.sum(jnp.sum(mine * partner, axis=1, keepdims=True), axis=0, keepdims=True) / SOFTMAX_DIVISOR
    tops, tots = r.nrecv[:, KL, :], r.nrecv[:, KL + 1, :]
    peak = jnp.maximum(jnp.max(jnp.max(tops, axis=0, keepdims=True), axis=1, keepdims=True), match)
    total = jnp.sum(tots * jnp.exp(tops - peak), axis=0, keepdims=True)[:, 0:1]
    level = peak + jnp.log(total + jnp.exp(match - peak))
    loss = level - match
    scale = jnp.exp(r.nrecv[:, KL : KL + 1, :] - level.reshape(1, 1, 1)) * (1.0 / SOFTMAX_DIVISOR)
    du = jnp.sum(r.nrecv[:, 0:KL, :] * scale, axis=0) + (jnp.exp(match - level) - 1.0) / SOFTMAX_DIVISOR * partner
    du = jnp.concatenate([du[i : i + 1, :] for i in range(KL)], axis=1)
    along = jnp.sum(q_pooled * du, axis=-1, keepdims=True)
    d_pooled = q_inverse * du - q_pooled * (q_inverse * q_inverse * q_inverse) * along
    per_token = d_pooled / lengths[0][0].astype(F32)

    loads["cot"].wait()
    bbase = kb + 3 * NCH
    small = [jnp.zeros((1, D), F32) for _ in range(6)]
    x_of["dF"] = []
    for j in range(NCH):
        rows = pl.ds(j * RC, RC)
        valid = lax.broadcasted_iota(jnp.int32, (RC, 1), 0) + j * RC < lengths[0][0]
        dy = r.cot[rows, :].astype(F32) + jnp.where(valid, per_token, 0.0)
        n2 = r.N2[rows, :]
        d2 = norm_back(dy, n2, r.i2[rows, 0:1], gain[0][1:2, :])
        r.d2[rows, :] = d2
        r.dF[0, rows, :] = d2.astype(BF16)
        x_of["dF"].append(send(r.dF.at[0, rows], r.dF.at[1, rows], xs, bbase + j, d_x))
        small[1] += jnp.sum(d2, axis=0, keepdims=True)
        small[3] += jnp.sum(dy * n2, axis=0, keepdims=True)
        small[5] += jnp.sum(dy, axis=0, keepdims=True)

    def feed_back(crop, row0, rows_n, out):
        rows = pl.ds(row0, rows_n)
        df = r.dF[crop, rows, :]

        total = None
        for i in range(2 * (FS // FT)):
            s, j = i // (FS // FT), i % (FS // FT)
            cols = slice(j * FT, j * FT + FT)
            dh = dot(df, r.ws[s, cols, :], NT)
            dz = (dh * r.slope[s, crop, rows, cols].astype(F32)).astype(BF16)
            r.dZ[s, crop, rows, cols] = dz
            du_ = dot(dz, r.we[s, :, cols], NT)

            total = du_ if total is None else total + du_
        out[rows, :] = total

    feed_back(0, 0, L, r.own.at[0])
    x_of["dU"] = []
    for j in range(NCH):
        x_of["dF"][j].wait_recv()
        feed_back(1, j * RC, RC, r.part)
        rows = pl.ds(j * RC, RC)
        r.dusend[rows, :] = r.part[rows, :].astype(BF16)
        x_of["dU"].append(send(r.dusend.at[rows], r.durecv.at[rows], xs, bbase + NCH + j, d_x))

    PR = 3 * 2 * D // (2 * 3) // 2
    HF, CH = PR // 2, PR // 2 // max(NZ, 1)
    ws_sem = (r.ws_s, r.ws_r)
    per = 2 + 2 * (NZ - 1) + NZ

    def piece_part(p, s):
        if p < 2:
            h = r.H[s].reshape(2 * L, FS)[:, p * PR : (p + 1) * PR]
            return dot(h, r.dF[...].reshape(2 * L, D), TN)
        u = r.U[0].reshape(2 * L, D)[:, (p - 2) * PR : (p - 1) * PR]
        return dot(u, r.dZ[s].reshape(2 * L, FS), TN)

    w_of = {}

    def w_sib_send(p):
        w_of["s", p] = send(r.wsend.at[p], r.wrecv.at[p], ws_sem, p * per, d_sib)

    def w_sib(p):
        if p < 4:
            r.wsend[p] = piece_part(p, 1).astype(BF16)
        else:
            for q in range(2):
                i = (p - 4) * 2 + q
                a = r.dqkv[i].reshape(2 * L, 2 * HS) if i < 3 else r.C[...].reshape(2 * L, 2 * HS)
                b = r.X[0].reshape(2 * L, D) if i < 3 else r.dA[...].reshape(2 * L, D)
                v = dot(a, b, TN)
                rows = slice(q * HS, (q + 1) * HS)
                r.hacc[p - 4, rows, :] = v[0:HS, :]
                r.wsend[p, rows, :] = v[HS:, :].astype(BF16)
        w_sib_send(p)

    def half(h):
        return pl.ds(pl.multiple_of(h * HF, HF), HF)

    def w_own(p):
        v = piece_part(p, 0) if p < 4 else r.hacc[p - 4]
        w_of["s", p].wait_recv()
        v = v + r.wrecv[p].astype(F32)
        if cfg.gather:
            r.wacc[p] = v.astype(BF16)
        else:
            r.wacc32[p] = v
        if cfg.gather:
            w_of["y", p] = send(r.wacc.at[p, half(1 - y)], r.wyr.at[p], ws_sem, p * per + 1, d_y)
        else:
            store(r.wacc32.at[p], r.grads.at[p])

    def chunk(zz):
        return pl.ds(pl.multiple_of(zz * CH, CH), CH)

    def place(yy, zz):
        return pl.ds(pl.multiple_of(yy * HF + zz * CH, CH), CH)

    def w_y(p):
        w_of["y", p].wait_recv()
        r.wys[p] = (r.wacc[p, half(y), :].astype(F32) + r.wyr[p].astype(F32)).astype(BF16)
        for k in range(1, NZ):
            to = lax.rem(z + k, NZ)
            w_of["z", p, k] = send(r.wys.at[p, chunk(to)], r.wzr.at[p, k - 1], ws_sem, p * per + 1 + k, d_z(k))

    def w_z(p):
        v = r.wys[p, chunk(z), :].astype(F32)
        for k in range(1, NZ):
            w_of["z", p, k].wait_recv()
            v += r.wzr[p, k - 1].astype(F32)
        at = place(y, z)
        r.wout[p, at, :] = v.astype(BF16)
        for k in range(1, NZ):
            w_of["a", p, k] = send(r.wout.at[p, at], r.wout.at[p, at], ws_sem, p * per + NZ + k, d_z(k))
        w_of["b", p, 0] = send(r.wout.at[p, at], r.wout.at[p, at], ws_sem, p * per + 2 * NZ, d_y)

    def w_a(p):
        for k in range(1, NZ):
            w_of["a", p, k].wait_recv()
            at = place(y, from_z(k))
            w_of["b", p, k] = send(r.wout.at[p, at], r.wout.at[p, at], ws_sem, p * per + 2 * NZ + k, d_y)

    def w_b(p):
        for k in range(NZ):
            w_of["b", p, k].wait_recv()
        store(r.wout.at[p], r.grads.at[p])

    if not cfg.gather:
        w_y = w_z = w_a = w_b = lambda p: None

    for p in range(4):
        w_sib(p)
    for p in range(4):
        w_own(p)

    x_of["dA"] = []
    for j in range(NCH):
        rows = pl.ds(j * RC, RC)
        x_of["dU"][j].wait_recv()
        du1 = r.d2[rows, :] + (r.own[0, rows, :] + r.durecv[rows, :].astype(F32))
        n1 = r.N1[rows, :]
        dm = norm_back(du1, n1, r.i1[rows, 0:1], gain[0][0:1, :])
        r.Uf[0, rows, :] = dm
        r.dA[0, rows, :] = dm.astype(BF16)
        x_of["dA"].append(send(r.dA.at[0, rows], r.dA.at[1, rows], xs, bbase + 2 * NCH + j, d_x))
        small[0] += jnp.sum(dm, axis=0, keepdims=True)
        small[2] += jnp.sum(du1 * n1, axis=0, keepdims=True)
        small[4] += jnp.sum(du1, axis=0, keepdims=True)
    for i in range(6):
        r.sm[0, i : i + 1, :] = small[i]
    r.sm[0, 6:7, :] = jnp.broadcast_to(loss, (1, D))
    w_y(0)

    def attend_back(crop, out):
        valid = key_at < lengths[0][crop]
        dc = dot(r.dA[crop], r.wo[...].reshape(2 * HS, D), NT).astype(BF16)
        q, k, v, g = r.qkv[0, crop], r.qkv[1, crop], r.qkv[2, crop], r.G[crop]
        grads = ([], [], [])
        for i in range(hpair):
            tile = slice(128 * i, 128 * i + 128)
            qt, dct = q[:, tile], dc[:, tile]
            qs, ks, vs, dcs = split(qt), split(k[:, tile]), split(v[:, tile]), split(dct)
            acc = None
            for h in range(2):
                sc = jnp.where(valid, dot(qt, ks[h], NT), MASKED_SCORE)
                pw = jnp.exp(sc - g[:, 2 * i + h : 2 * i + h + 1])
                dpw = dot(dct, vs[h], NT)
                inner = jnp.sum(dpw * pw, axis=-1, keepdims=True)
                ds = (pw * (dpw - inner)).astype(BF16)
                new = (dot(ds, ks[h]), dot(ds, qs[h], TN), dot(pw.astype(BF16), dcs[h], TN))
                acc = new if acc is None else tuple(a + b for a, b in zip(acc, new))
            for m, (into, a) in enumerate(zip(grads, acc)):
                into.append((a * HEAD**-0.5 if m == 0 else a).astype(BF16))
        total = None
        for m in range(3):
            d = jnp.concatenate(grads[m], axis=1)
            r.dqkv[m, crop] = d
            a = dot(d, r.wqi[m].reshape(2 * HS, D))
            total = a if total is None else total + a
        out[...] = total

    attend_back(0, r.own.at[1])
    w_y(1)
    w_z(0)
    for j in range(NCH):
        x_of["dA"][j].wait_recv()
    attend_back(1, r.part)
    x_of["dX"] = swap(r.part, r.dxsend, r.dxrecv, bbase + 3 * NCH)
    w_sib(4)
    w_sib(5)

    bq = jnp.sum(r.dqkv[0].reshape(2 * L, 2 * HS).astype(F32), axis=0, keepdims=True)
    bv = jnp.sum(r.dqkv[2].reshape(2 * L, 2 * HS).astype(F32), axis=0, keepdims=True)
    for s in range(2):
        eb = jnp.sum(r.dZ[s].reshape(2 * L, FS).astype(F32), axis=0, keepdims=True)
        dst = (r.sm.at[0], r.smx)[s]
        dst[8:9, 0:FS] = eb
        dst[9:10, 0:HS] = bq[:, s * HS : (s + 1) * HS]
        dst[10:11, 0:HS] = bv[:, s * HS : (s + 1) * HS]
    r.smx[0:8, :] = r.sm[0, 0:8, :]
    bs = (r.bs, r.br)
    send(r.smx, r.smr.at[0], bs, 0, d_sib).wait_recv()
    r.sm[1] = r.sm[0] + r.smr[0]
    b_x = send(r.sm.at[1, 0:8], r.smr.at[1, 0:8], bs, 1, d_x)
    w_own(4)
    w_own(5)
    w_y(2)
    w_z(1)
    b_x.wait_recv()
    r.sm[2] = r.sm[1]
    r.sm[2, 0:8, :] = r.sm[1, 0:8, :] + r.smr[1, 0:8, :]
    nb = DP.bit_length() - 1 if cfg.gather else 0

    def butterfly(k):
        other = dp + (1 - 2 * lax.rem(dp // (1 << k), 2)) * (1 << k)
        return send(r.sm.at[2 + k], r.smr.at[2 + k], bs, 2 + k, (other, t))

    def add_up(k, c):
        c.wait_recv()
        r.sm[3 + k] = r.sm[2 + k] + r.smr[2 + k]

    b_k = butterfly(0) if nb else None
    for j in range(NCH):
        rows = pl.ds(j * RC, RC)
        x_of["dX"][j].wait_recv()
        r.Uf[1, rows, :] = r.Uf[0, rows, :] + (r.own[1, rows, :] + r.dxrecv[rows, :].astype(F32))
    store(r.Uf.at[1], r.input_gradient)
    order = [(w_y, 3), (w_z, 2), (w_a, 0), (w_y, 4), (w_z, 3), (w_a, 1), (w_y, 5), (w_z, 4), (w_a, 2), (w_b, 0), (w_z, 5),
             (w_a, 3), (w_b, 1), (w_a, 4), (w_b, 2), (w_a, 5), (w_b, 3), (w_b, 4), (w_b, 5)]
    for n, (f, p) in enumerate(order):
        f(p)
        if nb and n % 3 == 0 and n // 3 < nb:
            k = n // 3
            add_up(k, b_k)
            b_k = butterfly(k + 1) if k + 1 < nb else None
    store(r.sm.at[2 + nb], r.vectors)

    for c in sends:
        c.wait_send()
    sent_all(r.usend, us, 0)
    sent_all(r.usend, us, N - 1)
    sent_all(r.usend, us, 2 * (N - 1))
    for c in stores:
        c.wait()


def blend(old, new):
    return MOMENTUM * old + (1.0 - MOMENTUM) * new.astype(F32)


def local(mesh_shape, query_tokens, key_tokens, query_lengths, key_lengths, positives, key_queue, token_cotangent, heads_in,
          heads_bias, heads_out, expand_weight, expand_bias, shrink_weight, branch_bias, norm_gain, norm_shift,
          momentum_heads_in, momentum_heads_bias, momentum_heads_out, momentum_expand_weight, momentum_expand_bias,
          momentum_shrink_weight, momentum_branch_bias, momentum_norm_gain, momentum_norm_shift):
    DP = mesh_shape["dp"]
    L, D = query_tokens.shape
    HS, FS = heads_in.shape[2], expand_weight.shape[1]
    SH = D // DP
    N = DP * TENSOR
    PR = D // 2
    QN = key_queue.shape[0]
    gather = SH % 16 == 0 and (PR // DP) % 16 == 0
    RC = 128
    NCH = L // RC
    NZ = DP // 2
    t, dp = lax.axis_index("tensor"), lax.axis_index("dp")
    cfg = types.SimpleNamespace(D=D, HS=HS, FS=FS, L=L, DP=DP, SH=SH, RC=RC, gather=gather)

    vm = lambda shape, dtype: pltpu.VMEM(shape, dtype)
    any_, vmem, smem = (pl.BlockSpec(memory_space=m) for m in (pl.ANY, pltpu.VMEM, pltpu.SMEM))
    small = {
        "heads_bias": heads_bias, "expand_bias": expand_bias.reshape(-1, 128), "branch_bias": branch_bias,
        "norm_gain": norm_gain, "norm_shift": norm_shift, "momentum_heads_bias": momentum_heads_bias,
        "momentum_expand_bias": momentum_expand_bias.reshape(-1, 128), "momentum_branch_bias": momentum_branch_bias,
        "momentum_norm_gain": momentum_norm_gain, "momentum_norm_shift": momentum_norm_shift,
    }
    cfg.small = list(small)
    ins = [
        ("query_tokens", query_tokens, any_), ("key_tokens", key_tokens, any_),
        ("query_lengths", query_lengths, smem), ("key_lengths", key_lengths, smem), ("positives", positives, smem),
        ("key_queue", key_queue, any_), ("token_cotangent", token_cotangent, any_),
        ("heads_in", jnp.swapaxes(heads_in, 1, 2), any_), ("heads_out", heads_out, any_),
        ("expand_weight", expand_weight, any_), ("shrink_weight", shrink_weight, any_),
    ] + [(n, a, any_) for n, a in small.items()]
    outs = [
        ("query_output", (L, D), BF16), ("key_output", (L, D), BF16), ("input_gradient", (L, D), F32),
        ("grads", (PIECES, PR, D), BF16 if gather else F32), ("vectors", (16, D), F32),
    ]
    if gather:
        ins += [("momentum_heads_in", momentum_heads_in, any_), ("momentum_heads_out", momentum_heads_out, any_),
                ("momentum_expand_weight", momentum_expand_weight, any_),
                ("momentum_shrink_weight", momentum_shrink_weight.T, any_)]
        outs += [("o_heads_in", momentum_heads_in.shape, F32), ("o_heads_out", momentum_heads_out.shape, F32),
                 ("o_expand", momentum_expand_weight.shape, F32), ("o_shrink", momentum_shrink_weight.shape[::-1], F32)]
    else:
        updated = (
            blend(momentum_heads_in, lax.dynamic_slice_in_dim(heads_in, dp * SH, SH, 1)),
            blend(momentum_heads_out, lax.dynamic_slice_in_dim(heads_out, dp * SH, SH, 1)),
            blend(momentum_expand_weight, lax.dynamic_slice_in_dim(expand_weight, dp * SH, SH, 0)),
            blend(momentum_shrink_weight, lax.dynamic_slice_in_dim(shrink_weight, dp * SH, SH, 1)),
        )
        whole = lambda a, axis: lax.all_gather(a.astype(BF16), "dp", axis=axis, tiled=True)
        heads = jnp.concatenate([whole(updated[0], 1), whole(updated[1].T, 0)[None]], axis=0)
        ins += [("key_weights", jnp.stack([pack(*heads), whole(updated[2], 0), whole(updated[3].T, 0)]), any_)]
    scratch = [
        ("X", vm((2, 2, L, D), BF16)), ("wqi", vm((3, 2, HS, D), BF16)), ("wo", vm((2, HS, D), BF16)),
        ("we", vm((2, D, FS), BF16)), ("ws", vm((2, FS, D), BF16)),
        ("wk", vm((2, 3, D, D), BF16)),
        ("queue", vm((QN, D), BF16)), ("cot", vm((L, D), BF16)),
        ("hb", vm((2, 4, HS), F32)), ("eb", vm((2, TENSOR, FS), F32)),
        ("qkv", vm((3, 2, L, 2 * HS), BF16)), ("G", vm((2, L, 128), F32)), ("C", vm((2, L, 2 * HS), BF16)),
        ("U", vm((2, 2, L, D), BF16)), ("Uf", vm((2, L, D), F32)), ("H", vm((2, 2, L, FS), BF16)),
        ("slope", vm((2, 2, L, FS), BF16)), ("N1", vm((L, D), F32)), ("N2", vm((L, D), F32)),
        ("i1", vm((L, 128), F32)), ("i2", vm((L, 128), F32)), ("own", vm((2, L, D), F32)), ("part", vm((L, D), F32)),
        ("asend", vm((2, L, D), BF16)), ("arecv", vm((2, L, D), BF16)), ("fsend", vm((2, L, D), BF16)),
        ("frecv", vm((2, L, D), BF16)), ("oq", vm((L, D), BF16)), ("ok", vm((L, D), BF16)),
        ("usend", vm((2, 8, 128), F32)), ("units", vm((2, N, 8, 128), F32)), ("nsend", vm((N, 8, 128), F32)),
        ("nrecv", vm((N, 8, 128), F32)), ("d2", vm((L, D), F32)), ("dF", vm((2, L, D), BF16)),
        ("dZ", vm((2, 2, L, FS), BF16)), ("dusend", vm((L, D), BF16)), ("durecv", vm((L, D), BF16)),
        ("dA", vm((2, L, D), BF16)), ("dqkv", vm((3, 2, L, 2 * HS), BF16)), ("hacc", vm((2, PR, D), F32)),
        ("dxsend", vm((L, D), BF16)), ("dxrecv", vm((L, D), BF16)),
        ("wsend", vm((PIECES, PR, D), BF16)), ("wrecv", vm((PIECES, PR, D), BF16)),
        ("sm", vm((3 + DP.bit_length(), 16, D), F32)), ("smx", vm((16, D), F32)),
        ("smr", vm((2 + DP.bit_length(), 16, D), F32)),
    ]
    if gather:
        scratch += [
            ("mhi", vm(momentum_heads_in.shape, F32)), ("mho", vm(momentum_heads_out.shape, F32)),
            ("mex", vm(momentum_expand_weight.shape, F32)), ("msh", vm(momentum_shrink_weight.shape[::-1], F32)),
            ("wacc", vm((PIECES, PR, D), BF16)), ("wyr", vm((PIECES, PR // 2, D), BF16)),
            ("wys", vm((PIECES, PR // 2, D), BF16)), ("wzr", vm((PIECES, NZ - 1, PR // DP, D), BF16)),
            ("wout", vm((PIECES, PR, D), BF16)),
        ]
    else:
        scratch += [("wacc32", vm((PIECES, PR, D), F32))]
    scratch += [("v_" + n, vm(a.shape, a.dtype)) for n, a in small.items()]
    dma = pltpu.SemaphoreType.DMA
    nx = 2 + 6 * NCH + 4 * NCH
    ng = 3 * (NZ - 1) + 3 * NZ + 3
    nw = PIECES * (2 + 2 * (NZ - 1) + NZ)
    nv = 3 * (N - 1)
    for pair, count in ((("xs", "xr"), nx), (("cs", "cr"), 5), (("gs", "gr"), ng), (("us", "ur"), nv),
                        (("ws_s", "ws_r"), nw), (("bs", "br"), 2 + DP.bit_length())):
        for name in pair:
            scratch.append((name, dma((count,))))
    scratch += [("lsem", dma((32,))), ("ssem", dma((16,)))]
    cfg.names = [n for n, *_ in ins] + [n for n, *_ in outs] + [n for n, _ in scratch]

    def body(*refs):
        kernel(cfg, *refs)

    res = pl.pallas_call(
        body,
        out_shape=[jax.ShapeDtypeStruct(s, d) for _, s, d in outs],
        in_specs=[s for _, _, s in ins],
        out_specs=[any_] * len(outs),
        scratch_shapes=[s for _, s in scratch],
        compiler_params=pltpu.CompilerParams(collective_id=0, has_side_effects=True, vmem_limit_bytes=cfg_limit()),
        name="step",
    )(*[a for _, a, _ in ins])
    query_out, key_out, d_tokens, grads, vectors = res[:5]
    if gather:
        updates = res[5:]
    else:
        updates = (updated[0], updated[1], updated[2], updated[3].T)
        grads, vectors = lax.psum((grads, vectors), "dp")
    copies = (query_out, key_out, d_tokens) + tuple(updates)
    fin = types.SimpleNamespace(D=D, HS=HS, FS=FS, small=list(small))
    out = [jax.ShapeDtypeStruct(a.shape, a.dtype) for a in copies]
    out += [jax.ShapeDtypeStruct(sh, F32) for sh in ((FS, D), (D, FS), (3, HS, D), (HS, D))]
    tiny = ((1, 1), (2, HS), (FS // 128, 128), (2, D), (2, D), (2, D), (2, HS), (FS // 128, 128), (2, D), (2, D), (2, D))
    out += [jax.ShapeDtypeStruct(sh, F32) for sh in tiny]
    out_dmas = len(copies) + 7 + len(tiny)
    done = pl.pallas_call(
        lambda *a: finish(fin, *a),
        out_shape=out,
        in_specs=[any_] * (len(copies) + 2 + len(small)),
        out_specs=[any_] * len(out),
        scratch_shapes=[vm(a.shape, a.dtype) for a in small.values()] + [vm(sh, F32) for sh in tiny]
        + [vm(a.shape, a.dtype) for a in copies]
        + [vm(vectors.shape, F32), vm((PIECES, PR, D), grads.dtype), vm((PIECES, PR, D), F32), dma((32,)), dma((out_dmas,))],
        compiler_params=pltpu.CompilerParams(vmem_limit_bytes=cfg_limit()),
        name="finish",
    )(*copies, grads, vectors, *small.values())
    (query_out, key_out, d_tokens, up_in, up_out, up_expand, up_shrink, g_shrink, g_expand, g_in, g_out, loss, g_hb, g_eb,
     g_bias, g_gain, g_shift, up_hb, up_eb, up_bias, up_gain, up_shift) = done
    return (
        query_out, key_out, loss[0, 0], d_tokens, jnp.swapaxes(g_in, 1, 2), g_hb, g_out, g_expand, g_eb.reshape(FS), g_shrink,
        g_bias, g_gain, g_shift, up_in, up_hb, up_out, up_expand, up_eb.reshape(FS), up_shrink.T, up_bias, up_gain, up_shift,
    )


def finish(fin, *refs):
    HS = fin.HS
    ns, n, nt = len(fin.small), 7, 11
    src, grads, vectors, small = refs[:n], refs[n], refs[n + 1], refs[n + 2 : n + 2 + ns]
    outs, scratch = refs[n + 2 + ns : n + 2 + ns + n + 4 + nt], refs[n + 2 + ns + n + 4 + nt :]
    v = dict(zip(fin.small, scratch[:ns]))
    tiny, held = scratch[ns : ns + nt], scratch[ns + nt : ns + nt + n]
    vecs, low, wide, isem, osem = scratch[ns + nt + n :]
    dst, (g_shrink, g_expand, g_in, g_out), tiny_out = outs[:n], outs[n : n + 4], outs[n + 4 :]
    loss, g_hb, g_eb, g_bias, g_gain, g_shift, up_hb, up_eb, up_bias, up_gain, up_shift = tiny
    PR = low.shape[1]
    ins = [pltpu.make_async_copy(grads.at[p], low.at[p], isem.at[p]) for p in range(PIECES)]
    ins += [pltpu.make_async_copy(a, b, isem.at[PIECES + i]) for i, (a, b) in enumerate(zip(small, scratch))]
    ins.append(pltpu.make_async_copy(vectors, vecs, isem.at[PIECES + ns]))
    ins += [pltpu.make_async_copy(a, b, isem.at[PIECES + ns + 1 + i]) for i, (a, b) in enumerate(zip(src, held))]
    for c in ins:
        c.start()
    for c in ins[PIECES:]:
        c.wait()
    waits = [pltpu.make_async_copy(a, b, osem.at[i]) for i, (a, b) in enumerate(zip(held, dst))]
    for c in waits:
        c.start()
    t = lax.axis_index("tensor")
    whole = vecs[...]
    loss[...] = whole[6:7, 0:1]
    g_hb[...] = whole[9:11, 0:HS]
    g_bias[...], g_gain[...], g_shift[...] = whole[0:2, :], whole[2:4, :], whole[4:6, :]
    for name, o in (("heads_bias", up_hb), ("branch_bias", up_bias), ("norm_gain", up_gain), ("norm_shift", up_shift)):
        o[...] = MOMENTUM * v["momentum_" + name][...] + (1.0 - MOMENTUM) * v[name][...].astype(F32)
    eb = MOMENTUM * v["momentum_expand_bias"][...] + (1.0 - MOMENTUM) * v["expand_bias"][...].astype(F32)
    at = lax.broadcasted_iota(jnp.int32, eb.shape, 0)
    for i in range(fin.FS // 128):
        g_eb[i : i + 1, :] = whole[8:9, i * 128 : i * 128 + 128]
        row = jnp.where(at == t * (fin.FS // 128) + i, eb, 0.0)
        up_eb[i : i + 1, :] = jnp.sum(row, axis=0, keepdims=True)
    for i, (a, b) in enumerate(zip(tiny, tiny_out)):
        c = pltpu.make_async_copy(a, b, osem.at[n + 6 + i])
        c.start()
        waits.append(c)
    homes = [
        [(g_shrink.at[0:PR], 0, PR)], [(g_shrink.at[PR : 2 * PR], 0, PR)], [(g_expand.at[0:PR], 0, PR)],
        [(g_expand.at[PR : 2 * PR], 0, PR)], [(g_in.at[0], 0, HS), (g_in.at[1], HS, 2 * HS)],
        [(g_in.at[2], 0, HS), (g_out, HS, 2 * HS)],
    ]
    k = n
    for p in range(PIECES):
        ins[p].wait()
        wide[p] = low[p].astype(F32)
        for home, a, b in homes[p]:
            c = pltpu.make_async_copy(wide.at[p, a:b], home, osem.at[k])
            c.start()
            waits.append(c)
            k += 1
    for c in waits:
        c.wait()


def cfg_limit():
    return 64 * 1024 * 1024 - 4096


def solution(mesh):
    both = ("dp", "tensor")
    in_specs = (
        P(both, None), P(both, None), P("dp"), P("dp"), P(), P(both, None), P(both, None), P(None, None, "tensor"),
        P(None, "tensor"), P("tensor", None), P(None, "tensor"), P(), P("tensor", None), P(), P(), P(),
        P(None, "dp", "tensor"), P(None, "tensor"), P("tensor", "dp"), P("dp", "tensor"), P(), P("tensor", "dp"), P(), P(), P(),
    )
    out_specs = (
        P(both, None), P(both, None), P(), P(both, None), P(None, None, "tensor"), P(None, "tensor"), P("tensor", None),
        P(None, "tensor"), P("tensor"), P("tensor", None), P(), P(), P(), P(None, "dp", "tensor"), P(None, "tensor"),
        P("tensor", "dp"), P("dp", "tensor"), P("tensor"), P("tensor", "dp"), P(), P(), P(),
    )
    shape = dict(mesh.shape)
    return jax.shard_map(lambda *a: local(shape, *a), mesh=mesh, in_specs=in_specs, out_specs=out_specs, check_vma=False)
```

```python
import types

import jax
import jax.numpy as jnp
from jax import lax
from jax.experimental import pallas as pl
from jax.experimental.pallas import tpu as pltpu
from jax.sharding import PartitionSpec as P

HEAD = 64
SOFTMAX_DIVISOR = 0.05
MOMENTUM = 0.5
NORM_EPSILON = 1e-12
MASKED_SCORE = -1e30
ROOT_HALF = 0.7071067811865476
GAUSS_SCALE = 0.3989422804014327
MESH = pl.DeviceIdType.MESH
F32, BF16 = jnp.float32, jnp.bfloat16
NN = (((1,), (0,)), ((), ()))
NT = (((1,), (1,)), ((), ()))
TN = (((0,), (0,)), ((), ()))
TENSOR = 4
PIECES = 6


TAIL = (
    (1, 3), (4, 0), (0, 4), (3, 2), (5, 0), (2, 3), (4, 1), (1, 4), (0, 5), (5, 1), (4, 2), (3, 3), (1, 5), (2, 4), (5, 2), (4, 3),
    (3, 4), (2, 5), (5, 3), (4, 4), (3, 5), (5, 4), (4, 5), (5, 5),
)


def dot(a, b, dims=NN):
    return lax.dot_general(a, b, dims, preferred_element_type=F32)


def norm_rows(v, gain, shift):
    c = v - jnp.mean(v, axis=-1, keepdims=True)
    inverse = lax.rsqrt(jnp.mean(c * c, axis=-1, keepdims=True) + NORM_EPSILON)
    n = c * inverse
    return n * gain + shift, n, inverse


def norm_back(up, n, inverse, gain):
    e = up * gain
    inner = e - jnp.mean(e, axis=-1, keepdims=True) - n * jnp.mean(e * n, axis=-1, keepdims=True)
    return inner * inverse


def gelu_parts(z):
    a = jnp.abs(z) * ROOT_HALF
    g = jnp.exp(-0.5 * z * z)
    s = 1.0 / (1.0 + 0.3275911 * a)
    poly = ((((1.061405429 * s - 1.453152027) * s + 1.421413741) * s - 0.284496736) * s + 0.254829592) * s
    q = 0.5 * poly * g
    cdf = jnp.where(z >= 0, 1.0 - q, q)
    return z * cdf, cdf + z * GAUSS_SCALE * g


def pack(q, k, v, o):
    lo, hi = slice(0, 128), slice(128, 192)
    pair = lambda a, b: jnp.concatenate([a[:, hi], b[:, hi]], axis=1)
    tiles = [q[:, lo], pair(q, v), k[:, lo], v[:, lo], pair(k, o), o[:, lo]]
    return jnp.concatenate([a.astype(BF16) for a in tiles], axis=1)


def kernel(cfg, *refs):
    r = types.SimpleNamespace(**dict(zip(cfg.names, refs)))
    D, HS, FS, L, DP, RC = cfg.D, cfg.HS, cfg.FS, cfg.L, cfg.DP, cfg.RC
    N, SH, NZ = DP * TENSOR, cfg.SH, DP // 2
    NCH = L // RC
    dp, t = lax.axis_index("dp"), lax.axis_index("tensor")
    px = lax.rem(t + 2, TENSOR)
    sib = t + 1 - 2 * lax.rem(t, 2)
    y, z = lax.rem(dp, 2), dp // 2
    me = dp * TENSOR + t
    d_x, d_sib, d_y = (dp, px), (dp, sib), (dp + 1 - 2 * y, t)

    def d_z(k):
        return (lax.rem(z + k, NZ) * 2 + y, t)

    def from_z(k):
        return lax.rem(z - k + NZ, NZ)

    def remote(src, dst, sems, i, dev):
        return pltpu.make_async_remote_copy(
            src_ref=src, dst_ref=dst, send_sem=sems[0].at[i], recv_sem=sems[1].at[i], device_id=dev, device_id_type=MESH
        )

    sends = []

    def send(src, dst, sems, i, dev):
        c = remote(src, dst, sems, i, dev)
        c.start()
        sends.append(c)
        return c

    last = []

    class Spread:
        def __init__(self, block, sems, base):
            self.block, self.sems, self.base = block, sems, base

        def copy(self, i, owner_z, dev):
            b = self.block(y, owner_z)
            return remote(b, b, self.sems, self.base + i, dev)

        def right(self, k):
            return self.copy(k - 1, z - k + 1, (dp + 2, t))

        def left(self, k):
            return self.copy(NZ - 1 + k - 1, z + k - 1, (dp - 2, t))

        def over(self, owner_z):
            return self.copy(2 * (NZ - 1) + owner_z, owner_z, d_y)

        def start(self):
            pl.when(z < NZ - 1)(lambda: self.right(1).start())
            pl.when(z > 0)(lambda: self.left(1).start())
            self.over(z).start()
            last.append(self.sent)

        def step(self, k):
            @pl.when(z >= k)
            def _():
                self.copy(k - 1, z - k, d_y).wait_recv()
                if k < NZ - 1:
                    pl.when(z < NZ - 1)(lambda: self.right(k + 1).start())
                self.over(z - k).start()

            @pl.when(z + k <= NZ - 1)
            def _():
                self.copy(NZ - 1 + k - 1, z + k, d_y).wait_recv()
                if k < NZ - 1:
                    pl.when(z > 0)(lambda: self.left(k + 1).start())
                self.over(z + k).start()

        def finish(self):
            for o in range(NZ):
                b = self.block(1 - y, o)
                remote(b, b, self.sems, self.base + 2 * (NZ - 1) + o, d_y).wait_recv()

        def sent(self):
            for k in range(1, NZ):
                pl.when(jnp.logical_and(z >= k - 1, z < NZ - 1))(lambda: self.copy(k - 1, z, d_y).wait_send())
                pl.when(jnp.logical_and(z + k - 1 <= NZ - 1, z > 0))(lambda: self.copy(NZ - 1 + k - 1, z, d_y).wait_send())
            for o in range(NZ):
                self.copy(2 * (NZ - 1) + o, z, d_y).wait_send()

    loads = {}

    def load(name, src, dst):
        c = pltpu.make_async_copy(src, dst, r.lsem.at[len(loads)])
        c.start()
        loads[name] = c

    stores = []

    def store(src, dst):
        c = pltpu.make_async_copy(src, dst, r.ssem.at[len(stores)])
        c.start()
        stores.append(c)

    xs, cs = (r.xs, r.xr), (r.cs, r.cr)

    load("q", r.query_tokens, r.X.at[0, 0])
    load("hi", r.heads_in, r.wqi.at[:, 0])
    load("wo", r.heads_out, r.wo.at[0])
    small_in = cfg.small
    for name in small_in:
        load(name, getattr(r, name), getattr(r, "v_" + name))
    if cfg.gather:
        load("mhi", r.momentum_heads_in, r.mhi)
        load("mo", r.momentum_heads_out, r.mho)
    load("we", r.expand_weight, r.we.at[0])
    load("ws", r.shrink_weight, r.ws.at[0])
    if cfg.gather:
        load("me", r.momentum_expand_weight, r.mex)
        load("ms", r.momentum_shrink_weight, r.msh)
    else:
        load("kw", r.key_weights, r.wk.at[0])
    load("k", r.key_tokens, r.X.at[1, 0])
    load("queue", r.key_queue, r.queue)
    load("cot", r.token_cotangent, r.cot)

    bar = pltpu.get_barrier_semaphore()

    def greet(i, c):
        o = lax.rem(me + i, N)
        pl.semaphore_signal(bar, inc=1, device_id=(o // TENSOR, lax.rem(o, TENSOR)), device_id_type=MESH)
        return c

    lax.fori_loop(1, N, greet, 0)
    pl.semaphore_wait(bar, N - 1)

    c_xq = send(r.query_tokens, r.X.at[0, 1], xs, 0, d_x)
    c_xk = send(r.key_tokens, r.X.at[1, 1], xs, 1, d_x)
    c_hi = send(r.heads_in, r.wqi.at[:, 1], cs, 0, d_sib)
    c_wo = send(r.heads_out, r.wo.at[1], cs, 1, d_sib)

    def small_blend(name):
        return MOMENTUM * getattr(r, "v_momentum_" + name)[...] + (1.0 - MOMENTUM) * getattr(r, "v_" + name)[...].astype(F32)

    for name in small_in:
        loads[name].wait()
    r.hb[0, 0:2, :] = r.v_heads_bias[...].astype(F32)
    r.hb[0, 2:4, :] = small_blend("heads_bias")
    c_hb = send(r.hb.at[0], r.hb.at[1], cs, 4, d_sib)
    bb = (r.v_branch_bias[...].astype(F32), small_blend("branch_bias"))
    gain = (r.v_norm_gain[...].astype(F32), small_blend("norm_gain"))
    shift = (r.v_norm_shift[...].astype(F32), small_blend("norm_shift"))
    for w, b in enumerate((r.v_expand_bias[...].astype(F32), small_blend("expand_bias"))):
        for k in range(TENSOR):
            for i in range(FS // 128):
                at = k * (FS // 128) + i
                r.eb[w, k : k + 1, i * 128 : i * 128 + 128] = b[at : at + 1, :]

    gs = (r.gs, r.gr)
    spread_n = 2 * (NZ - 1) + NZ

    def g_block(part):
        return lambda yy, zz: r.wk.at[0, part, pl.ds(pl.multiple_of((zz * 2 + yy) * SH, SH), SH), :]

    g_of = [Spread(g_block(part), gs, part * spread_n) for part in range(3)]

    g_done = {}

    def g_sib(part):
        g_done[part] = send(r.wk.at[0, part], r.wk.at[1, part], gs, 3 * spread_n + part, d_sib)

    def g_step(part, k):
        if cfg.gather:
            if k < NZ:
                g_of[part].step(k)
            else:
                g_of[part].finish()
                g_sib(part)

    if cfg.gather:
        own = pl.ds(pl.multiple_of(dp * SH, SH), SH)
        pick = (
            lax.broadcasted_iota(jnp.int32, (SH, D), 1) == lax.broadcasted_iota(jnp.int32, (SH, D), 0) + dp * SH
        ).astype(F32).astype(BF16)
        eye = (
            lax.broadcasted_iota(jnp.int32, (D, D), 0) == lax.broadcasted_iota(jnp.int32, (D, D), 1)
        ).astype(F32).astype(BF16)
        for name in ("hi", "mhi", "wo", "mo"):
            loads[name].wait()
        blocks = [
            MOMENTUM * r.mhi[i] + (1.0 - MOMENTUM) * dot(pick, r.wqi[i, 0], NT) for i in range(3)
        ]
        for i in range(3):
            r.mhi[i] = blocks[i]
        u = MOMENTUM * r.mho[...] + (1.0 - MOMENTUM) * dot(r.wo[0], pick, NT)
        r.mho[...] = u
        blocks.append(dot(eye[:SH, :SH], u.astype(BF16), NT))
        r.wk[0, 0, own, :] = pack(*blocks)
        g_of[0].start()
        for name in ("we", "me", "ws", "ms"):
            loads[name].wait()
        u = MOMENTUM * r.mex[...] + (1.0 - MOMENTUM) * r.we[0, own, :].astype(F32)
        r.mex[...] = u
        r.wk[0, 1, own, :] = u.astype(BF16)
        g_of[1].start()
        u = MOMENTUM * r.msh[...] + (1.0 - MOMENTUM) * dot(pick, r.ws[0], NT)
        r.msh[...] = u
        r.wk[0, 2, own, :] = u.astype(BF16)
        g_of[2].start()
        store(r.mhi, r.o_heads_in)
        store(r.mho, r.o_heads_out)
        store(r.mex, r.o_expand)
        store(r.msh, r.o_shrink)
    else:
        for name in ("hi", "wo", "we", "ws", "kw"):
            loads[name].wait()
        for part in range(3):
            g_sib(part)
    c_we = send(r.expand_weight, r.we.at[1], cs, 2, d_sib)
    c_ws = send(r.shrink_weight, r.ws.at[1], cs, 3, d_sib)

    lengths = ((r.query_lengths[t], r.query_lengths[px]), (r.key_lengths[t], r.key_lengths[px]))
    low_half = lax.broadcasted_iota(jnp.int32, (1, 128), 1) < HEAD
    key_at = lax.broadcasted_iota(jnp.int32, (1, L), 1)

    def split(tile):
        zero = jnp.zeros_like(tile)
        return jnp.where(low_half, tile, zero), jnp.where(low_half, zero, tile)

    def softmax(q, k, valid):
        sc = jnp.where(valid, dot(q, k, NT), MASKED_SCORE)
        top = jnp.max(sc, axis=-1, keepdims=True)
        e = jnp.exp(sc - top)
        tot = jnp.sum(e, axis=-1, keepdims=True)
        return (e * (1.0 / tot)).astype(BF16), top + jnp.log(tot)

    def scaled(v):
        return (v.astype(BF16).astype(F32) * HEAD**-0.5).astype(BF16)

    hpair = 2 * HS // 128

    def attend_query(crop, out):
        x = r.X[0, crop]
        valid = key_at < lengths[0][crop]
        q = scaled(dot(x, r.wqi[0].reshape(2 * HS, D), NT) + bias_q)
        k = dot(x, r.wqi[1].reshape(2 * HS, D), NT).astype(BF16)
        v = (dot(x, r.wqi[2].reshape(2 * HS, D), NT) + bias_v).astype(BF16)
        r.qkv[0, crop], r.qkv[1, crop], r.qkv[2, crop] = q, k, v
        at = lax.broadcasted_iota(jnp.int32, (L, 128), 1)
        logs = jnp.zeros((L, 128), F32)
        ctx = []
        for i in range(hpair):
            tile = slice(128 * i, 128 * i + 128)
            ks, vs = split(k[:, tile]), split(v[:, tile])
            c = None
            for h in range(2):
                p, g = softmax(q[:, tile], ks[h], valid)
                logs = jnp.where(at == 2 * i + h, g, logs)
                d = dot(p, vs[h])
                c = d if c is None else c + d
            ctx.append(c.astype(BF16))
        r.G[crop] = logs
        ctx = jnp.concatenate(ctx, axis=1)
        r.C[crop] = ctx
        out[...] = dot(ctx, r.wo[...].reshape(2 * HS, D))

    def attend_key(crop, out):
        x = r.X[1, crop]
        valid = key_at < lengths[1][crop]
        total = None
        for s in range(2):
            w = r.wk[s, 0]
            hb = r.hb[s]
            qb, vb, none = hb[2:3, :], hb[3:4, :], jnp.zeros((1, 128), F32)
            bias = jnp.concatenate(
                [qb[:, 0:128], jnp.concatenate([qb[:, 128:192], vb[:, 128:192]], axis=1), none, vb[:, 0:128], none], axis=1
            )
            pr = dot(x, w[:, 0:640]) + bias
            q01, m = pr[:, 0:128], pr[:, 128:256].astype(BF16)
            q01, q2 = scaled(q01), (m.astype(F32) * HEAD**-0.5).astype(BF16)
            k01, v01, k2 = (pr[:, 128 * i : 128 * i + 128].astype(BF16) for i in (2, 3, 4))
            ks, vs = split(k01), split(v01)
            p0, _ = softmax(q01, ks[0], valid)
            p1, _ = softmax(q01, ks[1], valid)
            p2, _ = softmax(q2, split(k2)[0], valid)
            c01 = (dot(p0, vs[0]) + dot(p1, vs[1])).astype(BF16)
            c2 = dot(p2, split(m)[1]).astype(BF16)
            a = dot(jnp.concatenate([c2, c01], axis=1), w[:, 512:768], NT)
            total = a if total is None else total + a
        out[...] = total

    def attend(w, crop, out):
        (attend_query, attend_key)[w](crop, out)

    def swap(src32, sbuf, rbuf, base):
        out = []
        for j in range(NCH):
            rows = pl.ds(j * RC, RC)
            sbuf[rows, :] = src32[rows, :].astype(BF16)
            out.append(send(sbuf.at[rows], rbuf.at[rows], xs, base + j, d_x))
        return out

    FT = 256

    def feed(w, crop, row0, rows_n, out):
        rows = pl.ds(row0, rows_n)
        u = r.U[w, crop, rows, :]

        total = None
        for i in range(2 * (FS // FT)):
            s, j = i // (FS // FT), i % (FS // FT)
            cols = slice(j * FT, j * FT + FT)
            b = r.eb[w, pl.ds(t if s == 0 else sib, 1), cols]
            if w == 0:
                zz = dot(u, r.we[s, :, cols]) + b
            else:
                zz = dot(u, r.wk[s, 1, :, cols]) + b
            h, slope = gelu_parts(zz)
            h = h.astype(BF16)
            if w == 0:
                r.H[s, crop, rows, cols] = h
                r.slope[s, crop, rows, cols] = slope.astype(BF16)
                f = dot(h, r.ws[s, cols, :])
            else:
                f = dot(h, r.wk[s, 2, :, cols], NT)

            total = f if total is None else total + f
        out[rows, :] = total

    x_of = {}

    def first_norm(w, base):
        out = []
        for j in range(NCH):
            rows = pl.ds(j * RC, RC)
            x_of["A", w][j].wait_recv()
            m = r.X[w, 0, rows, :].astype(F32) + (r.own[w, rows, :] + r.arecv[w, rows, :].astype(F32)) + bb[w][0:1, :]
            u, n, inv = norm_rows(m, gain[w][0:1, :], shift[w][0:1, :])
            r.Uf[w, rows, :] = u
            r.U[w, 0, rows, :] = u.astype(BF16)
            if w == 0:
                r.N1[rows, :] = n
                r.i1[rows, :] = jnp.broadcast_to(inv, (RC, 128))
            out.append(send(r.U.at[w, 0, rows], r.U.at[w, 1, rows], xs, base + j, d_x))
        x_of["U", w] = out

    def second_norm(w, o_ref, o_hbm):
        pooled = jnp.zeros((1, D), F32)
        length = lengths[w][0]
        for j in range(NCH):
            rows = pl.ds(j * RC, RC)
            x_of["F", w][j].wait_recv()
            m = r.Uf[w, rows, :] + (r.own[w, rows, :] + r.frecv[w, rows, :].astype(F32)) + bb[w][1:2, :]
            out, n, inv = norm_rows(m, gain[w][1:2, :], shift[w][1:2, :])
            o_ref[rows, :] = out.astype(BF16)
            if w == 0:
                r.N2[rows, :] = n
                r.i2[rows, :] = jnp.broadcast_to(inv, (RC, 128))
            valid = lax.broadcasted_iota(jnp.int32, (RC, 1), 0) + j * RC < length
            pooled += jnp.sum(jnp.where(valid, out, 0.0), axis=0, keepdims=True)
        store(o_ref, o_hbm)
        pooled = pooled / length.astype(F32)
        inverse = lax.rsqrt(jnp.sum(pooled * pooled, axis=-1, keepdims=True) + 1e-06)
        unit = (pooled * inverse).astype(BF16).astype(F32)
        return pooled, inverse, unit

    KL = D // 128

    def tile_of(row):
        return jnp.concatenate([row[:, i * 128 : (i + 1) * 128] for i in range(KL)], axis=0)

    def to_all(sbuf_of, rbuf, sems, base):
        def go(i, c):
            o = lax.rem(me + i, N)
            remote(sbuf_of(o), rbuf.at[me], sems, base, (o // TENSOR, lax.rem(o, TENSOR))).start()
            return c

        lax.fori_loop(1, N, go, 0)

    def from_all(rbuf, sems, base):
        tiles = rbuf.at[pl.ds(0, N - 1)]
        remote(tiles, tiles, sems, base, d_x).wait_recv()

    def sent_all(sems, base):
        tiles = r.nrecv.at[pl.ds(0, N - 1)]
        remote(tiles, tiles, sems, base, d_x).wait_send()

    us = (r.us, r.ur)

    loads["q"].wait()
    c_hi.wait_recv()
    c_wo.wait_recv()
    c_hb.wait_recv()
    bias_q = jnp.concatenate([r.hb[0, 0:1, :], r.hb[1, 0:1, :]], axis=1)
    bias_v = jnp.concatenate([r.hb[0, 1:2, :], r.hb[1, 1:2, :]], axis=1)
    attend(0, 0, r.own.at[0])
    g_step(0, 1)
    c_xq.wait_recv()
    attend(0, 1, r.part)
    x_of["A", 0] = swap(r.part, r.asend.at[0], r.arecv.at[0], 2)
    g_step(0, 2)
    g_step(1, 1)
    g_step(2, 1)
    g_step(0, 3)
    c_we.wait_recv()
    c_ws.wait_recv()
    first_norm(0, 2 + NCH)
    g_step(1, 2)
    feed(0, 0, 0, L, r.own.at[0])
    g_step(2, 2)
    g_step(0, NZ)
    g_step(1, 3)
    kb = 2 + 3 * NCH
    c_xk.wait_recv()
    loads["k"].wait()
    g_done[0].wait_recv()
    attend(1, 1, r.part)
    x_of["A", 1] = swap(r.part, r.asend.at[1], r.arecv.at[1], kb)
    attend(1, 0, r.own.at[1])

    def feed_partner(w, base):
        x_of["F", w] = []
        for j in range(NCH):
            x_of["U", w][j].wait_recv()
            feed(w, 1, j * RC, RC, r.part)
            rows = pl.ds(j * RC, RC)
            r.fsend[w, rows, :] = r.part[rows, :].astype(BF16)
            x_of["F", w].append(send(r.fsend.at[w, rows], r.frecv.at[w, rows], xs, base + j, d_x))

    feed_partner(0, 2 + 2 * NCH)
    g_step(2, 3)
    g_step(1, NZ)
    first_norm(1, kb + NCH)
    q_pooled, q_inverse, q_unit = second_norm(0, r.oq, r.query_output)
    r.usend[0, 0:KL, :] = tile_of(q_unit)
    r.units[0, me, 0:KL, :] = tile_of(q_unit)
    to_all(lambda o: r.usend.at[0], r.units.at[0], us, 0)
    g_step(2, NZ)
    g_done[1].wait_recv()
    g_done[2].wait_recv()
    feed(1, 0, 0, L, r.own.at[1])
    feed_partner(1, kb + 2 * NCH)
    loads["queue"].wait()
    from_all(r.units.at[0], us, 0)
    all_q = jnp.concatenate([r.units[0, :, i, :] for i in range(KL)], axis=1).astype(BF16)
    logits = dot(all_q, r.queue[...], NT) / SOFTMAX_DIVISOR
    top = jnp.max(logits, axis=-1, keepdims=True)
    e = jnp.exp(logits - top)
    tot = jnp.sum(e, axis=-1, keepdims=True)
    grad = dot(e.astype(BF16), r.queue[...])
    for i in range(KL):
        r.nsend[:, i, :] = grad[:, i * 128 : (i + 1) * 128]
    r.nsend[:, KL, :] = jnp.broadcast_to(top, (N, 128))
    r.nsend[:, KL + 1, :] = jnp.broadcast_to(tot, (N, 128))
    r.nrecv[me] = r.nsend[me]
    to_all(lambda o: r.nsend.at[o], r.nrecv, us, 1)
    k_pooled, k_inverse, k_unit = second_norm(1, r.ok, r.key_output)
    r.usend[1, 0:KL, :] = tile_of(k_unit)
    r.units[1, me, 0:KL, :] = tile_of(k_unit)
    to_all(lambda o: r.usend.at[1], r.units.at[1], us, 2)
    from_all(r.nrecv, us, 1)
    from_all(r.units.at[1], us, 2)

    pos = r.positives[me]
    hit = lax.broadcasted_iota(jnp.int32, (N, 1, 1), 0) == pos
    partner = jnp.sum(jnp.where(hit, r.units[1][:, 0:KL, :], 0.0), axis=0)
    mine = r.usend[0, 0:KL, :]
    match = jnp.sum(jnp.sum(mine * partner, axis=1, keepdims=True), axis=0, keepdims=True) / SOFTMAX_DIVISOR
    tops, tots = r.nrecv[:, KL, :], r.nrecv[:, KL + 1, :]
    peak = jnp.maximum(jnp.max(jnp.max(tops, axis=0, keepdims=True), axis=1, keepdims=True), match)
    total = jnp.sum(tots * jnp.exp(tops - peak), axis=0, keepdims=True)[:, 0:1]
    level = peak + jnp.log(total + jnp.exp(match - peak))
    loss = level - match
    scale = jnp.exp(r.nrecv[:, KL : KL + 1, :] - level.reshape(1, 1, 1)) * (1.0 / SOFTMAX_DIVISOR)
    du = jnp.sum(r.nrecv[:, 0:KL, :] * scale, axis=0) + (jnp.exp(match - level) - 1.0) / SOFTMAX_DIVISOR * partner
    du = jnp.concatenate([du[i : i + 1, :] for i in range(KL)], axis=1)
    along = jnp.sum(q_pooled * du, axis=-1, keepdims=True)
    d_pooled = q_inverse * du - q_pooled * (q_inverse * q_inverse * q_inverse) * along
    per_token = d_pooled / lengths[0][0].astype(F32)

    loads["cot"].wait()
    bbase = kb + 3 * NCH
    small = [jnp.zeros((1, D), F32) for _ in range(6)]
    x_of["dF"] = []
    for j in range(NCH):
        rows = pl.ds(j * RC, RC)
        valid = lax.broadcasted_iota(jnp.int32, (RC, 1), 0) + j * RC < lengths[0][0]
        dy = r.cot[rows, :].astype(F32) + jnp.where(valid, per_token, 0.0)
        n2 = r.N2[rows, :]
        d2 = norm_back(dy, n2, r.i2[rows, 0:1], gain[0][1:2, :])
        r.d2[rows, :] = d2
        r.dF[0, rows, :] = d2.astype(BF16)
        x_of["dF"].append(send(r.dF.at[0, rows], r.dF.at[1, rows], xs, bbase + j, d_x))
        small[1] += jnp.sum(d2, axis=0, keepdims=True)
        small[3] += jnp.sum(dy * n2, axis=0, keepdims=True)
        small[5] += jnp.sum(dy, axis=0, keepdims=True)

    def feed_back(crop, row0, rows_n, out):
        rows = pl.ds(row0, rows_n)
        df = r.dF[crop, rows, :]

        total = None
        for i in range(2 * (FS // FT)):
            s, j = i // (FS // FT), i % (FS // FT)
            cols = slice(j * FT, j * FT + FT)
            dh = dot(df, r.ws[s, cols, :], NT)
            dz = (dh * r.slope[s, crop, rows, cols].astype(F32)).astype(BF16)
            r.dZ[s, crop, rows, cols] = dz
            du_ = dot(dz, r.we[s, :, cols], NT)

            total = du_ if total is None else total + du_
        out[rows, :] = total

    feed_back(0, 0, L, r.own.at[0])
    PR = 3 * 2 * D // (2 * 3) // 2
    HF, CH = PR // 2, PR // 2 // max(NZ, 1)
    ws_sem = (r.ws_s, r.ws_r)
    per = 2 + NZ - 1 + 2 * (NZ - 1) + NZ

    def piece_part(p, s):
        if p < 2:
            h = r.H[s].reshape(2 * L, FS)[:, p * PR : (p + 1) * PR]
            return dot(h, r.dF[...].reshape(2 * L, D), TN)
        u = r.U[0].reshape(2 * L, D)[:, (p - 2) * PR : (p - 1) * PR]
        return dot(u, r.dZ[s].reshape(2 * L, FS), TN)

    w_of = {}

    def w_sib_send(p):
        w_of["s", p] = send(r.wsend.at[p], r.wrecv.at[p], ws_sem, p * per, d_sib)

    def w_sib(p):
        if p < 4:
            r.wsend[p] = piece_part(p, 1).astype(BF16)
        else:
            for q in range(2):
                i = (p - 4) * 2 + q
                a = r.dqkv[i].reshape(2 * L, 2 * HS) if i < 3 else r.C[...].reshape(2 * L, 2 * HS)
                b = r.X[0].reshape(2 * L, D) if i < 3 else r.dA[...].reshape(2 * L, D)
                v = dot(a, b, TN)
                rows = slice(q * HS, (q + 1) * HS)
                r.hacc[p - 4, rows, :] = v[0:HS, :]
                r.wsend[p, rows, :] = v[HS:, :].astype(BF16)
        w_sib_send(p)

    def half(h):
        return pl.ds(pl.multiple_of(h * HF, HF), HF)

    def w_own(p):
        v = piece_part(p, 0) if p < 4 else r.hacc[p - 4]
        w_of["s", p].wait_recv()
        v = v + r.wrecv[p].astype(F32)
        if cfg.gather:
            r.wacc[p] = v.astype(BF16)
        else:
            r.wacc32[p] = v
        if cfg.gather:
            w_of["y", p] = send(r.wacc.at[p, half(1 - y)], r.wyr.at[p], ws_sem, p * per + 1, d_y)
        else:
            store(r.wacc32.at[p], r.grads.at[p])

    def chunk(zz):
        return pl.ds(pl.multiple_of(zz * CH, CH), CH)

    def place(yy, zz):
        return pl.ds(pl.multiple_of(yy * HF + zz * CH, CH), CH)

    def w_y(p):
        w_of["y", p].wait_recv()
        r.wys[p] = (r.wacc[p, half(y), :].astype(F32) + r.wyr[p].astype(F32)).astype(BF16)
        for k in range(1, NZ):
            to = lax.rem(z + k, NZ)
            w_of["z", p, k] = send(r.wys.at[p, chunk(to)], r.wzr.at[p, k - 1], ws_sem, p * per + 1 + k, d_z(k))

    def w_z(p):
        v = r.wys[p, chunk(z), :].astype(F32)
        for k in range(1, NZ):
            w_of["z", p, k].wait_recv()
            v += r.wzr[p, k - 1].astype(F32)
        r.wout[p, place(y, z), :] = v.astype(BF16)
        w_of["b", p] = Spread(lambda yy, zz: r.wout.at[p, place(yy, zz)], ws_sem, p * per + 2 + NZ - 1)
        w_of["b", p].start()

    def w_step(p, k):
        if not cfg.gather:
            return
        if k < 2:
            (w_y, w_z)[k](p)
        elif k < 1 + NZ:
            w_of["b", p].step(k - 1)
        else:
            w_of["b", p].finish()
            store(r.wout.at[p], r.grads.at[p])

    for j in range(NCH):
        x_of["dF"][j].wait_recv()
    w_sib(0)
    x_of["dU"] = []
    for j in range(NCH):
        feed_back(1, j * RC, RC, r.part)
        rows = pl.ds(j * RC, RC)
        r.dusend[rows, :] = r.part[rows, :].astype(BF16)
        x_of["dU"].append(send(r.dusend.at[rows], r.durecv.at[rows], xs, bbase + NCH + j, d_x))
        if j == 0:
            w_own(0)
    w_sib(1)
    w_sib(2)
    w_own(1)
    w_sib(3)
    w_own(2)
    w_own(3)
    x_of["dA"] = []
    for j in range(NCH):
        rows = pl.ds(j * RC, RC)
        x_of["dU"][j].wait_recv()
        du1 = r.d2[rows, :] + (r.own[0, rows, :] + r.durecv[rows, :].astype(F32))
        n1 = r.N1[rows, :]
        dm = norm_back(du1, n1, r.i1[rows, 0:1], gain[0][0:1, :])
        r.Uf[0, rows, :] = dm
        r.dA[0, rows, :] = dm.astype(BF16)
        x_of["dA"].append(send(r.dA.at[0, rows], r.dA.at[1, rows], xs, bbase + 2 * NCH + j, d_x))
        small[0] += jnp.sum(dm, axis=0, keepdims=True)
        small[2] += jnp.sum(du1 * n1, axis=0, keepdims=True)
        small[4] += jnp.sum(du1, axis=0, keepdims=True)
    for i in range(6):
        r.sm[0, i : i + 1, :] = small[i]
    r.sm[0, 6:7, :] = jnp.broadcast_to(loss, (1, D))
    w_step(0, 0)

    def attend_back(crop, out):
        valid = key_at < lengths[0][crop]
        dc = dot(r.dA[crop], r.wo[...].reshape(2 * HS, D), NT).astype(BF16)
        q, k, v, g = r.qkv[0, crop], r.qkv[1, crop], r.qkv[2, crop], r.G[crop]
        grads = ([], [], [])
        for i in range(hpair):
            tile = slice(128 * i, 128 * i + 128)
            qt, dct = q[:, tile], dc[:, tile]
            qs, ks, vs, dcs = split(qt), split(k[:, tile]), split(v[:, tile]), split(dct)
            acc = None
            for h in range(2):
                sc = jnp.where(valid, dot(qt, ks[h], NT), MASKED_SCORE)
                pw = jnp.exp(sc - g[:, 2 * i + h : 2 * i + h + 1])
                dpw = dot(dct, vs[h], NT)
                inner = jnp.sum(dpw * pw, axis=-1, keepdims=True)
                ds = (pw * (dpw - inner)).astype(BF16)
                new = (dot(ds, ks[h]), dot(ds, qs[h], TN), dot(pw.astype(BF16), dcs[h], TN))
                acc = new if acc is None else tuple(a + b for a, b in zip(acc, new))
            for m, (into, a) in enumerate(zip(grads, acc)):
                into.append((a * HEAD**-0.5 if m == 0 else a).astype(BF16))
        total = None
        for m in range(3):
            d = jnp.concatenate(grads[m], axis=1)
            r.dqkv[m, crop] = d
            a = dot(d, r.wqi[m].reshape(2 * HS, D))
            total = a if total is None else total + a
        out[...] = total

    attend_back(0, r.own.at[1])
    w_step(1, 0)
    w_step(0, 1)
    w_step(2, 0)
    for j in range(NCH):
        x_of["dA"][j].wait_recv()
    w_step(1, 1)
    attend_back(1, r.part)
    x_of["dX"] = swap(r.part, r.dxsend, r.dxrecv, bbase + 3 * NCH)
    w_step(0, 2)
    w_sib(4)
    w_step(3, 0)
    w_sib(5)
    w_step(2, 1)
    w_own(4)
    w_step(1, 2)
    w_own(5)
    w_step(0, 3)
    bq = jnp.sum(r.dqkv[0].reshape(2 * L, 2 * HS).astype(F32), axis=0, keepdims=True)
    bv = jnp.sum(r.dqkv[2].reshape(2 * L, 2 * HS).astype(F32), axis=0, keepdims=True)
    for s in range(2):
        eb = jnp.sum(r.dZ[s].reshape(2 * L, FS).astype(F32), axis=0, keepdims=True)
        dst = (r.sm.at[0], r.smx)[s]
        dst[8:9, 0:FS] = eb
        dst[9:10, 0:HS] = bq[:, s * HS : (s + 1) * HS]
        dst[10:11, 0:HS] = bv[:, s * HS : (s + 1) * HS]
    r.smx[0:8, :] = r.sm[0, 0:8, :]
    bs = (r.bs, r.br)
    send(r.smx, r.smr.at[0], bs, 0, d_sib).wait_recv()
    r.sm[1] = r.sm[0] + r.smr[0]
    b_x = send(r.sm.at[1, 0:8], r.smr.at[1, 0:8], bs, 1, d_x)
    w_step(3, 1)
    w_step(2, 2)
    b_x.wait_recv()
    r.sm[2] = r.sm[1]
    r.sm[2, 0:8, :] = r.sm[1, 0:8, :] + r.smr[1, 0:8, :]
    nb = DP.bit_length() - 1 if cfg.gather else 0

    def butterfly(k):
        other = dp + (1 - 2 * lax.rem(dp // (1 << k), 2)) * (1 << k)
        return send(r.sm.at[2 + k], r.smr.at[2 + k], bs, 2 + k, (other, t))

    def add_up(k, c):
        c.wait_recv()
        r.sm[3 + k] = r.sm[2 + k] + r.smr[2 + k]

    b_k = butterfly(0) if nb else None
    for j in range(NCH):
        rows = pl.ds(j * RC, RC)
        x_of["dX"][j].wait_recv()
        r.Uf[1, rows, :] = r.Uf[0, rows, :] + (r.own[1, rows, :] + r.dxrecv[rows, :].astype(F32))
    store(r.Uf.at[1], r.input_gradient)
    for n, (p, k) in enumerate(TAIL):
        w_step(p, k)
        if nb and n % 4 == 0 and n // 4 < nb:
            add_up(n // 4, b_k)
            b_k = butterfly(n // 4 + 1) if n // 4 + 1 < nb else None
    store(r.sm.at[2 + nb], r.vectors)

    for c in sends:
        c.wait_send()
    for i in range(3):
        sent_all(us, i)
    for f in last:
        f()
    for c in stores:
        c.wait()


def blend(old, new):
    return MOMENTUM * old + (1.0 - MOMENTUM) * new.astype(F32)


def local(mesh_shape, query_tokens, key_tokens, query_lengths, key_lengths, positives, key_queue, token_cotangent, heads_in,
          heads_bias, heads_out, expand_weight, expand_bias, shrink_weight, branch_bias, norm_gain, norm_shift,
          momentum_heads_in, momentum_heads_bias, momentum_heads_out, momentum_expand_weight, momentum_expand_bias,
          momentum_shrink_weight, momentum_branch_bias, momentum_norm_gain, momentum_norm_shift):
    DP = mesh_shape["dp"]
    L, D = query_tokens.shape
    HS, FS = heads_in.shape[2], expand_weight.shape[1]
    SH = D // DP
    N = DP * TENSOR
    PR = D // 2
    QN = key_queue.shape[0]
    gather = DP > 2 and SH % 16 == 0 and (PR // DP) % 16 == 0
    RC = 128
    NCH = L // RC
    NZ = DP // 2
    t, dp = lax.axis_index("tensor"), lax.axis_index("dp")
    cfg = types.SimpleNamespace(D=D, HS=HS, FS=FS, L=L, DP=DP, SH=SH, RC=RC, gather=gather)

    vm = lambda shape, dtype: pltpu.VMEM(shape, dtype)
    any_, vmem, smem = (pl.BlockSpec(memory_space=m) for m in (pl.ANY, pltpu.VMEM, pltpu.SMEM))
    small = {
        "heads_bias": heads_bias, "expand_bias": expand_bias.reshape(-1, 128), "branch_bias": branch_bias,
        "norm_gain": norm_gain, "norm_shift": norm_shift, "momentum_heads_bias": momentum_heads_bias,
        "momentum_expand_bias": momentum_expand_bias.reshape(-1, 128), "momentum_branch_bias": momentum_branch_bias,
        "momentum_norm_gain": momentum_norm_gain, "momentum_norm_shift": momentum_norm_shift,
    }
    cfg.small = list(small)
    ins = [
        ("query_tokens", query_tokens, any_), ("key_tokens", key_tokens, any_),
        ("query_lengths", query_lengths, smem), ("key_lengths", key_lengths, smem), ("positives", positives, smem),
        ("key_queue", key_queue, any_), ("token_cotangent", token_cotangent, any_),
        ("heads_in", jnp.swapaxes(heads_in, 1, 2), any_), ("heads_out", heads_out, any_),
        ("expand_weight", expand_weight, any_), ("shrink_weight", shrink_weight, any_),
    ] + [(n, a, any_) for n, a in small.items()]
    outs = [
        ("query_output", (L, D), BF16), ("key_output", (L, D), BF16), ("input_gradient", (L, D), F32),
        ("grads", (PIECES, PR, D), BF16 if gather else F32), ("vectors", (16, D), F32),
    ]
    if gather:
        ins += [("momentum_heads_in", momentum_heads_in, any_), ("momentum_heads_out", momentum_heads_out, any_),
                ("momentum_expand_weight", momentum_expand_weight, any_),
                ("momentum_shrink_weight", momentum_shrink_weight.T, any_)]
        outs += [("o_heads_in", momentum_heads_in.shape, F32), ("o_heads_out", momentum_heads_out.shape, F32),
                 ("o_expand", momentum_expand_weight.shape, F32), ("o_shrink", momentum_shrink_weight.shape[::-1], F32)]
    else:
        updated = (
            blend(momentum_heads_in, lax.dynamic_slice_in_dim(heads_in, dp * SH, SH, 1)),
            blend(momentum_heads_out, lax.dynamic_slice_in_dim(heads_out, dp * SH, SH, 1)),
            blend(momentum_expand_weight, lax.dynamic_slice_in_dim(expand_weight, dp * SH, SH, 0)),
            blend(momentum_shrink_weight, lax.dynamic_slice_in_dim(shrink_weight, dp * SH, SH, 1)),
        )
        whole = lambda a, axis: lax.all_gather(a.astype(BF16), "dp", axis=axis, tiled=True)
        heads = jnp.concatenate([whole(updated[0], 1), whole(updated[1].T, 0)[None]], axis=0)
        ins += [("key_weights", jnp.stack([pack(*heads), whole(updated[2], 0), whole(updated[3].T, 0)]), any_)]
    scratch = [
        ("X", vm((2, 2, L, D), BF16)), ("wqi", vm((3, 2, HS, D), BF16)), ("wo", vm((2, HS, D), BF16)),
        ("we", vm((2, D, FS), BF16)), ("ws", vm((2, FS, D), BF16)),
        ("wk", vm((2, 3, D, D), BF16)),
        ("queue", vm((QN, D), BF16)), ("cot", vm((L, D), BF16)),
        ("hb", vm((2, 4, HS), F32)), ("eb", vm((2, TENSOR, FS), F32)),
        ("qkv", vm((3, 2, L, 2 * HS), BF16)), ("G", vm((2, L, 128), F32)), ("C", vm((2, L, 2 * HS), BF16)),
        ("U", vm((2, 2, L, D), BF16)), ("Uf", vm((2, L, D), F32)), ("H", vm((2, 2, L, FS), BF16)),
        ("slope", vm((2, 2, L, FS), BF16)), ("N1", vm((L, D), F32)), ("N2", vm((L, D), F32)),
        ("i1", vm((L, 128), F32)), ("i2", vm((L, 128), F32)), ("own", vm((2, L, D), F32)), ("part", vm((L, D), F32)),
        ("asend", vm((2, L, D), BF16)), ("arecv", vm((2, L, D), BF16)), ("fsend", vm((2, L, D), BF16)),
        ("frecv", vm((2, L, D), BF16)), ("oq", vm((L, D), BF16)), ("ok", vm((L, D), BF16)),
        ("usend", vm((2, 8, 128), F32)), ("units", vm((2, N, 8, 128), F32)), ("nsend", vm((N, 8, 128), F32)),
        ("nrecv", vm((N, 8, 128), F32)), ("d2", vm((L, D), F32)), ("dF", vm((2, L, D), BF16)),
        ("dZ", vm((2, 2, L, FS), BF16)), ("dusend", vm((L, D), BF16)), ("durecv", vm((L, D), BF16)),
        ("dA", vm((2, L, D), BF16)), ("dqkv", vm((3, 2, L, 2 * HS), BF16)), ("hacc", vm((2, PR, D), F32)),
        ("dxsend", vm((L, D), BF16)), ("dxrecv", vm((L, D), BF16)),
        ("wsend", vm((PIECES, PR, D), BF16)), ("wrecv", vm((PIECES, PR, D), BF16)),
        ("sm", vm((3 + DP.bit_length(), 16, D), F32)), ("smx", vm((16, D), F32)),
        ("smr", vm((2 + DP.bit_length(), 16, D), F32)),
    ]
    if gather:
        scratch += [
            ("mhi", vm(momentum_heads_in.shape, F32)), ("mho", vm(momentum_heads_out.shape, F32)),
            ("mex", vm(momentum_expand_weight.shape, F32)), ("msh", vm(momentum_shrink_weight.shape[::-1], F32)),
            ("wacc", vm((PIECES, PR, D), BF16)), ("wyr", vm((PIECES, PR // 2, D), BF16)),
            ("wys", vm((PIECES, PR // 2, D), BF16)), ("wzr", vm((PIECES, NZ - 1, PR // DP, D), BF16)),
            ("wout", vm((PIECES, PR, D), BF16)),
        ]
    else:
        scratch += [("wacc32", vm((PIECES, PR, D), F32))]
    scratch += [("v_" + n, vm(a.shape, a.dtype)) for n, a in small.items()]
    dma = pltpu.SemaphoreType.DMA
    nx = 2 + 6 * NCH + 4 * NCH
    ng = 3 * (2 * (NZ - 1) + NZ) + 3
    nw = PIECES * (2 + 3 * (NZ - 1) + NZ)
    nv = 3
    for pair, count in ((("xs", "xr"), nx), (("cs", "cr"), 5), (("gs", "gr"), ng), (("us", "ur"), nv),
                        (("ws_s", "ws_r"), nw), (("bs", "br"), 2 + DP.bit_length())):
        for name in pair:
            scratch.append((name, dma((count,))))
    scratch += [("lsem", dma((32,))), ("ssem", dma((16,)))]
    cfg.names = [n for n, *_ in ins] + [n for n, *_ in outs] + [n for n, _ in scratch]

    def body(*refs):
        kernel(cfg, *refs)

    res = pl.pallas_call(
        body,
        out_shape=[jax.ShapeDtypeStruct(s, d) for _, s, d in outs],
        in_specs=[s for _, _, s in ins],
        out_specs=[any_] * len(outs),
        scratch_shapes=[s for _, s in scratch],
        compiler_params=pltpu.CompilerParams(collective_id=0, has_side_effects=True, vmem_limit_bytes=cfg_limit()),
        name="step",
    )(*[a for _, a, _ in ins])
    query_out, key_out, d_tokens, grads, vectors = res[:5]
    if gather:
        updates = res[5:]
    else:
        updates = (updated[0], updated[1], updated[2], updated[3].T)
        grads, vectors = lax.psum((grads, vectors), "dp")
    copies = (query_out, key_out, d_tokens) + tuple(updates)
    fin = types.SimpleNamespace(D=D, HS=HS, FS=FS, small=list(small))
    out = [jax.ShapeDtypeStruct(a.shape, a.dtype) for a in copies]
    out += [jax.ShapeDtypeStruct(sh, F32) for sh in ((FS, D), (D, FS), (3, HS, D), (HS, D))]
    tiny = ((1, 1), (2, HS), (FS // 128, 128), (2, D), (2, D), (2, D), (2, HS), (FS // 128, 128), (2, D), (2, D), (2, D))
    out += [jax.ShapeDtypeStruct(sh, F32) for sh in tiny]
    out_dmas = len(copies) + 7 + len(tiny)
    done = pl.pallas_call(
        lambda *a: finish(fin, *a),
        out_shape=out,
        in_specs=[any_] * (len(copies) + 2 + len(small)),
        out_specs=[any_] * len(out),
        scratch_shapes=[vm(a.shape, a.dtype) for a in small.values()] + [vm(sh, F32) for sh in tiny]
        + [vm(a.shape, a.dtype) for a in copies]
        + [vm(vectors.shape, F32), vm((PIECES, PR, D), grads.dtype), vm((PIECES, PR, D), F32), dma((32,)), dma((out_dmas,))],
        compiler_params=pltpu.CompilerParams(vmem_limit_bytes=cfg_limit()),
        name="finish",
    )(*copies, grads, vectors, *small.values())
    (query_out, key_out, d_tokens, up_in, up_out, up_expand, up_shrink, g_shrink, g_expand, g_in, g_out, loss, g_hb, g_eb,
     g_bias, g_gain, g_shift, up_hb, up_eb, up_bias, up_gain, up_shift) = done
    return (
        query_out, key_out, loss[0, 0], d_tokens, jnp.swapaxes(g_in, 1, 2), g_hb, g_out, g_expand, g_eb.reshape(FS), g_shrink,
        g_bias, g_gain, g_shift, up_in, up_hb, up_out, up_expand, up_eb.reshape(FS), up_shrink.T, up_bias, up_gain, up_shift,
    )


def finish(fin, *refs):
    HS = fin.HS
    ns, n, nt = len(fin.small), 7, 11
    src, grads, vectors, small = refs[:n], refs[n], refs[n + 1], refs[n + 2 : n + 2 + ns]
    outs, scratch = refs[n + 2 + ns : n + 2 + ns + n + 4 + nt], refs[n + 2 + ns + n + 4 + nt :]
    v = dict(zip(fin.small, scratch[:ns]))
    tiny, held = scratch[ns : ns + nt], scratch[ns + nt : ns + nt + n]
    vecs, low, wide, isem, osem = scratch[ns + nt + n :]
    dst, (g_shrink, g_expand, g_in, g_out), tiny_out = outs[:n], outs[n : n + 4], outs[n + 4 :]
    loss, g_hb, g_eb, g_bias, g_gain, g_shift, up_hb, up_eb, up_bias, up_gain, up_shift = tiny
    PR = low.shape[1]
    ins = [pltpu.make_async_copy(grads.at[p], low.at[p], isem.at[p]) for p in range(PIECES)]
    ins += [pltpu.make_async_copy(a, b, isem.at[PIECES + i]) for i, (a, b) in enumerate(zip(small, scratch))]
    ins.append(pltpu.make_async_copy(vectors, vecs, isem.at[PIECES + ns]))
    ins += [pltpu.make_async_copy(a, b, isem.at[PIECES + ns + 1 + i]) for i, (a, b) in enumerate(zip(src, held))]
    for c in ins:
        c.start()
    homes = [
        [(g_shrink.at[0:PR], 0, PR)], [(g_shrink.at[PR : 2 * PR], 0, PR)], [(g_expand.at[0:PR], 0, PR)],
        [(g_expand.at[PR : 2 * PR], 0, PR)], [(g_in.at[0], 0, HS), (g_in.at[1], HS, 2 * HS)],
        [(g_in.at[2], 0, HS), (g_out, HS, 2 * HS)],
    ]
    waits, k = [], n
    for p in range(PIECES):
        ins[p].wait()
        wide[p] = low[p].astype(F32)
        for home, a, b in homes[p]:
            c = pltpu.make_async_copy(wide.at[p, a:b], home, osem.at[k])
            c.start()
            waits.append(c)
            k += 1
    for c in ins[PIECES : PIECES + ns + 1]:
        c.wait()
    for i, (a, b) in enumerate(zip(held, dst)):
        ins[PIECES + ns + 1 + i].wait()
        c = pltpu.make_async_copy(a, b, osem.at[i])
        c.start()
        waits.append(c)
    t = lax.axis_index("tensor")
    whole = vecs[...]
    loss[...] = whole[6:7, 0:1]
    g_hb[...] = whole[9:11, 0:HS]
    g_bias[...], g_gain[...], g_shift[...] = whole[0:2, :], whole[2:4, :], whole[4:6, :]
    for name, o in (("heads_bias", up_hb), ("branch_bias", up_bias), ("norm_gain", up_gain), ("norm_shift", up_shift)):
        o[...] = MOMENTUM * v["momentum_" + name][...] + (1.0 - MOMENTUM) * v[name][...].astype(F32)
    eb = MOMENTUM * v["momentum_expand_bias"][...] + (1.0 - MOMENTUM) * v["expand_bias"][...].astype(F32)
    at = lax.broadcasted_iota(jnp.int32, eb.shape, 0)
    for i in range(fin.FS // 128):
        g_eb[i : i + 1, :] = whole[8:9, i * 128 : i * 128 + 128]
        row = jnp.where(at == t * (fin.FS // 128) + i, eb, 0.0)
        up_eb[i : i + 1, :] = jnp.sum(row, axis=0, keepdims=True)
    for i, (a, b) in enumerate(zip(tiny, tiny_out)):
        c = pltpu.make_async_copy(a, b, osem.at[n + 6 + i])
        c.start()
        waits.append(c)
    for c in waits:
        c.wait()


def cfg_limit():
    return 64 * 1024 * 1024 - 4096


def solution(mesh):
    both = ("dp", "tensor")
    in_specs = (
        P(both, None), P(both, None), P("dp"), P("dp"), P(), P(both, None), P(both, None), P(None, None, "tensor"),
        P(None, "tensor"), P("tensor", None), P(None, "tensor"), P(), P("tensor", None), P(), P(), P(),
        P(None, "dp", "tensor"), P(None, "tensor"), P("tensor", "dp"), P("dp", "tensor"), P(), P("tensor", "dp"), P(), P(), P(),
    )
    out_specs = (
        P(both, None), P(both, None), P(), P(both, None), P(None, None, "tensor"), P(None, "tensor"), P("tensor", None),
        P(None, "tensor"), P("tensor"), P("tensor", None), P(), P(), P(), P(None, "dp", "tensor"), P(None, "tensor"),
        P("tensor", "dp"), P("dp", "tensor"), P("tensor"), P("tensor", "dp"), P(), P(), P(),
    )
    shape = dict(mesh.shape)
    return jax.shard_map(lambda *a: local(shape, *a), mesh=mesh, in_specs=in_specs, out_specs=out_specs, check_vma=False)
```

```python
import types

import jax
import jax.numpy as jnp
from jax import lax
from jax.experimental import pallas as pl
from jax.experimental.pallas import tpu as pltpu
from jax.sharding import PartitionSpec as P

HEAD = 64
SOFTMAX_DIVISOR = 0.05
MOMENTUM = 0.5
NORM_EPSILON = 1e-12
MASKED_SCORE = -1e30
ROOT_HALF = 0.7071067811865476
GAUSS_SCALE = 0.3989422804014327
MESH = pl.DeviceIdType.MESH
F32, BF16 = jnp.float32, jnp.bfloat16
NN = (((1,), (0,)), ((), ()))
NT = (((1,), (1,)), ((), ()))
TN = (((0,), (0,)), ((), ()))
TENSOR = 4
PIECES = 6


TAIL = (
    (2, 3), (4, 1), (1, 4), (0, 5), (5, 1), (4, 2), (3, 3), (1, 5), (2, 4), (5, 2), (4, 3),
    (3, 4), (2, 5), (5, 3), (4, 4), (3, 5), (5, 4), (4, 5), (5, 5),
)


def dot(a, b, dims=NN):
    return lax.dot_general(a, b, dims, preferred_element_type=F32)


def norm_rows(v, gain, shift):
    c = v - jnp.mean(v, axis=-1, keepdims=True)
    inverse = lax.rsqrt(jnp.mean(c * c, axis=-1, keepdims=True) + NORM_EPSILON)
    n = c * inverse
    return n * gain + shift, n, inverse


def norm_back(up, n, inverse, gain):
    e = up * gain
    inner = e - jnp.mean(e, axis=-1, keepdims=True) - n * jnp.mean(e * n, axis=-1, keepdims=True)
    return inner * inverse


def gelu_parts(z):
    a = jnp.abs(z) * ROOT_HALF
    g = jnp.exp(-0.5 * z * z)
    s = 1.0 / (1.0 + 0.3275911 * a)
    poly = ((((1.061405429 * s - 1.453152027) * s + 1.421413741) * s - 0.284496736) * s + 0.254829592) * s
    q = 0.5 * poly * g
    cdf = jnp.where(z >= 0, 1.0 - q, q)
    return z * cdf, cdf + z * GAUSS_SCALE * g


def pack(q, k, v, o):
    lo, hi = slice(0, 128), slice(128, 192)
    pair = lambda a, b: jnp.concatenate([a[:, hi], b[:, hi]], axis=1)
    tiles = [q[:, lo], pair(q, v), k[:, lo], v[:, lo], pair(k, o), o[:, lo]]
    return jnp.concatenate([a.astype(BF16) for a in tiles], axis=1)


def kernel(cfg, *refs):
    r = types.SimpleNamespace(**dict(zip(cfg.names, refs)))
    D, HS, FS, L, DP, RC = cfg.D, cfg.HS, cfg.FS, cfg.L, cfg.DP, cfg.RC
    N, SH, NZ = DP * TENSOR, cfg.SH, DP // 2
    NCH = L // RC
    dp, t = lax.axis_index("dp"), lax.axis_index("tensor")
    px = lax.rem(t + 2, TENSOR)
    sib = t + 1 - 2 * lax.rem(t, 2)
    y, z = lax.rem(dp, 2), dp // 2
    me = dp * TENSOR + t
    d_x, d_sib, d_y = (dp, px), (dp, sib), (dp + 1 - 2 * y, t)

    def d_z(k):
        return (lax.rem(z + k, NZ) * 2 + y, t)

    def from_z(k):
        return lax.rem(z - k + NZ, NZ)

    def remote(src, dst, sems, i, dev):
        return pltpu.make_async_remote_copy(
            src_ref=src, dst_ref=dst, send_sem=sems[0].at[i], recv_sem=sems[1].at[i], device_id=dev, device_id_type=MESH
        )

    sends = []

    def send(src, dst, sems, i, dev):
        c = remote(src, dst, sems, i, dev)
        c.start()
        sends.append(c)
        return c

    last = []

    class Spread:
        def __init__(self, block, sems, base):
            self.block, self.sems, self.base = block, sems, base

        def copy(self, i, owner_z, dev):
            b = self.block(y, owner_z)
            return remote(b, b, self.sems, self.base + i, dev)

        def right(self, k):
            return self.copy(k - 1, z - k + 1, (dp + 2, t))

        def left(self, k):
            return self.copy(NZ - 1 + k - 1, z + k - 1, (dp - 2, t))

        def over(self, owner_z):
            return self.copy(2 * (NZ - 1) + owner_z, owner_z, d_y)

        def start(self):
            pl.when(z < NZ - 1)(lambda: self.right(1).start())
            pl.when(z > 0)(lambda: self.left(1).start())
            self.over(z).start()
            last.append(self.sent)

        def step(self, k):
            @pl.when(z >= k)
            def _():
                self.copy(k - 1, z - k, d_y).wait_recv()
                if k < NZ - 1:
                    pl.when(z < NZ - 1)(lambda: self.right(k + 1).start())
                self.over(z - k).start()

            @pl.when(z + k <= NZ - 1)
            def _():
                self.copy(NZ - 1 + k - 1, z + k, d_y).wait_recv()
                if k < NZ - 1:
                    pl.when(z > 0)(lambda: self.left(k + 1).start())
                self.over(z + k).start()

        def finish(self):
            for o in range(NZ):
                b = self.block(1 - y, o)
                remote(b, b, self.sems, self.base + 2 * (NZ - 1) + o, d_y).wait_recv()

        def sent(self):
            for k in range(1, NZ):
                pl.when(jnp.logical_and(z >= k - 1, z < NZ - 1))(lambda: self.copy(k - 1, z, d_y).wait_send())
                pl.when(jnp.logical_and(z + k - 1 <= NZ - 1, z > 0))(lambda: self.copy(NZ - 1 + k - 1, z, d_y).wait_send())
            for o in range(NZ):
                self.copy(2 * (NZ - 1) + o, z, d_y).wait_send()

    loads = {}

    def load(name, src, dst):
        c = pltpu.make_async_copy(src, dst, r.lsem.at[len(loads)])
        c.start()
        loads[name] = c

    stores = []

    def store(src, dst):
        c = pltpu.make_async_copy(src, dst, r.ssem.at[len(stores)])
        c.start()
        stores.append(c)

    xs, cs = (r.xs, r.xr), (r.cs, r.cr)

    load("q", r.query_tokens, r.X.at[0, 0])
    load("hi", r.heads_in, r.wqi.at[:, 0])
    load("wo", r.heads_out, r.wo.at[0])
    small_in = cfg.small
    for name in small_in:
        load(name, getattr(r, name), getattr(r, "v_" + name))
    if cfg.gather:
        load("mhi", r.momentum_heads_in, r.mhi)
        load("mo", r.momentum_heads_out, r.mho)
    load("we", r.expand_weight, r.we.at[0])
    load("ws", r.shrink_weight, r.ws.at[0])
    if cfg.gather:
        load("me", r.momentum_expand_weight, r.mex)
        load("ms", r.momentum_shrink_weight, r.msh)
    else:
        load("kw", r.key_weights, r.wk.at[0])
    load("k", r.key_tokens, r.X.at[1, 0])
    load("queue", r.key_queue, r.queue)
    load("cot", r.token_cotangent, r.cot)

    bar = pltpu.get_barrier_semaphore()

    def greet(i, c):
        o = lax.rem(me + i, N)
        pl.semaphore_signal(bar, inc=1, device_id=(o // TENSOR, lax.rem(o, TENSOR)), device_id_type=MESH)
        return c

    lax.fori_loop(1, N, greet, 0)
    pl.semaphore_wait(bar, N - 1)

    c_xq = send(r.query_tokens, r.X.at[0, 1], xs, 0, d_x)
    c_xk = send(r.key_tokens, r.X.at[1, 1], xs, 1, d_x)
    c_hi = send(r.heads_in, r.wqi.at[:, 1], cs, 0, d_sib)
    c_wo = send(r.heads_out, r.wo.at[1], cs, 1, d_sib)

    def small_blend(name):
        return MOMENTUM * getattr(r, "v_momentum_" + name)[...] + (1.0 - MOMENTUM) * getattr(r, "v_" + name)[...].astype(F32)

    for name in small_in:
        loads[name].wait()
    r.hb[0, 0:2, :] = r.v_heads_bias[...].astype(F32)
    r.hb[0, 2:4, :] = small_blend("heads_bias")
    c_hb = send(r.hb.at[0], r.hb.at[1], cs, 4, d_sib)
    bb = (r.v_branch_bias[...].astype(F32), small_blend("branch_bias"))
    gain = (r.v_norm_gain[...].astype(F32), small_blend("norm_gain"))
    shift = (r.v_norm_shift[...].astype(F32), small_blend("norm_shift"))
    for w, b in enumerate((r.v_expand_bias[...].astype(F32), small_blend("expand_bias"))):
        for k in range(TENSOR):
            for i in range(FS // 128):
                at = k * (FS // 128) + i
                r.eb[w, k : k + 1, i * 128 : i * 128 + 128] = b[at : at + 1, :]

    gs = (r.gs, r.gr)
    spread_n = 2 * (NZ - 1) + NZ

    def g_block(part):
        return lambda yy, zz: r.wk.at[0, part, pl.ds(pl.multiple_of((zz * 2 + yy) * SH, SH), SH), :]

    g_of = [Spread(g_block(part), gs, part * spread_n) for part in range(3)]

    g_done = {}

    def g_sib(part):
        g_done[part] = send(r.wk.at[0, part], r.wk.at[1, part], gs, 3 * spread_n + part, d_sib)

    def g_step(part, k):
        if cfg.gather:
            if k < NZ:
                g_of[part].step(k)
            else:
                g_of[part].finish()
                g_sib(part)

    if cfg.gather:
        own = pl.ds(pl.multiple_of(dp * SH, SH), SH)
        pick = (
            lax.broadcasted_iota(jnp.int32, (SH, D), 1) == lax.broadcasted_iota(jnp.int32, (SH, D), 0) + dp * SH
        ).astype(F32).astype(BF16)
        eye = (
            lax.broadcasted_iota(jnp.int32, (D, D), 0) == lax.broadcasted_iota(jnp.int32, (D, D), 1)
        ).astype(F32).astype(BF16)
        for name in ("hi", "mhi", "wo", "mo"):
            loads[name].wait()
        blocks = [
            MOMENTUM * r.mhi[i] + (1.0 - MOMENTUM) * dot(pick, r.wqi[i, 0], NT) for i in range(3)
        ]
        for i in range(3):
            r.mhi[i] = blocks[i]
        u = MOMENTUM * r.mho[...] + (1.0 - MOMENTUM) * dot(r.wo[0], pick, NT)
        r.mho[...] = u
        blocks.append(dot(eye[:SH, :SH], u.astype(BF16), NT))
        r.wk[0, 0, own, :] = pack(*blocks)
        g_of[0].start()
        for name in ("we", "me", "ws", "ms"):
            loads[name].wait()
        u = MOMENTUM * r.mex[...] + (1.0 - MOMENTUM) * r.we[0, own, :].astype(F32)
        r.mex[...] = u
        r.wk[0, 1, own, :] = u.astype(BF16)
        u = MOMENTUM * r.msh[...] + (1.0 - MOMENTUM) * dot(pick, r.ws[0], NT)
        r.msh[...] = u
        r.wk[0, 2, own, :] = u.astype(BF16)
        store(r.mhi, r.o_heads_in)
        store(r.mho, r.o_heads_out)
        store(r.mex, r.o_expand)
        store(r.msh, r.o_shrink)
    else:
        for name in ("hi", "wo", "we", "ws", "kw"):
            loads[name].wait()
        for part in range(3):
            g_sib(part)
    c_we = send(r.expand_weight, r.we.at[1], cs, 2, d_sib)
    c_ws = send(r.shrink_weight, r.ws.at[1], cs, 3, d_sib)

    lengths = ((r.query_lengths[t], r.query_lengths[px]), (r.key_lengths[t], r.key_lengths[px]))
    low_half = lax.broadcasted_iota(jnp.int32, (1, 128), 1) < HEAD
    key_at = lax.broadcasted_iota(jnp.int32, (1, L), 1)

    def split(tile):
        zero = jnp.zeros_like(tile)
        return jnp.where(low_half, tile, zero), jnp.where(low_half, zero, tile)

    def softmax(q, k, valid):
        sc = jnp.where(valid, dot(q, k, NT), MASKED_SCORE)
        top = jnp.max(sc, axis=-1, keepdims=True)
        e = jnp.exp(sc - top)
        tot = jnp.sum(e, axis=-1, keepdims=True)
        return (e * (1.0 / tot)).astype(BF16), top + jnp.log(tot)

    def scaled(v):
        return (v.astype(BF16).astype(F32) * HEAD**-0.5).astype(BF16)

    hpair = 2 * HS // 128

    def attend_query(crop, out):
        x = r.X[0, crop]
        valid = key_at < lengths[0][crop]
        q = scaled(dot(x, r.wqi[0].reshape(2 * HS, D), NT) + bias_q)
        k = dot(x, r.wqi[1].reshape(2 * HS, D), NT).astype(BF16)
        v = (dot(x, r.wqi[2].reshape(2 * HS, D), NT) + bias_v).astype(BF16)
        r.qkv[0, crop], r.qkv[1, crop], r.qkv[2, crop] = q, k, v
        at = lax.broadcasted_iota(jnp.int32, (L, 128), 1)
        logs = jnp.zeros((L, 128), F32)
        ctx = []
        for i in range(hpair):
            tile = slice(128 * i, 128 * i + 128)
            ks, vs = split(k[:, tile]), split(v[:, tile])
            c = None
            for h in range(2):
                p, g = softmax(q[:, tile], ks[h], valid)
                logs = jnp.where(at == 2 * i + h, g, logs)
                d = dot(p, vs[h])
                c = d if c is None else c + d
            ctx.append(c.astype(BF16))
        r.G[crop] = logs
        ctx = jnp.concatenate(ctx, axis=1)
        r.C[crop] = ctx
        out[...] = dot(ctx, r.wo[...].reshape(2 * HS, D))

    def attend_key(crop, out):
        x = r.X[1, crop]
        valid = key_at < lengths[1][crop]
        total = None
        for s in range(2):
            w = r.wk[s, 0]
            hb = r.hb[s]
            qb, vb, none = hb[2:3, :], hb[3:4, :], jnp.zeros((1, 128), F32)
            bias = jnp.concatenate(
                [qb[:, 0:128], jnp.concatenate([qb[:, 128:192], vb[:, 128:192]], axis=1), none, vb[:, 0:128], none], axis=1
            )
            pr = dot(x, w[:, 0:640]) + bias
            q01, m = pr[:, 0:128], pr[:, 128:256].astype(BF16)
            q01, q2 = scaled(q01), (m.astype(F32) * HEAD**-0.5).astype(BF16)
            k01, v01, k2 = (pr[:, 128 * i : 128 * i + 128].astype(BF16) for i in (2, 3, 4))
            ks, vs = split(k01), split(v01)
            p0, _ = softmax(q01, ks[0], valid)
            p1, _ = softmax(q01, ks[1], valid)
            p2, _ = softmax(q2, split(k2)[0], valid)
            c01 = (dot(p0, vs[0]) + dot(p1, vs[1])).astype(BF16)
            c2 = dot(p2, split(m)[1]).astype(BF16)
            a = dot(jnp.concatenate([c2, c01], axis=1), w[:, 512:768], NT)
            total = a if total is None else total + a
        out[...] = total

    def attend(w, crop, out):
        (attend_query, attend_key)[w](crop, out)

    def swap(src32, sbuf, rbuf, base):
        out = []
        for j in range(NCH):
            rows = pl.ds(j * RC, RC)
            sbuf[rows, :] = src32[rows, :].astype(BF16)
            out.append(send(sbuf.at[rows], rbuf.at[rows], xs, base + j, d_x))
        return out

    FT = 256

    def feed(w, crop, row0, rows_n, out):
        rows = pl.ds(row0, rows_n)
        u = r.U[w, crop, rows, :]

        total = None
        for i in range(2 * (FS // FT)):
            s, j = i // (FS // FT), i % (FS // FT)
            cols = slice(j * FT, j * FT + FT)
            b = r.eb[w, pl.ds(t if s == 0 else sib, 1), cols]
            if w == 0:
                zz = dot(u, r.we[s, :, cols]) + b
            else:
                zz = dot(u, r.wk[s, 1, :, cols]) + b
            h, slope = gelu_parts(zz)
            h = h.astype(BF16)
            if w == 0:
                r.H[s, crop, rows, cols] = h
                r.slope[s, crop, rows, cols] = slope.astype(BF16)
                f = dot(h, r.ws[s, cols, :])
            else:
                f = dot(h, r.wk[s, 2, :, cols], NT)

            total = f if total is None else total + f
        out[rows, :] = total

    x_of = {}

    def first_norm(w, base):
        out = []
        for j in range(NCH):
            rows = pl.ds(j * RC, RC)
            x_of["A", w][j].wait_recv()
            m = r.X[w, 0, rows, :].astype(F32) + (r.own[w, rows, :] + r.arecv[w, rows, :].astype(F32)) + bb[w][0:1, :]
            u, n, inv = norm_rows(m, gain[w][0:1, :], shift[w][0:1, :])
            r.Uf[w, rows, :] = u
            r.U[w, 0, rows, :] = u.astype(BF16)
            if w == 0:
                r.N1[rows, :] = n
                r.i1[rows, :] = jnp.broadcast_to(inv, (RC, 128))
            out.append(send(r.U.at[w, 0, rows], r.U.at[w, 1, rows], xs, base + j, d_x))
        x_of["U", w] = out

    def second_norm(w, o_ref, o_hbm):
        pooled = jnp.zeros((1, D), F32)
        length = lengths[w][0]
        for j in range(NCH):
            rows = pl.ds(j * RC, RC)
            x_of["F", w][j].wait_recv()
            m = r.Uf[w, rows, :] + (r.own[w, rows, :] + r.frecv[w, rows, :].astype(F32)) + bb[w][1:2, :]
            out, n, inv = norm_rows(m, gain[w][1:2, :], shift[w][1:2, :])
            o_ref[rows, :] = out.astype(BF16)
            if w == 0:
                r.N2[rows, :] = n
                r.i2[rows, :] = jnp.broadcast_to(inv, (RC, 128))
            valid = lax.broadcasted_iota(jnp.int32, (RC, 1), 0) + j * RC < length
            pooled += jnp.sum(jnp.where(valid, out, 0.0), axis=0, keepdims=True)
        store(o_ref, o_hbm)
        pooled = pooled / length.astype(F32)
        inverse = lax.rsqrt(jnp.sum(pooled * pooled, axis=-1, keepdims=True) + 1e-06)
        unit = (pooled * inverse).astype(BF16).astype(F32)
        return pooled, inverse, unit

    KL = D // 128

    def tile_of(row):
        return jnp.concatenate([row[:, i * 128 : (i + 1) * 128] for i in range(KL)], axis=0)

    def to_all(sbuf_of, rbuf, sems, base):
        def go(i, c):
            o = lax.rem(me + i, N)
            remote(sbuf_of(o), rbuf.at[me], sems, base, (o // TENSOR, lax.rem(o, TENSOR))).start()
            return c

        lax.fori_loop(1, N, go, 0)

    def from_all(rbuf, sems, base):
        tiles = rbuf.at[pl.ds(0, N - 1)]
        remote(tiles, tiles, sems, base, d_x).wait_recv()

    def sent_all(sems, base):
        tiles = r.nrecv.at[pl.ds(0, N - 1)]
        remote(tiles, tiles, sems, base, d_x).wait_send()

    us = (r.us, r.ur)

    loads["q"].wait()
    c_hi.wait_recv()
    c_wo.wait_recv()
    c_hb.wait_recv()
    bias_q = jnp.concatenate([r.hb[0, 0:1, :], r.hb[1, 0:1, :]], axis=1)
    bias_v = jnp.concatenate([r.hb[0, 1:2, :], r.hb[1, 1:2, :]], axis=1)
    attend(0, 0, r.own.at[0])
    g_step(0, 1)
    if cfg.gather:
        g_of[1].start()
        g_of[2].start()
    c_xq.wait_recv()
    attend(0, 1, r.part)
    x_of["A", 0] = swap(r.part, r.asend.at[0], r.arecv.at[0], 2)
    g_step(0, 2)
    g_step(1, 1)
    g_step(2, 1)
    g_step(0, 3)
    c_we.wait_recv()
    c_ws.wait_recv()
    first_norm(0, 2 + NCH)
    g_step(1, 2)
    feed(0, 0, 0, L, r.own.at[0])
    g_step(2, 2)
    g_step(0, NZ)
    g_step(1, 3)
    kb = 2 + 3 * NCH
    c_xk.wait_recv()
    loads["k"].wait()
    g_done[0].wait_recv()
    attend(1, 1, r.part)
    x_of["A", 1] = swap(r.part, r.asend.at[1], r.arecv.at[1], kb)
    attend(1, 0, r.own.at[1])

    def feed_partner(w, base):
        x_of["F", w] = []
        for j in range(NCH):
            x_of["U", w][j].wait_recv()
            feed(w, 1, j * RC, RC, r.part)
            rows = pl.ds(j * RC, RC)
            r.fsend[w, rows, :] = r.part[rows, :].astype(BF16)
            x_of["F", w].append(send(r.fsend.at[w, rows], r.frecv.at[w, rows], xs, base + j, d_x))

    feed_partner(0, 2 + 2 * NCH)
    g_step(2, 3)
    g_step(1, NZ)
    first_norm(1, kb + NCH)
    q_pooled, q_inverse, q_unit = second_norm(0, r.oq, r.query_output)
    r.usend[0, 0:KL, :] = tile_of(q_unit)
    r.units[0, me, 0:KL, :] = tile_of(q_unit)
    to_all(lambda o: r.usend.at[0], r.units.at[0], us, 0)
    g_step(2, NZ)
    g_done[1].wait_recv()
    g_done[2].wait_recv()
    feed(1, 0, 0, L, r.own.at[1])
    feed_partner(1, kb + 2 * NCH)
    loads["queue"].wait()
    from_all(r.units.at[0], us, 0)
    all_q = jnp.concatenate([r.units[0, :, i, :] for i in range(KL)], axis=1).astype(BF16)
    logits = dot(all_q, r.queue[...], NT) / SOFTMAX_DIVISOR
    top = jnp.max(logits, axis=-1, keepdims=True)
    e = jnp.exp(logits - top)
    tot = jnp.sum(e, axis=-1, keepdims=True)
    grad = dot(e.astype(BF16), r.queue[...])
    for i in range(KL):
        r.nsend[:, i, :] = grad[:, i * 128 : (i + 1) * 128]
    r.nsend[:, KL, :] = jnp.broadcast_to(top, (N, 128))
    r.nsend[:, KL + 1, :] = jnp.broadcast_to(tot, (N, 128))
    r.nrecv[me] = r.nsend[me]
    to_all(lambda o: r.nsend.at[o], r.nrecv, us, 1)
    k_pooled, k_inverse, k_unit = second_norm(1, r.ok, r.key_output)
    r.usend[1, 0:KL, :] = tile_of(k_unit)
    r.units[1, me, 0:KL, :] = tile_of(k_unit)
    to_all(lambda o: r.usend.at[1], r.units.at[1], us, 2)
    from_all(r.nrecv, us, 1)
    from_all(r.units.at[1], us, 2)

    pos = r.positives[me]
    hit = lax.broadcasted_iota(jnp.int32, (N, 1, 1), 0) == pos
    partner = jnp.sum(jnp.where(hit, r.units[1][:, 0:KL, :], 0.0), axis=0)
    mine = r.usend[0, 0:KL, :]
    match = jnp.sum(jnp.sum(mine * partner, axis=1, keepdims=True), axis=0, keepdims=True) / SOFTMAX_DIVISOR
    tops, tots = r.nrecv[:, KL, :], r.nrecv[:, KL + 1, :]
    peak = jnp.maximum(jnp.max(jnp.max(tops, axis=0, keepdims=True), axis=1, keepdims=True), match)
    total = jnp.sum(tots * jnp.exp(tops - peak), axis=0, keepdims=True)[:, 0:1]
    level = peak + jnp.log(total + jnp.exp(match - peak))
    loss = level - match
    scale = jnp.exp(r.nrecv[:, KL : KL + 1, :] - level.reshape(1, 1, 1)) * (1.0 / SOFTMAX_DIVISOR)
    du = jnp.sum(r.nrecv[:, 0:KL, :] * scale, axis=0) + (jnp.exp(match - level) - 1.0) / SOFTMAX_DIVISOR * partner
    du = jnp.concatenate([du[i : i + 1, :] for i in range(KL)], axis=1)
    along = jnp.sum(q_pooled * du, axis=-1, keepdims=True)
    d_pooled = q_inverse * du - q_pooled * (q_inverse * q_inverse * q_inverse) * along
    per_token = d_pooled / lengths[0][0].astype(F32)

    loads["cot"].wait()
    bbase = kb + 3 * NCH
    small = [jnp.zeros((1, D), F32) for _ in range(6)]
    x_of["dF"] = []
    for j in range(NCH):
        rows = pl.ds(j * RC, RC)
        valid = lax.broadcasted_iota(jnp.int32, (RC, 1), 0) + j * RC < lengths[0][0]
        dy = r.cot[rows, :].astype(F32) + jnp.where(valid, per_token, 0.0)
        n2 = r.N2[rows, :]
        d2 = norm_back(dy, n2, r.i2[rows, 0:1], gain[0][1:2, :])
        r.d2[rows, :] = d2
        r.dF[0, rows, :] = d2.astype(BF16)
        x_of["dF"].append(send(r.dF.at[0, rows], r.dF.at[1, rows], xs, bbase + j, d_x))
        small[1] += jnp.sum(d2, axis=0, keepdims=True)
        small[3] += jnp.sum(dy * n2, axis=0, keepdims=True)
        small[5] += jnp.sum(dy, axis=0, keepdims=True)

    def feed_back(crop, row0, rows_n, out):
        rows = pl.ds(row0, rows_n)
        df = r.dF[crop, rows, :]

        total = None
        for i in range(2 * (FS // FT)):
            s, j = i // (FS // FT), i % (FS // FT)
            cols = slice(j * FT, j * FT + FT)
            dh = dot(df, r.ws[s, cols, :], NT)
            dz = (dh * r.slope[s, crop, rows, cols].astype(F32)).astype(BF16)
            r.dZ[s, crop, rows, cols] = dz
            du_ = dot(dz, r.we[s, :, cols], NT)

            total = du_ if total is None else total + du_
        out[rows, :] = total

    feed_back(0, 0, L, r.own.at[0])
    PR = 3 * 2 * D // (2 * 3) // 2
    HF, CH = PR // 2, PR // 2 // max(NZ, 1)
    ws_sem = (r.ws_s, r.ws_r)
    per = 2 + NZ - 1 + 2 * (NZ - 1) + NZ

    def piece_part(p, s):
        if p < 2:
            h = r.H[s].reshape(2 * L, FS)[:, p * PR : (p + 1) * PR]
            return dot(h, r.dF[...].reshape(2 * L, D), TN)
        u = r.U[0].reshape(2 * L, D)[:, (p - 2) * PR : (p - 1) * PR]
        return dot(u, r.dZ[s].reshape(2 * L, FS), TN)

    w_of = {}

    def w_sib_send(p):
        w_of["s", p] = send(r.wsend.at[p], r.wrecv.at[p], ws_sem, p * per, d_sib)

    def w_sib(p):
        if p < 4:
            r.wsend[p] = piece_part(p, 1).astype(BF16)
        else:
            for q in range(2):
                i = (p - 4) * 2 + q
                a = r.dqkv[i].reshape(2 * L, 2 * HS) if i < 3 else r.C[...].reshape(2 * L, 2 * HS)
                b = r.X[0].reshape(2 * L, D) if i < 3 else r.dA[...].reshape(2 * L, D)
                v = dot(a, b, TN)
                rows = slice(q * HS, (q + 1) * HS)
                r.hacc[p - 4, rows, :] = v[0:HS, :]
                r.wsend[p, rows, :] = v[HS:, :].astype(BF16)
        w_sib_send(p)

    def half(h):
        return pl.ds(pl.multiple_of(h * HF, HF), HF)

    def w_own(p):
        v = piece_part(p, 0) if p < 4 else r.hacc[p - 4]
        w_of["s", p].wait_recv()
        v = v + r.wrecv[p].astype(F32)
        if cfg.gather:
            r.wacc[p] = v.astype(BF16)
        else:
            r.wacc32[p] = v
        if cfg.gather:
            w_of["y", p] = send(r.wacc.at[p, half(1 - y)], r.wyr.at[p], ws_sem, p * per + 1, d_y)
        else:
            store(r.wacc32.at[p], r.grads.at[p])

    def chunk(zz):
        return pl.ds(pl.multiple_of(zz * CH, CH), CH)

    def place(yy, zz):
        return pl.ds(pl.multiple_of(yy * HF + zz * CH, CH), CH)

    def w_y(p):
        w_of["y", p].wait_recv()
        r.wys[p] = (r.wacc[p, half(y), :].astype(F32) + r.wyr[p].astype(F32)).astype(BF16)
        for k in range(1, NZ):
            to = lax.rem(z + k, NZ)
            w_of["z", p, k] = send(r.wys.at[p, chunk(to)], r.wzr.at[p, k - 1], ws_sem, p * per + 1 + k, d_z(k))

    def w_z(p):
        v = r.wys[p, chunk(z), :].astype(F32)
        for k in range(1, NZ):
            w_of["z", p, k].wait_recv()
            v += r.wzr[p, k - 1].astype(F32)
        r.wout[p, place(y, z), :] = v.astype(BF16)
        w_of["b", p] = Spread(lambda yy, zz: r.wout.at[p, place(yy, zz)], ws_sem, p * per + 2 + NZ - 1)
        w_of["b", p].start()

    def w_step(p, k):
        if not cfg.gather:
            return
        if k < 2:
            (w_y, w_z)[k](p)
        elif k < 1 + NZ:
            w_of["b", p].step(k - 1)
        else:
            w_of["b", p].finish()
            store(r.wout.at[p], r.grads.at[p])

    for j in range(NCH):
        x_of["dF"][j].wait_recv()
    w_sib(0)
    x_of["dU"] = []
    for j in range(NCH):
        feed_back(1, j * RC, RC, r.part)
        rows = pl.ds(j * RC, RC)
        r.dusend[rows, :] = r.part[rows, :].astype(BF16)
        x_of["dU"].append(send(r.dusend.at[rows], r.durecv.at[rows], xs, bbase + NCH + j, d_x))
        if j == 0:
            w_own(0)
    w_sib(1)
    w_sib(2)
    w_own(1)
    w_sib(3)
    w_own(2)
    w_own(3)
    x_of["dA"] = []
    for j in range(NCH):
        rows = pl.ds(j * RC, RC)
        x_of["dU"][j].wait_recv()
        du1 = r.d2[rows, :] + (r.own[0, rows, :] + r.durecv[rows, :].astype(F32))
        n1 = r.N1[rows, :]
        dm = norm_back(du1, n1, r.i1[rows, 0:1], gain[0][0:1, :])
        r.Uf[0, rows, :] = dm
        r.dA[0, rows, :] = dm.astype(BF16)
        x_of["dA"].append(send(r.dA.at[0, rows], r.dA.at[1, rows], xs, bbase + 2 * NCH + j, d_x))
        small[0] += jnp.sum(dm, axis=0, keepdims=True)
        small[2] += jnp.sum(du1 * n1, axis=0, keepdims=True)
        small[4] += jnp.sum(du1, axis=0, keepdims=True)
    for i in range(6):
        r.sm[0, i : i + 1, :] = small[i]
    r.sm[0, 6:7, :] = jnp.broadcast_to(loss, (1, D))
    w_step(0, 0)

    def attend_back(crop, out):
        valid = key_at < lengths[0][crop]
        dc = dot(r.dA[crop], r.wo[...].reshape(2 * HS, D), NT).astype(BF16)
        q, k, v, g = r.qkv[0, crop], r.qkv[1, crop], r.qkv[2, crop], r.G[crop]
        grads = ([], [], [])
        for i in range(hpair):
            tile = slice(128 * i, 128 * i + 128)
            qt, dct = q[:, tile], dc[:, tile]
            qs, ks, vs, dcs = split(qt), split(k[:, tile]), split(v[:, tile]), split(dct)
            acc = None
            for h in range(2):
                sc = jnp.where(valid, dot(qt, ks[h], NT), MASKED_SCORE)
                pw = jnp.exp(sc - g[:, 2 * i + h : 2 * i + h + 1])
                dpw = dot(dct, vs[h], NT)
                inner = jnp.sum(dpw * pw, axis=-1, keepdims=True)
                ds = (pw * (dpw - inner)).astype(BF16)
                new = (dot(ds, ks[h]), dot(ds, qs[h], TN), dot(pw.astype(BF16), dcs[h], TN))
                acc = new if acc is None else tuple(a + b for a, b in zip(acc, new))
            for m, (into, a) in enumerate(zip(grads, acc)):
                into.append((a * HEAD**-0.5 if m == 0 else a).astype(BF16))
        total = None
        for m in range(3):
            d = jnp.concatenate(grads[m], axis=1)
            r.dqkv[m, crop] = d
            a = dot(d, r.wqi[m].reshape(2 * HS, D))
            total = a if total is None else total + a
        out[...] = total

    attend_back(0, r.own.at[1])
    w_step(1, 0)
    w_step(0, 1)
    w_step(2, 0)
    for j in range(NCH):
        x_of["dA"][j].wait_recv()
    w_step(1, 1)
    attend_back(1, r.part)
    x_of["dX"] = swap(r.part, r.dxsend, r.dxrecv, bbase + 3 * NCH)
    w_step(0, 2)
    w_sib(4)
    w_step(3, 0)
    w_sib(5)
    w_step(2, 1)
    w_own(4)
    w_step(1, 2)
    w_own(5)
    w_step(0, 3)
    w_step(3, 1)
    w_step(2, 2)
    w_step(1, 3)
    bq = jnp.sum(r.dqkv[0].reshape(2 * L, 2 * HS).astype(F32), axis=0, keepdims=True)
    bv = jnp.sum(r.dqkv[2].reshape(2 * L, 2 * HS).astype(F32), axis=0, keepdims=True)
    for s in range(2):
        eb = jnp.sum(r.dZ[s].reshape(2 * L, FS).astype(F32), axis=0, keepdims=True)
        dst = (r.sm.at[0], r.smx)[s]
        dst[8:9, 0:FS] = eb
        dst[9:10, 0:HS] = bq[:, s * HS : (s + 1) * HS]
        dst[10:11, 0:HS] = bv[:, s * HS : (s + 1) * HS]
    r.smx[0:8, :] = r.sm[0, 0:8, :]
    bs = (r.bs, r.br)
    b_sib = send(r.smx, r.smr.at[0], bs, 0, d_sib)
    w_step(4, 0)
    w_step(0, 4)
    b_sib.wait_recv()
    r.sm[1] = r.sm[0] + r.smr[0]
    b_x = send(r.sm.at[1, 0:8], r.smr.at[1, 0:8], bs, 1, d_x)
    w_step(3, 2)
    w_step(5, 0)
    b_x.wait_recv()
    r.sm[2] = r.sm[1]
    r.sm[2, 0:8, :] = r.sm[1, 0:8, :] + r.smr[1, 0:8, :]
    nb = DP.bit_length() - 1 if cfg.gather else 0

    def butterfly(k):
        other = dp + (1 - 2 * lax.rem(dp // (1 << k), 2)) * (1 << k)
        return send(r.sm.at[2 + k], r.smr.at[2 + k], bs, 2 + k, (other, t))

    def add_up(k, c):
        c.wait_recv()
        r.sm[3 + k] = r.sm[2 + k] + r.smr[2 + k]

    b_k = butterfly(0) if nb else None
    for n, (p, k) in enumerate(TAIL):
        w_step(p, k)
        if n == 4:
            for j in range(NCH):
                rows = pl.ds(j * RC, RC)
                x_of["dX"][j].wait_recv()
                r.Uf[1, rows, :] = r.Uf[0, rows, :] + (r.own[1, rows, :] + r.dxrecv[rows, :].astype(F32))
            store(r.Uf.at[1], r.input_gradient)
        if nb and n % 4 == 0 and n // 4 < nb:
            add_up(n // 4, b_k)
            b_k = butterfly(n // 4 + 1) if n // 4 + 1 < nb else None
    store(r.sm.at[2 + nb], r.vectors)

    for c in sends:
        c.wait_send()
    for i in range(3):
        sent_all(us, i)
    for f in last:
        f()
    for c in stores:
        c.wait()


def blend(old, new):
    return MOMENTUM * old + (1.0 - MOMENTUM) * new.astype(F32)


def local(mesh_shape, query_tokens, key_tokens, query_lengths, key_lengths, positives, key_queue, token_cotangent, heads_in,
          heads_bias, heads_out, expand_weight, expand_bias, shrink_weight, branch_bias, norm_gain, norm_shift,
          momentum_heads_in, momentum_heads_bias, momentum_heads_out, momentum_expand_weight, momentum_expand_bias,
          momentum_shrink_weight, momentum_branch_bias, momentum_norm_gain, momentum_norm_shift):
    DP = mesh_shape["dp"]
    L, D = query_tokens.shape
    HS, FS = heads_in.shape[2], expand_weight.shape[1]
    SH = D // DP
    N = DP * TENSOR
    PR = D // 2
    QN = key_queue.shape[0]
    gather = DP > 2 and SH % 16 == 0 and (PR // DP) % 16 == 0
    RC = 128
    NCH = L // RC
    NZ = DP // 2
    t, dp = lax.axis_index("tensor"), lax.axis_index("dp")
    cfg = types.SimpleNamespace(D=D, HS=HS, FS=FS, L=L, DP=DP, SH=SH, RC=RC, gather=gather)

    vm = lambda shape, dtype: pltpu.VMEM(shape, dtype)
    any_, vmem, smem = (pl.BlockSpec(memory_space=m) for m in (pl.ANY, pltpu.VMEM, pltpu.SMEM))
    small = {
        "heads_bias": heads_bias, "expand_bias": expand_bias.reshape(-1, 128), "branch_bias": branch_bias,
        "norm_gain": norm_gain, "norm_shift": norm_shift, "momentum_heads_bias": momentum_heads_bias,
        "momentum_expand_bias": momentum_expand_bias.reshape(-1, 128), "momentum_branch_bias": momentum_branch_bias,
        "momentum_norm_gain": momentum_norm_gain, "momentum_norm_shift": momentum_norm_shift,
    }
    cfg.small = list(small)
    ins = [
        ("query_tokens", query_tokens, any_), ("key_tokens", key_tokens, any_),
        ("query_lengths", query_lengths, smem), ("key_lengths", key_lengths, smem), ("positives", positives, smem),
        ("key_queue", key_queue, any_), ("token_cotangent", token_cotangent, any_),
        ("heads_in", jnp.swapaxes(heads_in, 1, 2), any_), ("heads_out", heads_out, any_),
        ("expand_weight", expand_weight, any_), ("shrink_weight", shrink_weight, any_),
    ] + [(n, a, any_) for n, a in small.items()]
    outs = [
        ("query_output", (L, D), BF16), ("key_output", (L, D), BF16), ("input_gradient", (L, D), F32),
        ("grads", (PIECES, PR, D), BF16 if gather else F32), ("vectors", (16, D), F32),
    ]
    if gather:
        ins += [("momentum_heads_in", momentum_heads_in, any_), ("momentum_heads_out", momentum_heads_out, any_),
                ("momentum_expand_weight", momentum_expand_weight, any_),
                ("momentum_shrink_weight", momentum_shrink_weight.T, any_)]
        outs += [("o_heads_in", momentum_heads_in.shape, F32), ("o_heads_out", momentum_heads_out.shape, F32),
                 ("o_expand", momentum_expand_weight.shape, F32), ("o_shrink", momentum_shrink_weight.shape[::-1], F32)]
    else:
        updated = (
            blend(momentum_heads_in, lax.dynamic_slice_in_dim(heads_in, dp * SH, SH, 1)),
            blend(momentum_heads_out, lax.dynamic_slice_in_dim(heads_out, dp * SH, SH, 1)),
            blend(momentum_expand_weight, lax.dynamic_slice_in_dim(expand_weight, dp * SH, SH, 0)),
            blend(momentum_shrink_weight, lax.dynamic_slice_in_dim(shrink_weight, dp * SH, SH, 1)),
        )
        whole = lambda a, axis: lax.all_gather(a.astype(BF16), "dp", axis=axis, tiled=True)
        heads = jnp.concatenate([whole(updated[0], 1), whole(updated[1].T, 0)[None]], axis=0)
        ins += [("key_weights", jnp.stack([pack(*heads), whole(updated[2], 0), whole(updated[3].T, 0)]), any_)]
    scratch = [
        ("X", vm((2, 2, L, D), BF16)), ("wqi", vm((3, 2, HS, D), BF16)), ("wo", vm((2, HS, D), BF16)),
        ("we", vm((2, D, FS), BF16)), ("ws", vm((2, FS, D), BF16)),
        ("wk", vm((2, 3, D, D), BF16)),
        ("queue", vm((QN, D), BF16)), ("cot", vm((L, D), BF16)),
        ("hb", vm((2, 4, HS), F32)), ("eb", vm((2, TENSOR, FS), F32)),
        ("qkv", vm((3, 2, L, 2 * HS), BF16)), ("G", vm((2, L, 128), F32)), ("C", vm((2, L, 2 * HS), BF16)),
        ("U", vm((2, 2, L, D), BF16)), ("Uf", vm((2, L, D), F32)), ("H", vm((2, 2, L, FS), BF16)),
        ("slope", vm((2, 2, L, FS), BF16)), ("N1", vm((L, D), F32)), ("N2", vm((L, D), F32)),
        ("i1", vm((L, 128), F32)), ("i2", vm((L, 128), F32)), ("own", vm((2, L, D), F32)), ("part", vm((L, D), F32)),
        ("asend", vm((2, L, D), BF16)), ("arecv", vm((2, L, D), BF16)), ("fsend", vm((2, L, D), BF16)),
        ("frecv", vm((2, L, D), BF16)), ("oq", vm((L, D), BF16)), ("ok", vm((L, D), BF16)),
        ("usend", vm((2, 8, 128), F32)), ("units", vm((2, N, 8, 128), F32)), ("nsend", vm((N, 8, 128), F32)),
        ("nrecv", vm((N, 8, 128), F32)), ("d2", vm((L, D), F32)), ("dF", vm((2, L, D), BF16)),
        ("dZ", vm((2, 2, L, FS), BF16)), ("dusend", vm((L, D), BF16)), ("durecv", vm((L, D), BF16)),
        ("dA", vm((2, L, D), BF16)), ("dqkv", vm((3, 2, L, 2 * HS), BF16)), ("hacc", vm((2, PR, D), F32)),
        ("dxsend", vm((L, D), BF16)), ("dxrecv", vm((L, D), BF16)),
        ("wsend", vm((PIECES, PR, D), BF16)), ("wrecv", vm((PIECES, PR, D), BF16)),
        ("sm", vm((3 + DP.bit_length(), 16, D), F32)), ("smx", vm((16, D), F32)),
        ("smr", vm((2 + DP.bit_length(), 16, D), F32)),
    ]
    if gather:
        scratch += [
            ("mhi", vm(momentum_heads_in.shape, F32)), ("mho", vm(momentum_heads_out.shape, F32)),
            ("mex", vm(momentum_expand_weight.shape, F32)), ("msh", vm(momentum_shrink_weight.shape[::-1], F32)),
            ("wacc", vm((PIECES, PR, D), BF16)), ("wyr", vm((PIECES, PR // 2, D), BF16)),
            ("wys", vm((PIECES, PR // 2, D), BF16)), ("wzr", vm((PIECES, NZ - 1, PR // DP, D), BF16)),
            ("wout", vm((PIECES, PR, D), BF16)),
        ]
    else:
        scratch += [("wacc32", vm((PIECES, PR, D), F32))]
    scratch += [("v_" + n, vm(a.shape, a.dtype)) for n, a in small.items()]
    dma = pltpu.SemaphoreType.DMA
    nx = 2 + 6 * NCH + 4 * NCH
    ng = 3 * (2 * (NZ - 1) + NZ) + 3
    nw = PIECES * (2 + 3 * (NZ - 1) + NZ)
    nv = 3
    for pair, count in ((("xs", "xr"), nx), (("cs", "cr"), 5), (("gs", "gr"), ng), (("us", "ur"), nv),
                        (("ws_s", "ws_r"), nw), (("bs", "br"), 2 + DP.bit_length())):
        for name in pair:
            scratch.append((name, dma((count,))))
    scratch += [("lsem", dma((32,))), ("ssem", dma((16,)))]
    cfg.names = [n for n, *_ in ins] + [n for n, *_ in outs] + [n for n, _ in scratch]

    def body(*refs):
        kernel(cfg, *refs)

    res = pl.pallas_call(
        body,
        out_shape=[jax.ShapeDtypeStruct(s, d) for _, s, d in outs],
        in_specs=[s for _, _, s in ins],
        out_specs=[any_] * len(outs),
        scratch_shapes=[s for _, s in scratch],
        compiler_params=pltpu.CompilerParams(collective_id=0, has_side_effects=True, vmem_limit_bytes=cfg_limit()),
        name="step",
    )(*[a for _, a, _ in ins])
    query_out, key_out, d_tokens, grads, vectors = res[:5]
    if gather:
        updates = res[5:]
    else:
        updates = (updated[0], updated[1], updated[2], updated[3].T)
        grads, vectors = lax.psum((grads, vectors), "dp")
    copies = (query_out, key_out, d_tokens) + tuple(updates)
    fin = types.SimpleNamespace(D=D, HS=HS, FS=FS, small=list(small))
    out = [jax.ShapeDtypeStruct(a.shape, a.dtype) for a in copies]
    out += [jax.ShapeDtypeStruct(sh, F32) for sh in ((FS, D), (D, FS), (3, HS, D), (HS, D))]
    tiny = ((1, 1), (2, HS), (FS // 128, 128), (2, D), (2, D), (2, D), (2, HS), (FS // 128, 128), (2, D), (2, D), (2, D))
    out += [jax.ShapeDtypeStruct(sh, F32) for sh in tiny]
    out_dmas = len(copies) + 7 + len(tiny)
    done = pl.pallas_call(
        lambda *a: finish(fin, *a),
        out_shape=out,
        in_specs=[any_] * (len(copies) + 2 + len(small)),
        out_specs=[any_] * len(out),
        scratch_shapes=[vm(a.shape, a.dtype) for a in small.values()] + [vm(sh, F32) for sh in tiny]
        + [vm(a.shape, a.dtype) for a in copies]
        + [vm(vectors.shape, F32), vm((PIECES, PR, D), grads.dtype), vm((PIECES, PR, D), F32), dma((32,)), dma((out_dmas,))],
        compiler_params=pltpu.CompilerParams(vmem_limit_bytes=cfg_limit()),
        name="finish",
    )(*copies, grads, vectors, *small.values())
    (query_out, key_out, d_tokens, up_in, up_out, up_expand, up_shrink, g_shrink, g_expand, g_in, g_out, loss, g_hb, g_eb,
     g_bias, g_gain, g_shift, up_hb, up_eb, up_bias, up_gain, up_shift) = done
    return (
        query_out, key_out, loss[0, 0], d_tokens, jnp.swapaxes(g_in, 1, 2), g_hb, g_out, g_expand, g_eb.reshape(FS), g_shrink,
        g_bias, g_gain, g_shift, up_in, up_hb, up_out, up_expand, up_eb.reshape(FS), up_shrink.T, up_bias, up_gain, up_shift,
    )


def finish(fin, *refs):
    HS = fin.HS
    ns, n, nt = len(fin.small), 7, 11
    src, grads, vectors, small = refs[:n], refs[n], refs[n + 1], refs[n + 2 : n + 2 + ns]
    outs, scratch = refs[n + 2 + ns : n + 2 + ns + n + 4 + nt], refs[n + 2 + ns + n + 4 + nt :]
    v = dict(zip(fin.small, scratch[:ns]))
    tiny, held = scratch[ns : ns + nt], scratch[ns + nt : ns + nt + n]
    vecs, low, wide, isem, osem = scratch[ns + nt + n :]
    dst, (g_shrink, g_expand, g_in, g_out), tiny_out = outs[:n], outs[n : n + 4], outs[n + 4 :]
    loss, g_hb, g_eb, g_bias, g_gain, g_shift, up_hb, up_eb, up_bias, up_gain, up_shift = tiny
    PR = low.shape[1]
    ins = [pltpu.make_async_copy(grads.at[p], low.at[p], isem.at[p]) for p in range(PIECES)]
    ins += [pltpu.make_async_copy(a, b, isem.at[PIECES + i]) for i, (a, b) in enumerate(zip(small, scratch))]
    ins.append(pltpu.make_async_copy(vectors, vecs, isem.at[PIECES + ns]))
    ins += [pltpu.make_async_copy(a, b, isem.at[PIECES + ns + 1 + i]) for i, (a, b) in enumerate(zip(src, held))]
    for c in ins:
        c.start()
    homes = [
        [(g_shrink.at[0:PR], 0, PR)], [(g_shrink.at[PR : 2 * PR], 0, PR)], [(g_expand.at[0:PR], 0, PR)],
        [(g_expand.at[PR : 2 * PR], 0, PR)], [(g_in.at[0], 0, HS), (g_in.at[1], HS, 2 * HS)],
        [(g_in.at[2], 0, HS), (g_out, HS, 2 * HS)],
    ]
    waits, k = [], n
    for p in range(PIECES):
        ins[p].wait()
        wide[p] = low[p].astype(F32)
        for home, a, b in homes[p]:
            c = pltpu.make_async_copy(wide.at[p, a:b], home, osem.at[k])
            c.start()
            waits.append(c)
            k += 1
    for c in ins[PIECES : PIECES + ns + 1]:
        c.wait()
    for i, (a, b) in enumerate(zip(held, dst)):
        ins[PIECES + ns + 1 + i].wait()
        c = pltpu.make_async_copy(a, b, osem.at[i])
        c.start()
        waits.append(c)
    t = lax.axis_index("tensor")
    whole = vecs[...]
    loss[...] = whole[6:7, 0:1]
    g_hb[...] = whole[9:11, 0:HS]
    g_bias[...], g_gain[...], g_shift[...] = whole[0:2, :], whole[2:4, :], whole[4:6, :]
    for name, o in (("heads_bias", up_hb), ("branch_bias", up_bias), ("norm_gain", up_gain), ("norm_shift", up_shift)):
        o[...] = MOMENTUM * v["momentum_" + name][...] + (1.0 - MOMENTUM) * v[name][...].astype(F32)
    eb = MOMENTUM * v["momentum_expand_bias"][...] + (1.0 - MOMENTUM) * v["expand_bias"][...].astype(F32)
    at = lax.broadcasted_iota(jnp.int32, eb.shape, 0)
    for i in range(fin.FS // 128):
        g_eb[i : i + 1, :] = whole[8:9, i * 128 : i * 128 + 128]
        row = jnp.where(at == t * (fin.FS // 128) + i, eb, 0.0)
        up_eb[i : i + 1, :] = jnp.sum(row, axis=0, keepdims=True)
    for i, (a, b) in enumerate(zip(tiny, tiny_out)):
        c = pltpu.make_async_copy(a, b, osem.at[n + 6 + i])
        c.start()
        waits.append(c)
    for c in waits:
        c.wait()


def cfg_limit():
    return 64 * 1024 * 1024 - 4096


def solution(mesh):
    both = ("dp", "tensor")
    in_specs = (
        P(both, None), P(both, None), P("dp"), P("dp"), P(), P(both, None), P(both, None), P(None, None, "tensor"),
        P(None, "tensor"), P("tensor", None), P(None, "tensor"), P(), P("tensor", None), P(), P(), P(),
        P(None, "dp", "tensor"), P(None, "tensor"), P("tensor", "dp"), P("dp", "tensor"), P(), P("tensor", "dp"), P(), P(), P(),
    )
    out_specs = (
        P(both, None), P(both, None), P(), P(both, None), P(None, None, "tensor"), P(None, "tensor"), P("tensor", None),
        P(None, "tensor"), P("tensor"), P("tensor", None), P(), P(), P(), P(None, "dp", "tensor"), P(None, "tensor"),
        P("tensor", "dp"), P("dp", "tensor"), P("tensor"), P("tensor", "dp"), P(), P(), P(),
    )
    shape = dict(mesh.shape)
    return jax.shard_map(lambda *a: local(shape, *a), mesh=mesh, in_specs=in_specs, out_specs=out_specs, check_vma=False)
```

```python
import types

import jax
import jax.numpy as jnp
from jax import lax
from jax.experimental import pallas as pl
from jax.experimental.pallas import tpu as pltpu
from jax.sharding import PartitionSpec as P

HEAD = 64
SOFTMAX_DIVISOR = 0.05
MOMENTUM = 0.5
NORM_EPSILON = 1e-12
MASKED_SCORE = -1e30
ROOT_HALF = 0.7071067811865476
GAUSS_SCALE = 0.3989422804014327
MESH = pl.DeviceIdType.MESH
F32, BF16 = jnp.float32, jnp.bfloat16
NN = (((1,), (0,)), ((), ()))
NT = (((1,), (1,)), ((), ()))
TN = (((0,), (0,)), ((), ()))
TENSOR = 4
PIECES = 6


TAIL = (
    (2, 3), (4, 1), (1, 4), (0, 5), (5, 1), (4, 2), (3, 3), (1, 5), (2, 4), (5, 2), (4, 3),
    (3, 4), (2, 5), (5, 3), (4, 4), (3, 5), (5, 4), (4, 5), (5, 5),
)


def dot(a, b, dims=NN):
    return lax.dot_general(a, b, dims, preferred_element_type=F32)


def norm_rows(v, gain, shift):
    c = v - jnp.mean(v, axis=-1, keepdims=True)
    inverse = lax.rsqrt(jnp.mean(c * c, axis=-1, keepdims=True) + NORM_EPSILON)
    n = c * inverse
    return n * gain + shift, n, inverse


def norm_back(up, n, inverse, gain):
    e = up * gain
    inner = e - jnp.mean(e, axis=-1, keepdims=True) - n * jnp.mean(e * n, axis=-1, keepdims=True)
    return inner * inverse


def gelu_parts(z):
    a = jnp.abs(z) * ROOT_HALF
    g = jnp.exp(-0.5 * z * z)
    s = 1.0 / (1.0 + 0.3275911 * a)
    poly = ((((1.061405429 * s - 1.453152027) * s + 1.421413741) * s - 0.284496736) * s + 0.254829592) * s
    q = 0.5 * poly * g
    cdf = jnp.where(z >= 0, 1.0 - q, q)
    return z * cdf, cdf + z * GAUSS_SCALE * g


def pack(q, k, v, o):
    lo, hi = slice(0, 128), slice(128, 192)
    pair = lambda a, b: jnp.concatenate([a[:, hi], b[:, hi]], axis=1)
    tiles = [q[:, lo], pair(q, v), k[:, lo], v[:, lo], pair(k, o), o[:, lo]]
    return jnp.concatenate([a.astype(BF16) for a in tiles], axis=1)


def kernel(cfg, *refs):
    r = types.SimpleNamespace(**dict(zip(cfg.names, refs)))
    D, HS, FS, L, DP, RC = cfg.D, cfg.HS, cfg.FS, cfg.L, cfg.DP, cfg.RC
    N, SH, NZ = DP * TENSOR, cfg.SH, DP // 2
    NCH = L // RC
    dp, t = lax.axis_index("dp"), lax.axis_index("tensor")
    px = lax.rem(t + 2, TENSOR)
    sib = t + 1 - 2 * lax.rem(t, 2)
    y, z = lax.rem(dp, 2), dp // 2
    me = dp * TENSOR + t
    d_x, d_sib, d_y = (dp, px), (dp, sib), (dp + 1 - 2 * y, t)

    def d_z(k):
        return (lax.rem(z + k, NZ) * 2 + y, t)

    def from_z(k):
        return lax.rem(z - k + NZ, NZ)

    def remote(src, dst, sems, i, dev):
        return pltpu.make_async_remote_copy(
            src_ref=src, dst_ref=dst, send_sem=sems[0].at[i], recv_sem=sems[1].at[i], device_id=dev, device_id_type=MESH
        )

    sends = []

    def send(src, dst, sems, i, dev):
        c = remote(src, dst, sems, i, dev)
        c.start()
        sends.append(c)
        return c

    last = []

    class Spread:
        def __init__(self, block, sems, base):
            self.block, self.sems, self.base = block, sems, base

        def copy(self, i, owner_z, dev):
            b = self.block(y, owner_z)
            return remote(b, b, self.sems, self.base + i, dev)

        def right(self, k):
            return self.copy(k - 1, z - k + 1, (dp + 2, t))

        def left(self, k):
            return self.copy(NZ - 1 + k - 1, z + k - 1, (dp - 2, t))

        def over(self, owner_z):
            return self.copy(2 * (NZ - 1) + owner_z, owner_z, d_y)

        def start(self):
            pl.when(z < NZ - 1)(lambda: self.right(1).start())
            pl.when(z > 0)(lambda: self.left(1).start())
            self.over(z).start()
            last.append(self.sent)

        def step(self, k):
            @pl.when(z >= k)
            def _():
                self.copy(k - 1, z - k, d_y).wait_recv()
                if k < NZ - 1:
                    pl.when(z < NZ - 1)(lambda: self.right(k + 1).start())
                self.over(z - k).start()

            @pl.when(z + k <= NZ - 1)
            def _():
                self.copy(NZ - 1 + k - 1, z + k, d_y).wait_recv()
                if k < NZ - 1:
                    pl.when(z > 0)(lambda: self.left(k + 1).start())
                self.over(z + k).start()

        def finish(self):
            for o in range(NZ):
                b = self.block(1 - y, o)
                remote(b, b, self.sems, self.base + 2 * (NZ - 1) + o, d_y).wait_recv()

        def sent(self):
            for k in range(1, NZ):
                pl.when(jnp.logical_and(z >= k - 1, z < NZ - 1))(lambda: self.copy(k - 1, z, d_y).wait_send())
                pl.when(jnp.logical_and(z + k - 1 <= NZ - 1, z > 0))(lambda: self.copy(NZ - 1 + k - 1, z, d_y).wait_send())
            for o in range(NZ):
                self.copy(2 * (NZ - 1) + o, z, d_y).wait_send()

    loads = {}

    def load(name, src, dst):
        c = pltpu.make_async_copy(src, dst, r.lsem.at[len(loads)])
        c.start()
        loads[name] = c

    stores = []

    def store(src, dst):
        c = pltpu.make_async_copy(src, dst, r.ssem.at[len(stores)])
        c.start()
        stores.append(c)

    xs, cs = (r.xs, r.xr), (r.cs, r.cr)

    load("q", r.query_tokens, r.X.at[0, 0])
    load("hi", r.heads_in, r.wqi.at[:, 0])
    load("wo", r.heads_out, r.wo.at[0])
    small_in = cfg.small
    for name in small_in:
        load(name, getattr(r, name), getattr(r, "v_" + name))
    if cfg.gather:
        load("mhi", r.momentum_heads_in, r.mhi)
        load("mo", r.momentum_heads_out, r.mho)
    load("we", r.expand_weight, r.we.at[0])
    load("ws", r.shrink_weight, r.ws.at[0])
    if cfg.gather:
        load("me", r.momentum_expand_weight, r.mex)
        load("ms", r.momentum_shrink_weight, r.msh)
    else:
        load("kw", r.key_weights, r.wk.at[0])
    load("k", r.key_tokens, r.X.at[1, 0])
    load("queue", r.key_queue, r.queue)
    load("cot", r.token_cotangent, r.cot)

    bar = pltpu.get_barrier_semaphore()

    def greet(i, c):
        o = lax.rem(me + i, N)
        pl.semaphore_signal(bar, inc=1, device_id=(o // TENSOR, lax.rem(o, TENSOR)), device_id_type=MESH)
        return c

    lax.fori_loop(1, N, greet, 0)
    pl.semaphore_wait(bar, N - 1)

    c_xq = send(r.query_tokens, r.X.at[0, 1], xs, 0, d_x)
    c_xk = send(r.key_tokens, r.X.at[1, 1], xs, 1, d_x)
    c_hi = send(r.heads_in, r.wqi.at[:, 1], cs, 0, d_sib)
    c_wo = send(r.heads_out, r.wo.at[1], cs, 1, d_sib)

    def small_blend(name):
        return MOMENTUM * getattr(r, "v_momentum_" + name)[...] + (1.0 - MOMENTUM) * getattr(r, "v_" + name)[...].astype(F32)

    for name in small_in:
        loads[name].wait()
    r.hb[0, 0:2, :] = r.v_heads_bias[...].astype(F32)
    r.hb[0, 2:4, :] = small_blend("heads_bias")
    c_hb = send(r.hb.at[0], r.hb.at[1], cs, 4, d_sib)
    bb = (r.v_branch_bias[...].astype(F32), small_blend("branch_bias"))
    gain = (r.v_norm_gain[...].astype(F32), small_blend("norm_gain"))
    shift = (r.v_norm_shift[...].astype(F32), small_blend("norm_shift"))
    for w, b in enumerate((r.v_expand_bias[...].astype(F32), small_blend("expand_bias"))):
        for k in range(TENSOR):
            for i in range(FS // 128):
                at = k * (FS // 128) + i
                r.eb[w, k : k + 1, i * 128 : i * 128 + 128] = b[at : at + 1, :]

    gs = (r.gs, r.gr)
    spread_n = 2 * (NZ - 1) + NZ

    def g_block(part):
        return lambda yy, zz: r.wk.at[0, part, pl.ds(pl.multiple_of((zz * 2 + yy) * SH, SH), SH), :]

    g_of = [Spread(g_block(part), gs, part * spread_n) for part in range(3)]

    g_done = {}

    def g_sib(part):
        g_done[part] = send(r.wk.at[0, part], r.wk.at[1, part], gs, 3 * spread_n + part, d_sib)

    def g_step(part, k):
        if cfg.gather:
            if k < NZ:
                g_of[part].step(k)
            else:
                g_of[part].finish()
                g_sib(part)

    if cfg.gather:
        own = pl.ds(pl.multiple_of(dp * SH, SH), SH)
        pick = (
            lax.broadcasted_iota(jnp.int32, (SH, D), 1) == lax.broadcasted_iota(jnp.int32, (SH, D), 0) + dp * SH
        ).astype(F32).astype(BF16)
        eye = (
            lax.broadcasted_iota(jnp.int32, (D, D), 0) == lax.broadcasted_iota(jnp.int32, (D, D), 1)
        ).astype(F32).astype(BF16)
        for name in ("hi", "mhi", "wo", "mo"):
            loads[name].wait()
        blocks = [
            MOMENTUM * r.mhi[i] + (1.0 - MOMENTUM) * dot(pick, r.wqi[i, 0], NT) for i in range(3)
        ]
        for i in range(3):
            r.mhi[i] = blocks[i]
        u = MOMENTUM * r.mho[...] + (1.0 - MOMENTUM) * dot(r.wo[0], pick, NT)
        r.mho[...] = u
        blocks.append(dot(eye[:SH, :SH], u.astype(BF16), NT))
        r.wk[0, 0, own, :] = pack(*blocks)
        g_of[0].start()
        for name in ("we", "me", "ws", "ms"):
            loads[name].wait()
        u = MOMENTUM * r.mex[...] + (1.0 - MOMENTUM) * r.we[0, own, :].astype(F32)
        r.mex[...] = u
        r.wk[0, 1, own, :] = u.astype(BF16)
        u = MOMENTUM * r.msh[...] + (1.0 - MOMENTUM) * dot(pick, r.ws[0], NT)
        r.msh[...] = u
        r.wk[0, 2, own, :] = u.astype(BF16)
        store(r.mhi, r.o_heads_in)
        store(r.mho, r.o_heads_out)
        store(r.mex, r.o_expand)
        store(r.msh, r.o_shrink)
    else:
        for name in ("hi", "wo", "we", "ws", "kw"):
            loads[name].wait()
        for part in range(3):
            g_sib(part)
    c_we = send(r.expand_weight, r.we.at[1], cs, 2, d_sib)
    c_ws = send(r.shrink_weight, r.ws.at[1], cs, 3, d_sib)

    lengths = ((r.query_lengths[t], r.query_lengths[px]), (r.key_lengths[t], r.key_lengths[px]))
    low_half = lax.broadcasted_iota(jnp.int32, (1, 128), 1) < HEAD
    key_at = lax.broadcasted_iota(jnp.int32, (1, L), 1)

    def split(tile):
        zero = jnp.zeros_like(tile)
        return jnp.where(low_half, tile, zero), jnp.where(low_half, zero, tile)

    def softmax(q, k, valid):
        sc = jnp.where(valid, dot(q, k, NT), MASKED_SCORE)
        top = jnp.max(sc, axis=-1, keepdims=True)
        e = jnp.exp(sc - top)
        tot = jnp.sum(e, axis=-1, keepdims=True)
        return (e * (1.0 / tot)).astype(BF16), top + jnp.log(tot)

    def scaled(v):
        return (v.astype(BF16).astype(F32) * HEAD**-0.5).astype(BF16)

    hpair = 2 * HS // 128

    def attend_query(crop, out):
        x = r.X[0, crop]
        valid = key_at < lengths[0][crop]
        q = scaled(dot(x, r.wqi[0].reshape(2 * HS, D), NT) + bias_q)
        k = dot(x, r.wqi[1].reshape(2 * HS, D), NT).astype(BF16)
        v = (dot(x, r.wqi[2].reshape(2 * HS, D), NT) + bias_v).astype(BF16)
        r.qkv[0, crop], r.qkv[1, crop], r.qkv[2, crop] = q, k, v
        at = lax.broadcasted_iota(jnp.int32, (L, 128), 1)
        logs = jnp.zeros((L, 128), F32)
        ctx = []
        for i in range(hpair):
            tile = slice(128 * i, 128 * i + 128)
            ks, vs = split(k[:, tile]), split(v[:, tile])
            c = None
            for h in range(2):
                p, g = softmax(q[:, tile], ks[h], valid)
                logs = jnp.where(at == 2 * i + h, g, logs)
                d = dot(p, vs[h])
                c = d if c is None else c + d
            ctx.append(c.astype(BF16))
        r.G[crop] = logs
        ctx = jnp.concatenate(ctx, axis=1)
        r.C[crop] = ctx
        out[...] = dot(ctx, r.wo[...].reshape(2 * HS, D))

    def attend_key(crop, out):
        x = r.X[1, crop]
        valid = key_at < lengths[1][crop]
        total = None
        for s in range(2):
            w = r.wk[s, 0]
            hb = r.hb[s]
            qb, vb, none = hb[2:3, :], hb[3:4, :], jnp.zeros((1, 128), F32)
            bias = jnp.concatenate(
                [qb[:, 0:128], jnp.concatenate([qb[:, 128:192], vb[:, 128:192]], axis=1), none, vb[:, 0:128], none], axis=1
            )
            pr = dot(x, w[:, 0:640]) + bias
            q01, m = pr[:, 0:128], pr[:, 128:256].astype(BF16)
            q01, q2 = scaled(q01), (m.astype(F32) * HEAD**-0.5).astype(BF16)
            k01, v01, k2 = (pr[:, 128 * i : 128 * i + 128].astype(BF16) for i in (2, 3, 4))
            ks, vs = split(k01), split(v01)
            p0, _ = softmax(q01, ks[0], valid)
            p1, _ = softmax(q01, ks[1], valid)
            p2, _ = softmax(q2, split(k2)[0], valid)
            c01 = (dot(p0, vs[0]) + dot(p1, vs[1])).astype(BF16)
            c2 = dot(p2, split(m)[1]).astype(BF16)
            a = dot(jnp.concatenate([c2, c01], axis=1), w[:, 512:768], NT)
            total = a if total is None else total + a
        out[...] = total

    def attend(w, crop, out):
        (attend_query, attend_key)[w](crop, out)

    def swap(src32, sbuf, rbuf, base):
        out = []
        for j in range(NCH):
            rows = pl.ds(j * RC, RC)
            sbuf[rows, :] = src32[rows, :].astype(BF16)
            out.append(send(sbuf.at[rows], rbuf.at[rows], xs, base + j, d_x))
        return out

    FT = 256

    def feed(w, crop, row0, rows_n, out):
        rows = pl.ds(row0, rows_n)
        u = r.U[w, crop, rows, :]

        total = None
        for i in range(2 * (FS // FT)):
            s, j = i // (FS // FT), i % (FS // FT)
            cols = slice(j * FT, j * FT + FT)
            b = r.eb[w, pl.ds(t if s == 0 else sib, 1), cols]
            if w == 0:
                zz = dot(u, r.we[s, :, cols]) + b
            else:
                zz = dot(u, r.wk[s, 1, :, cols]) + b
            h, slope = gelu_parts(zz)
            h = h.astype(BF16)
            if w == 0:
                r.H[s, crop, rows, cols] = h
                r.slope[s, crop, rows, cols] = slope.astype(BF16)
                f = dot(h, r.ws[s, cols, :])
            else:
                f = dot(h, r.wk[s, 2, :, cols], NT)

            total = f if total is None else total + f
        out[rows, :] = total

    x_of = {}

    def first_norm(w, base):
        out = []
        for j in range(NCH):
            rows = pl.ds(j * RC, RC)
            x_of["A", w][j].wait_recv()
            m = r.X[w, 0, rows, :].astype(F32) + (r.own[w, rows, :] + r.arecv[w, rows, :].astype(F32)) + bb[w][0:1, :]
            u, n, inv = norm_rows(m, gain[w][0:1, :], shift[w][0:1, :])
            r.Uf[w, rows, :] = u
            r.U[w, 0, rows, :] = u.astype(BF16)
            if w == 0:
                r.N1[rows, :] = n
                r.i1[rows, :] = jnp.broadcast_to(inv, (RC, 128))
            out.append(send(r.U.at[w, 0, rows], r.U.at[w, 1, rows], xs, base + j, d_x))
        x_of["U", w] = out

    def second_norm(w, o_ref, o_hbm):
        pooled = jnp.zeros((1, D), F32)
        length = lengths[w][0]
        for j in range(NCH):
            rows = pl.ds(j * RC, RC)
            x_of["F", w][j].wait_recv()
            m = r.Uf[w, rows, :] + (r.own[w, rows, :] + r.frecv[w, rows, :].astype(F32)) + bb[w][1:2, :]
            out, n, inv = norm_rows(m, gain[w][1:2, :], shift[w][1:2, :])
            o_ref[rows, :] = out.astype(BF16)
            if w == 0:
                r.N2[rows, :] = n
                r.i2[rows, :] = jnp.broadcast_to(inv, (RC, 128))
            valid = lax.broadcasted_iota(jnp.int32, (RC, 1), 0) + j * RC < length
            pooled += jnp.sum(jnp.where(valid, out, 0.0), axis=0, keepdims=True)
        store(o_ref, o_hbm)
        pooled = pooled / length.astype(F32)
        inverse = lax.rsqrt(jnp.sum(pooled * pooled, axis=-1, keepdims=True) + 1e-06)
        unit = (pooled * inverse).astype(BF16).astype(F32)
        return pooled, inverse, unit

    KL = D // 128

    def tile_of(row):
        return jnp.concatenate([row[:, i * 128 : (i + 1) * 128] for i in range(KL)], axis=0)

    def to_all(sbuf_of, rbuf, sems, base):
        def go(i, c):
            o = lax.rem(me + i, N)
            remote(sbuf_of(o), rbuf.at[me], sems, base, (o // TENSOR, lax.rem(o, TENSOR))).start()
            return c

        lax.fori_loop(1, N, go, 0)

    def from_all(rbuf, sems, base):
        tiles = rbuf.at[pl.ds(0, N - 1)]
        remote(tiles, tiles, sems, base, d_x).wait_recv()

    def sent_all(sems, base):
        tiles = r.nrecv.at[pl.ds(0, N - 1)]
        remote(tiles, tiles, sems, base, d_x).wait_send()

    us = (r.us, r.ur)

    loads["q"].wait()
    c_hi.wait_recv()
    c_wo.wait_recv()
    c_hb.wait_recv()
    bias_q = jnp.concatenate([r.hb[0, 0:1, :], r.hb[1, 0:1, :]], axis=1)
    bias_v = jnp.concatenate([r.hb[0, 1:2, :], r.hb[1, 1:2, :]], axis=1)
    attend(0, 0, r.own.at[0])
    g_step(0, 1)
    if cfg.gather:
        g_of[1].start()
        g_of[2].start()
    c_xq.wait_recv()
    attend(0, 1, r.part)
    x_of["A", 0] = swap(r.part, r.asend.at[0], r.arecv.at[0], 2)
    g_step(0, 2)
    g_step(1, 1)
    g_step(2, 1)
    g_step(0, 3)
    c_we.wait_recv()
    c_ws.wait_recv()
    first_norm(0, 2 + NCH)
    g_step(1, 2)
    feed(0, 0, 0, L, r.own.at[0])
    g_step(2, 2)
    g_step(0, NZ)
    g_step(1, 3)
    kb = 2 + 3 * NCH
    c_xk.wait_recv()
    loads["k"].wait()
    g_done[0].wait_recv()
    attend(1, 1, r.part)
    x_of["A", 1] = swap(r.part, r.asend.at[1], r.arecv.at[1], kb)
    attend(1, 0, r.own.at[1])

    def feed_partner(w, base):
        x_of["F", w] = []
        for j in range(NCH):
            x_of["U", w][j].wait_recv()
            feed(w, 1, j * RC, RC, r.part)
            rows = pl.ds(j * RC, RC)
            r.fsend[w, rows, :] = r.part[rows, :].astype(BF16)
            x_of["F", w].append(send(r.fsend.at[w, rows], r.frecv.at[w, rows], xs, base + j, d_x))

    feed_partner(0, 2 + 2 * NCH)
    g_step(2, 3)
    g_step(1, NZ)
    first_norm(1, kb + NCH)
    q_pooled, q_inverse, q_unit = second_norm(0, r.oq, r.query_output)
    r.usend[0, 0:KL, :] = tile_of(q_unit)
    r.units[0, me, 0:KL, :] = tile_of(q_unit)
    to_all(lambda o: r.usend.at[0], r.units.at[0], us, 0)
    g_step(2, NZ)
    g_done[1].wait_recv()
    g_done[2].wait_recv()
    feed(1, 0, 0, L, r.own.at[1])
    feed_partner(1, kb + 2 * NCH)
    loads["queue"].wait()
    from_all(r.units.at[0], us, 0)
    all_q = jnp.concatenate([r.units[0, :, i, :] for i in range(KL)], axis=1).astype(BF16)
    logits = dot(all_q, r.queue[...], NT) / SOFTMAX_DIVISOR
    top = jnp.max(logits, axis=-1, keepdims=True)
    e = jnp.exp(logits - top)
    tot = jnp.sum(e, axis=-1, keepdims=True)
    grad = dot(e.astype(BF16), r.queue[...])
    for i in range(KL):
        r.nsend[:, i, :] = grad[:, i * 128 : (i + 1) * 128]
    r.nsend[:, KL, :] = jnp.broadcast_to(top, (N, 128))
    r.nsend[:, KL + 1, :] = jnp.broadcast_to(tot, (N, 128))
    r.nrecv[me] = r.nsend[me]
    to_all(lambda o: r.nsend.at[o], r.nrecv, us, 1)
    k_pooled, k_inverse, k_unit = second_norm(1, r.ok, r.key_output)
    r.usend[1, 0:KL, :] = tile_of(k_unit)
    r.units[1, me, 0:KL, :] = tile_of(k_unit)
    to_all(lambda o: r.usend.at[1], r.units.at[1], us, 2)
    from_all(r.nrecv, us, 1)
    from_all(r.units.at[1], us, 2)

    pos = r.positives[me]
    hit = lax.broadcasted_iota(jnp.int32, (N, 1, 1), 0) == pos
    partner = jnp.sum(jnp.where(hit, r.units[1][:, 0:KL, :], 0.0), axis=0)
    mine = r.usend[0, 0:KL, :]
    match = jnp.sum(jnp.sum(mine * partner, axis=1, keepdims=True), axis=0, keepdims=True) / SOFTMAX_DIVISOR
    tops, tots = r.nrecv[:, KL, :], r.nrecv[:, KL + 1, :]
    peak = jnp.maximum(jnp.max(jnp.max(tops, axis=0, keepdims=True), axis=1, keepdims=True), match)
    total = jnp.sum(tots * jnp.exp(tops - peak), axis=0, keepdims=True)[:, 0:1]
    level = peak + jnp.log(total + jnp.exp(match - peak))
    loss = level - match
    scale = jnp.exp(r.nrecv[:, KL : KL + 1, :] - level.reshape(1, 1, 1)) * (1.0 / SOFTMAX_DIVISOR)
    du = jnp.sum(r.nrecv[:, 0:KL, :] * scale, axis=0) + (jnp.exp(match - level) - 1.0) / SOFTMAX_DIVISOR * partner
    du = jnp.concatenate([du[i : i + 1, :] for i in range(KL)], axis=1)
    along = jnp.sum(q_pooled * du, axis=-1, keepdims=True)
    d_pooled = q_inverse * du - q_pooled * (q_inverse * q_inverse * q_inverse) * along
    per_token = d_pooled / lengths[0][0].astype(F32)

    loads["cot"].wait()
    bbase = kb + 3 * NCH
    small = [jnp.zeros((1, D), F32) for _ in range(6)]
    x_of["dF"] = []
    for j in range(NCH):
        rows = pl.ds(j * RC, RC)
        valid = lax.broadcasted_iota(jnp.int32, (RC, 1), 0) + j * RC < lengths[0][0]
        dy = r.cot[rows, :].astype(F32) + jnp.where(valid, per_token, 0.0)
        n2 = r.N2[rows, :]
        d2 = norm_back(dy, n2, r.i2[rows, 0:1], gain[0][1:2, :])
        r.d2[rows, :] = d2
        r.dF[0, rows, :] = d2.astype(BF16)
        x_of["dF"].append(send(r.dF.at[0, rows], r.dF.at[1, rows], xs, bbase + j, d_x))
        small[1] += jnp.sum(d2, axis=0, keepdims=True)
        small[3] += jnp.sum(dy * n2, axis=0, keepdims=True)
        small[5] += jnp.sum(dy, axis=0, keepdims=True)

    def feed_back(crop, row0, rows_n, out):
        rows = pl.ds(row0, rows_n)
        df = r.dF[crop, rows, :]

        total = None
        for i in range(2 * (FS // FT)):
            s, j = i // (FS // FT), i % (FS // FT)
            cols = slice(j * FT, j * FT + FT)
            dh = dot(df, r.ws[s, cols, :], NT)
            dz = (dh * r.slope[s, crop, rows, cols].astype(F32)).astype(BF16)
            r.dZ[s, crop, rows, cols] = dz
            du_ = dot(dz, r.we[s, :, cols], NT)

            total = du_ if total is None else total + du_
        out[rows, :] = total

    feed_back(0, 0, L, r.own.at[0])
    PR = 3 * 2 * D // (2 * 3) // 2
    HF, CH = PR // 2, PR // 2 // max(NZ, 1)
    ws_sem = (r.ws_s, r.ws_r)
    per = 2 + NZ - 1 + 2 * (NZ - 1) + NZ

    def piece_part(p, s):
        if p < 2:
            h = r.H[s].reshape(2 * L, FS)[:, p * PR : (p + 1) * PR]
            return dot(h, r.dF[...].reshape(2 * L, D), TN)
        u = r.U[0].reshape(2 * L, D)[:, (p - 2) * PR : (p - 1) * PR]
        return dot(u, r.dZ[s].reshape(2 * L, FS), TN)

    w_of = {}

    def w_sib_send(p):
        w_of["s", p] = send(r.wsend.at[p], r.wrecv.at[p], ws_sem, p * per, d_sib)

    def w_sib(p):
        if p < 4:
            r.wsend[p] = piece_part(p, 1).astype(BF16)
        else:
            for q in range(2):
                i = (p - 4) * 2 + q
                a = r.dqkv[i].reshape(2 * L, 2 * HS) if i < 3 else r.C[...].reshape(2 * L, 2 * HS)
                b = r.X[0].reshape(2 * L, D) if i < 3 else r.dA[...].reshape(2 * L, D)
                v = dot(a, b, TN)
                rows = slice(q * HS, (q + 1) * HS)
                r.hacc[p - 4, rows, :] = v[0:HS, :]
                r.wsend[p, rows, :] = v[HS:, :].astype(BF16)
        w_sib_send(p)

    def half(h):
        return pl.ds(pl.multiple_of(h * HF, HF), HF)

    def w_own(p):
        v = piece_part(p, 0) if p < 4 else r.hacc[p - 4]
        w_of["s", p].wait_recv()
        v = v + r.wrecv[p].astype(F32)
        if cfg.gather:
            r.wacc[p] = v.astype(BF16)
        else:
            r.wacc32[p] = v
        if cfg.gather:
            w_of["y", p] = send(r.wacc.at[p, half(1 - y)], r.wyr.at[p], ws_sem, p * per + 1, d_y)
        else:
            store(r.wacc32.at[p], r.grads.at[p])

    def chunk(zz):
        return pl.ds(pl.multiple_of(zz * CH, CH), CH)

    def place(yy, zz):
        return pl.ds(pl.multiple_of(yy * HF + zz * CH, CH), CH)

    def w_y(p):
        w_of["y", p].wait_recv()
        r.wys[p] = (r.wacc[p, half(y), :].astype(F32) + r.wyr[p].astype(F32)).astype(BF16)
        for k in range(1, NZ):
            to = lax.rem(z + k, NZ)
            w_of["z", p, k] = send(r.wys.at[p, chunk(to)], r.wzr.at[p, k - 1], ws_sem, p * per + 1 + k, d_z(k))

    def w_z(p):
        v = r.wys[p, chunk(z), :].astype(F32)
        for k in range(1, NZ):
            w_of["z", p, k].wait_recv()
            v += r.wzr[p, k - 1].astype(F32)
        r.wout[p, place(y, z), :] = v.astype(BF16)
        w_of["b", p] = Spread(lambda yy, zz: r.wout.at[p, place(yy, zz)], ws_sem, p * per + 2 + NZ - 1)
        w_of["b", p].start()

    def w_step(p, k):
        if not cfg.gather:
            return
        if k < 2:
            (w_y, w_z)[k](p)
        elif k < 1 + NZ:
            w_of["b", p].step(k - 1)
        else:
            w_of["b", p].finish()
            store(r.wout.at[p], r.grads.at[p])

    for j in range(NCH):
        x_of["dF"][j].wait_recv()
    w_sib(0)
    x_of["dU"] = []
    for j in range(NCH):
        feed_back(1, j * RC, RC, r.part)
        rows = pl.ds(j * RC, RC)
        r.dusend[rows, :] = r.part[rows, :].astype(BF16)
        x_of["dU"].append(send(r.dusend.at[rows], r.durecv.at[rows], xs, bbase + NCH + j, d_x))
        if j == 0:
            w_own(0)
    w_sib(1)
    w_sib(2)
    w_own(1)
    w_sib(3)
    w_own(2)
    w_own(3)
    x_of["dA"] = []
    for j in range(NCH):
        rows = pl.ds(j * RC, RC)
        x_of["dU"][j].wait_recv()
        du1 = r.d2[rows, :] + (r.own[0, rows, :] + r.durecv[rows, :].astype(F32))
        n1 = r.N1[rows, :]
        dm = norm_back(du1, n1, r.i1[rows, 0:1], gain[0][0:1, :])
        r.Uf[0, rows, :] = dm
        r.dA[0, rows, :] = dm.astype(BF16)
        x_of["dA"].append(send(r.dA.at[0, rows], r.dA.at[1, rows], xs, bbase + 2 * NCH + j, d_x))
        small[0] += jnp.sum(dm, axis=0, keepdims=True)
        small[2] += jnp.sum(du1 * n1, axis=0, keepdims=True)
        small[4] += jnp.sum(du1, axis=0, keepdims=True)
    for i in range(6):
        r.sm[0, i : i + 1, :] = small[i]
    r.sm[0, 6:7, :] = jnp.broadcast_to(loss, (1, D))
    w_step(0, 0)

    def attend_back(crop, out):
        valid = key_at < lengths[0][crop]
        dc = dot(r.dA[crop], r.wo[...].reshape(2 * HS, D), NT).astype(BF16)
        q, k, v, g = r.qkv[0, crop], r.qkv[1, crop], r.qkv[2, crop], r.G[crop]
        grads = ([], [], [])
        for i in range(hpair):
            tile = slice(128 * i, 128 * i + 128)
            qt, dct = q[:, tile], dc[:, tile]
            qs, ks, vs, dcs = split(qt), split(k[:, tile]), split(v[:, tile]), split(dct)
            acc = None
            for h in range(2):
                sc = jnp.where(valid, dot(qt, ks[h], NT), MASKED_SCORE)
                pw = jnp.exp(sc - g[:, 2 * i + h : 2 * i + h + 1])
                dpw = dot(dct, vs[h], NT)
                inner = jnp.sum(dpw * pw, axis=-1, keepdims=True)
                ds = (pw * (dpw - inner)).astype(BF16)
                new = (dot(ds, ks[h]), dot(ds, qs[h], TN), dot(pw.astype(BF16), dcs[h], TN))
                acc = new if acc is None else tuple(a + b for a, b in zip(acc, new))
            for m, (into, a) in enumerate(zip(grads, acc)):
                into.append((a * HEAD**-0.5 if m == 0 else a).astype(BF16))
        total = None
        for m in range(3):
            d = jnp.concatenate(grads[m], axis=1)
            r.dqkv[m, crop] = d
            a = dot(d, r.wqi[m].reshape(2 * HS, D))
            total = a if total is None else total + a
        out[...] = total

    attend_back(0, r.own.at[1])
    w_step(1, 0)
    w_step(0, 1)
    w_step(2, 0)
    for j in range(NCH):
        x_of["dA"][j].wait_recv()
    w_step(1, 1)
    attend_back(1, r.part)
    x_of["dX"] = swap(r.part, r.dxsend, r.dxrecv, bbase + 3 * NCH)
    w_step(0, 2)
    w_sib(4)
    w_step(3, 0)
    w_sib(5)
    w_own(4)
    w_step(2, 1)
    w_own(5)
    w_step(1, 2)
    w_step(0, 3)
    w_step(3, 1)
    w_step(2, 2)
    w_step(4, 0)
    w_step(1, 3)
    w_step(0, 4)
    bq = jnp.sum(r.dqkv[0].reshape(2 * L, 2 * HS).astype(F32), axis=0, keepdims=True)
    bv = jnp.sum(r.dqkv[2].reshape(2 * L, 2 * HS).astype(F32), axis=0, keepdims=True)
    for s in range(2):
        eb = jnp.sum(r.dZ[s].reshape(2 * L, FS).astype(F32), axis=0, keepdims=True)
        dst = (r.sm.at[0], r.smx)[s]
        dst[8:9, 0:FS] = eb
        dst[9:10, 0:HS] = bq[:, s * HS : (s + 1) * HS]
        dst[10:11, 0:HS] = bv[:, s * HS : (s + 1) * HS]
    r.smx[0:8, :] = r.sm[0, 0:8, :]
    bs = (r.bs, r.br)
    b_sib = send(r.smx, r.smr.at[0], bs, 0, d_sib)
    w_step(3, 2)
    b_sib.wait_recv()
    r.sm[1] = r.sm[0] + r.smr[0]
    b_x = send(r.sm.at[1, 0:8], r.smr.at[1, 0:8], bs, 1, d_x)
    w_step(5, 0)
    b_x.wait_recv()
    r.sm[2] = r.sm[1]
    r.sm[2, 0:8, :] = r.sm[1, 0:8, :] + r.smr[1, 0:8, :]
    nb = DP.bit_length() - 1 if cfg.gather else 0

    def butterfly(k):
        other = dp + (1 - 2 * lax.rem(dp // (1 << k), 2)) * (1 << k)
        return send(r.sm.at[2 + k], r.smr.at[2 + k], bs, 2 + k, (other, t))

    def add_up(k, c):
        c.wait_recv()
        r.sm[3 + k] = r.sm[2 + k] + r.smr[2 + k]

    b_k = butterfly(0) if nb else None
    for n, (p, k) in enumerate(TAIL):
        w_step(p, k)
        if n == 10:
            for j in range(NCH):
                rows = pl.ds(j * RC, RC)
                x_of["dX"][j].wait_recv()
                r.Uf[1, rows, :] = r.Uf[0, rows, :] + (r.own[1, rows, :] + r.dxrecv[rows, :].astype(F32))
            store(r.Uf.at[1], r.input_gradient)
        if nb and n % 4 == 3 and n // 4 < nb:
            add_up(n // 4, b_k)
            b_k = butterfly(n // 4 + 1) if n // 4 + 1 < nb else None
    store(r.sm.at[2 + nb], r.vectors)

    for c in sends:
        c.wait_send()
    for i in range(3):
        sent_all(us, i)
    for f in last:
        f()
    for c in stores:
        c.wait()


def blend(old, new):
    return MOMENTUM * old + (1.0 - MOMENTUM) * new.astype(F32)


def local(mesh_shape, query_tokens, key_tokens, query_lengths, key_lengths, positives, key_queue, token_cotangent, heads_in,
          heads_bias, heads_out, expand_weight, expand_bias, shrink_weight, branch_bias, norm_gain, norm_shift,
          momentum_heads_in, momentum_heads_bias, momentum_heads_out, momentum_expand_weight, momentum_expand_bias,
          momentum_shrink_weight, momentum_branch_bias, momentum_norm_gain, momentum_norm_shift):
    DP = mesh_shape["dp"]
    L, D = query_tokens.shape
    HS, FS = heads_in.shape[2], expand_weight.shape[1]
    SH = D // DP
    N = DP * TENSOR
    PR = D // 2
    QN = key_queue.shape[0]
    gather = DP > 2 and SH % 16 == 0 and (PR // DP) % 16 == 0
    RC = 128
    NCH = L // RC
    NZ = DP // 2
    t, dp = lax.axis_index("tensor"), lax.axis_index("dp")
    cfg = types.SimpleNamespace(D=D, HS=HS, FS=FS, L=L, DP=DP, SH=SH, RC=RC, gather=gather)

    vm = lambda shape, dtype: pltpu.VMEM(shape, dtype)
    any_, vmem, smem = (pl.BlockSpec(memory_space=m) for m in (pl.ANY, pltpu.VMEM, pltpu.SMEM))
    small = {
        "heads_bias": heads_bias, "expand_bias": expand_bias.reshape(-1, 128), "branch_bias": branch_bias,
        "norm_gain": norm_gain, "norm_shift": norm_shift, "momentum_heads_bias": momentum_heads_bias,
        "momentum_expand_bias": momentum_expand_bias.reshape(-1, 128), "momentum_branch_bias": momentum_branch_bias,
        "momentum_norm_gain": momentum_norm_gain, "momentum_norm_shift": momentum_norm_shift,
    }
    cfg.small = list(small)
    ins = [
        ("query_tokens", query_tokens, any_), ("key_tokens", key_tokens, any_),
        ("query_lengths", query_lengths, smem), ("key_lengths", key_lengths, smem), ("positives", positives, smem),
        ("key_queue", key_queue, any_), ("token_cotangent", token_cotangent, any_),
        ("heads_in", jnp.swapaxes(heads_in, 1, 2), any_), ("heads_out", heads_out, any_),
        ("expand_weight", expand_weight, any_), ("shrink_weight", shrink_weight, any_),
    ] + [(n, a, any_) for n, a in small.items()]
    outs = [
        ("query_output", (L, D), BF16), ("key_output", (L, D), BF16), ("input_gradient", (L, D), F32),
        ("grads", (PIECES, PR, D), BF16 if gather else F32), ("vectors", (16, D), F32),
    ]
    if gather:
        ins += [("momentum_heads_in", momentum_heads_in, any_), ("momentum_heads_out", momentum_heads_out, any_),
                ("momentum_expand_weight", momentum_expand_weight, any_),
                ("momentum_shrink_weight", momentum_shrink_weight.T, any_)]
        outs += [("o_heads_in", momentum_heads_in.shape, F32), ("o_heads_out", momentum_heads_out.shape, F32),
                 ("o_expand", momentum_expand_weight.shape, F32), ("o_shrink", momentum_shrink_weight.shape[::-1], F32)]
    else:
        updated = (
            blend(momentum_heads_in, lax.dynamic_slice_in_dim(heads_in, dp * SH, SH, 1)),
            blend(momentum_heads_out, lax.dynamic_slice_in_dim(heads_out, dp * SH, SH, 1)),
            blend(momentum_expand_weight, lax.dynamic_slice_in_dim(expand_weight, dp * SH, SH, 0)),
            blend(momentum_shrink_weight, lax.dynamic_slice_in_dim(shrink_weight, dp * SH, SH, 1)),
        )
        whole = lambda a, axis: lax.all_gather(a.astype(BF16), "dp", axis=axis, tiled=True)
        heads = jnp.concatenate([whole(updated[0], 1), whole(updated[1].T, 0)[None]], axis=0)
        ins += [("key_weights", jnp.stack([pack(*heads), whole(updated[2], 0), whole(updated[3].T, 0)]), any_)]
    scratch = [
        ("X", vm((2, 2, L, D), BF16)), ("wqi", vm((3, 2, HS, D), BF16)), ("wo", vm((2, HS, D), BF16)),
        ("we", vm((2, D, FS), BF16)), ("ws", vm((2, FS, D), BF16)),
        ("wk", vm((2, 3, D, D), BF16)),
        ("queue", vm((QN, D), BF16)), ("cot", vm((L, D), BF16)),
        ("hb", vm((2, 4, HS), F32)), ("eb", vm((2, TENSOR, FS), F32)),
        ("qkv", vm((3, 2, L, 2 * HS), BF16)), ("G", vm((2, L, 128), F32)), ("C", vm((2, L, 2 * HS), BF16)),
        ("U", vm((2, 2, L, D), BF16)), ("Uf", vm((2, L, D), F32)), ("H", vm((2, 2, L, FS), BF16)),
        ("slope", vm((2, 2, L, FS), BF16)), ("N1", vm((L, D), F32)), ("N2", vm((L, D), F32)),
        ("i1", vm((L, 128), F32)), ("i2", vm((L, 128), F32)), ("own", vm((2, L, D), F32)), ("part", vm((L, D), F32)),
        ("asend", vm((2, L, D), BF16)), ("arecv", vm((2, L, D), BF16)), ("fsend", vm((2, L, D), BF16)),
        ("frecv", vm((2, L, D), BF16)), ("oq", vm((L, D), BF16)), ("ok", vm((L, D), BF16)),
        ("usend", vm((2, 8, 128), F32)), ("units", vm((2, N, 8, 128), F32)), ("nsend", vm((N, 8, 128), F32)),
        ("nrecv", vm((N, 8, 128), F32)), ("d2", vm((L, D), F32)), ("dF", vm((2, L, D), BF16)),
        ("dZ", vm((2, 2, L, FS), BF16)), ("dusend", vm((L, D), BF16)), ("durecv", vm((L, D), BF16)),
        ("dA", vm((2, L, D), BF16)), ("dqkv", vm((3, 2, L, 2 * HS), BF16)), ("hacc", vm((2, PR, D), F32)),
        ("dxsend", vm((L, D), BF16)), ("dxrecv", vm((L, D), BF16)),
        ("wsend", vm((PIECES, PR, D), BF16)), ("wrecv", vm((PIECES, PR, D), BF16)),
        ("sm", vm((3 + DP.bit_length(), 16, D), F32)), ("smx", vm((16, D), F32)),
        ("smr", vm((2 + DP.bit_length(), 16, D), F32)),
    ]
    if gather:
        scratch += [
            ("mhi", vm(momentum_heads_in.shape, F32)), ("mho", vm(momentum_heads_out.shape, F32)),
            ("mex", vm(momentum_expand_weight.shape, F32)), ("msh", vm(momentum_shrink_weight.shape[::-1], F32)),
            ("wacc", vm((PIECES, PR, D), BF16)), ("wyr", vm((PIECES, PR // 2, D), BF16)),
            ("wys", vm((PIECES, PR // 2, D), BF16)), ("wzr", vm((PIECES, NZ - 1, PR // DP, D), BF16)),
            ("wout", vm((PIECES, PR, D), BF16)),
        ]
    else:
        scratch += [("wacc32", vm((PIECES, PR, D), F32))]
    scratch += [("v_" + n, vm(a.shape, a.dtype)) for n, a in small.items()]
    dma = pltpu.SemaphoreType.DMA
    nx = 2 + 6 * NCH + 4 * NCH
    ng = 3 * (2 * (NZ - 1) + NZ) + 3
    nw = PIECES * (2 + 3 * (NZ - 1) + NZ)
    nv = 3
    for pair, count in ((("xs", "xr"), nx), (("cs", "cr"), 5), (("gs", "gr"), ng), (("us", "ur"), nv),
                        (("ws_s", "ws_r"), nw), (("bs", "br"), 2 + DP.bit_length())):
        for name in pair:
            scratch.append((name, dma((count,))))
    scratch += [("lsem", dma((32,))), ("ssem", dma((16,)))]
    cfg.names = [n for n, *_ in ins] + [n for n, *_ in outs] + [n for n, _ in scratch]

    def body(*refs):
        kernel(cfg, *refs)

    res = pl.pallas_call(
        body,
        out_shape=[jax.ShapeDtypeStruct(s, d) for _, s, d in outs],
        in_specs=[s for _, _, s in ins],
        out_specs=[any_] * len(outs),
        scratch_shapes=[s for _, s in scratch],
        compiler_params=pltpu.CompilerParams(collective_id=0, has_side_effects=True, vmem_limit_bytes=cfg_limit()),
        name="step",
    )(*[a for _, a, _ in ins])
    query_out, key_out, d_tokens, grads, vectors = res[:5]
    if gather:
        updates = res[5:]
    else:
        updates = (updated[0], updated[1], updated[2], updated[3].T)
        grads, vectors = lax.psum((grads, vectors), "dp")
    copies = (query_out, key_out, d_tokens) + tuple(updates)
    fin = types.SimpleNamespace(D=D, HS=HS, FS=FS, small=list(small))
    out = [jax.ShapeDtypeStruct(a.shape, a.dtype) for a in copies]
    out += [jax.ShapeDtypeStruct(sh, F32) for sh in ((FS, D), (D, FS), (3, HS, D), (HS, D))]
    tiny = ((1, 1), (2, HS), (FS // 128, 128), (2, D), (2, D), (2, D), (2, HS), (FS // 128, 128), (2, D), (2, D), (2, D))
    out += [jax.ShapeDtypeStruct(sh, F32) for sh in tiny]
    out_dmas = len(copies) + 7 + len(tiny)
    done = pl.pallas_call(
        lambda *a: finish(fin, *a),
        out_shape=out,
        in_specs=[any_] * (len(copies) + 2 + len(small)),
        out_specs=[any_] * len(out),
        scratch_shapes=[vm(a.shape, a.dtype) for a in small.values()] + [vm(sh, F32) for sh in tiny]
        + [vm(a.shape, a.dtype) for a in copies]
        + [vm(vectors.shape, F32), vm((PIECES, PR, D), grads.dtype), vm((PIECES, PR, D), F32), dma((32,)), dma((out_dmas,))],
        compiler_params=pltpu.CompilerParams(vmem_limit_bytes=cfg_limit()),
        name="finish",
    )(*copies, grads, vectors, *small.values())
    (query_out, key_out, d_tokens, up_in, up_out, up_expand, up_shrink, g_shrink, g_expand, g_in, g_out, loss, g_hb, g_eb,
     g_bias, g_gain, g_shift, up_hb, up_eb, up_bias, up_gain, up_shift) = done
    return (
        query_out, key_out, loss[0, 0], d_tokens, jnp.swapaxes(g_in, 1, 2), g_hb, g_out, g_expand, g_eb.reshape(FS), g_shrink,
        g_bias, g_gain, g_shift, up_in, up_hb, up_out, up_expand, up_eb.reshape(FS), up_shrink.T, up_bias, up_gain, up_shift,
    )


def finish(fin, *refs):
    HS = fin.HS
    ns, n, nt = len(fin.small), 7, 11
    src, grads, vectors, small = refs[:n], refs[n], refs[n + 1], refs[n + 2 : n + 2 + ns]
    outs, scratch = refs[n + 2 + ns : n + 2 + ns + n + 4 + nt], refs[n + 2 + ns + n + 4 + nt :]
    v = dict(zip(fin.small, scratch[:ns]))
    tiny, held = scratch[ns : ns + nt], scratch[ns + nt : ns + nt + n]
    vecs, low, wide, isem, osem = scratch[ns + nt + n :]
    dst, (g_shrink, g_expand, g_in, g_out), tiny_out = outs[:n], outs[n : n + 4], outs[n + 4 :]
    loss, g_hb, g_eb, g_bias, g_gain, g_shift, up_hb, up_eb, up_bias, up_gain, up_shift = tiny
    PR = low.shape[1]
    ins = [pltpu.make_async_copy(grads.at[p], low.at[p], isem.at[p]) for p in range(PIECES)]
    ins += [pltpu.make_async_copy(a, b, isem.at[PIECES + i]) for i, (a, b) in enumerate(zip(small, scratch))]
    ins.append(pltpu.make_async_copy(vectors, vecs, isem.at[PIECES + ns]))
    ins += [pltpu.make_async_copy(a, b, isem.at[PIECES + ns + 1 + i]) for i, (a, b) in enumerate(zip(src, held))]
    for c in ins:
        c.start()
    homes = [
        [(g_shrink.at[0:PR], 0, PR)], [(g_shrink.at[PR : 2 * PR], 0, PR)], [(g_expand.at[0:PR], 0, PR)],
        [(g_expand.at[PR : 2 * PR], 0, PR)], [(g_in.at[0], 0, HS), (g_in.at[1], HS, 2 * HS)],
        [(g_in.at[2], 0, HS), (g_out, HS, 2 * HS)],
    ]
    waits, k = [], n
    for p in range(PIECES):
        ins[p].wait()
        wide[p] = low[p].astype(F32)
        for home, a, b in homes[p]:
            c = pltpu.make_async_copy(wide.at[p, a:b], home, osem.at[k])
            c.start()
            waits.append(c)
            k += 1
    for c in ins[PIECES : PIECES + ns + 1]:
        c.wait()
    for i, (a, b) in enumerate(zip(held, dst)):
        ins[PIECES + ns + 1 + i].wait()
        c = pltpu.make_async_copy(a, b, osem.at[i])
        c.start()
        waits.append(c)
    t = lax.axis_index("tensor")
    whole = vecs[...]
    loss[...] = whole[6:7, 0:1]
    g_hb[...] = whole[9:11, 0:HS]
    g_bias[...], g_gain[...], g_shift[...] = whole[0:2, :], whole[2:4, :], whole[4:6, :]
    for name, o in (("heads_bias", up_hb), ("branch_bias", up_bias), ("norm_gain", up_gain), ("norm_shift", up_shift)):
        o[...] = MOMENTUM * v["momentum_" + name][...] + (1.0 - MOMENTUM) * v[name][...].astype(F32)
    eb = MOMENTUM * v["momentum_expand_bias"][...] + (1.0 - MOMENTUM) * v["expand_bias"][...].astype(F32)
    at = lax.broadcasted_iota(jnp.int32, eb.shape, 0)
    for i in range(fin.FS // 128):
        g_eb[i : i + 1, :] = whole[8:9, i * 128 : i * 128 + 128]
        row = jnp.where(at == t * (fin.FS // 128) + i, eb, 0.0)
        up_eb[i : i + 1, :] = jnp.sum(row, axis=0, keepdims=True)
    for i, (a, b) in enumerate(zip(tiny, tiny_out)):
        c = pltpu.make_async_copy(a, b, osem.at[n + 6 + i])
        c.start()
        waits.append(c)
    for c in waits:
        c.wait()


def cfg_limit():
    return 64 * 1024 * 1024 - 4096


def solution(mesh):
    both = ("dp", "tensor")
    in_specs = (
        P(both, None), P(both, None), P("dp"), P("dp"), P(), P(both, None), P(both, None), P(None, None, "tensor"),
        P(None, "tensor"), P("tensor", None), P(None, "tensor"), P(), P("tensor", None), P(), P(), P(),
        P(None, "dp", "tensor"), P(None, "tensor"), P("tensor", "dp"), P("dp", "tensor"), P(), P("tensor", "dp"), P(), P(), P(),
    )
    out_specs = (
        P(both, None), P(both, None), P(), P(both, None), P(None, None, "tensor"), P(None, "tensor"), P("tensor", None),
        P(None, "tensor"), P("tensor"), P("tensor", None), P(), P(), P(), P(None, "dp", "tensor"), P(None, "tensor"),
        P("tensor", "dp"), P("dp", "tensor"), P("tensor"), P("tensor", "dp"), P(), P(), P(),
    )
    shape = dict(mesh.shape)
    return jax.shard_map(lambda *a: local(shape, *a), mesh=mesh, in_specs=in_specs, out_specs=out_specs, check_vma=False)
```
